32 devices in a mesh: gy: 16 (over z, y, x), pa: 2 (over core).
Axes of the slice: x: 2, y: 2, z: 4, core: 2. Of those that a mesh axis runs over, the one named last changes fastest.
Arguments:
- mass_per_volume: float32 [128, 128, 128], P('gy', 'pa'), may hold values from 0.5 to 1.5
- mass_flux_vector: float32 [3, 128, 128, 128], P(None, 'gy', 'pa'), may hold values from -1.5 to 1.5
- total_heat_content: float32 [128, 128, 128], P('gy', 'pa'), may hold values from 1.6 to 4.4
Outputs:
- time_rate: float32 [5, 128, 128, 128], P(None, 'gy', 'pa')
- smoothed: float32 [5, 128, 128, 128], P(None, 'gy', 'pa')
The draws below stay inside these ranges and needn't reach their ends.
All inputs are finite; a program needn't handle non-finite values.
Results may differ from the reference program's by a relative error of at most 0.0003.
Values sent between devices are 32-bit elements; how exact they have to be, the bound alone decides.
A program may use at most 256 MiB of HBM per device.

```python
import jax
import jax.numpy as jnp
import numpy as np
from jax import lax

NX = 128
NY = 128
NZ = 128


def row_signs():
    return (1.0 - 2.0 * (jnp.arange(NY) % 2).astype(jnp.float32))[:, None, None]


def draw_mass_per_volume(key, part):
    shape_all = (NY, NZ, NX)
    rough = jnp.clip(0.1 * jax.random.normal(key, shape_all, jnp.float32), -0.2, 0.2)
    return 1.0 + 0.3 * row_signs() + rough


def draw_total_heat_content(key, part):
    shape_all = (NY, NZ, NX)
    rough = jnp.clip(0.25 * jax.random.normal(key, shape_all, jnp.float32), -0.5, 0.5)
    return 3.0 + 0.9 * row_signs() + rough


def draw_mass_flux_vector(key, part):
    shape_all = (3, NY, NZ, NX)
    return jnp.clip(0.4 * jax.random.normal(key, shape_all, jnp.float32), -1.5, 1.5)


def setup_inputs(seed: int = 0) -> dict:
    seeds = jax.random.split(jax.random.key(seed), 4)
    mass_per_volume = draw_mass_per_volume(jax.random.fold_in(seeds[3], 71), 0)
    mass_flux_vector = draw_mass_flux_vector(jax.random.fold_in(seeds[3], 71), 0)
    total_heat_content = draw_total_heat_content(jax.random.fold_in(seeds[3], 71), 0)
    return dict(mass_per_volume=mass_per_volume, mass_flux_vector=mass_flux_vector, total_heat_content=total_heat_content)


GAMMA_GAS = 1.4
PRANDTL = 0.72
VISCOSITY = 0.25
ALPHA_FILTER = 0.499
ALPHA_SLOPE = 0.498
STRETCH = 1.2
STREAM_STEP = 1.0
SPAN_STEP = 0.5

def slope_weights():
    near_weight = (2.0 + ALPHA_SLOPE) / 3.0
    far_weight = (4.0 * ALPHA_SLOPE - 1.0) / 12.0
    return (near_weight, far_weight)

def system_rows(system_kind, points):
    lower = np.zeros(points)
    middle = np.ones(points)
    upper = np.zeros(points)
    weights = np.zeros((7, points))
    if system_kind == 'slope':
        near_weight, far_weight = slope_weights()
        lower[:] = ALPHA_SLOPE
        upper[:] = ALPHA_SLOPE
        weights[1] = -far_weight
        weights[2] = -near_weight
        weights[4] = near_weight
        weights[5] = far_weight
        for edge_row in (1, points - 2):
            lower[edge_row] = 0.25
            upper[edge_row] = 0.25
            weights[:, edge_row] = 0.0
            weights[2, edge_row] = -0.75
            weights[4, edge_row] = 0.75
        lower[0] = 0.0
        upper[0] = 2.0
        weights[:, 0] = 0.0
        weights[3, 0] = -2.5
        weights[4, 0] = 2.0
        weights[5, 0] = 0.5
        lower[points - 1] = 2.0
        upper[points - 1] = 0.0
        weights[:, points - 1] = 0.0
        weights[3, points - 1] = 2.5
        weights[2, points - 1] = -2.0
        weights[1, points - 1] = -0.5
    else:
        strength = ALPHA_FILTER
        lower[:] = strength
        upper[:] = strength
        weights[3] = 11.0 / 16.0 + 5.0 * strength / 8.0
        weights[2] = 15.0 / 64.0 + 17.0 * strength / 32.0
        weights[4] = weights[2]
        weights[1] = -3.0 / 32.0 + 3.0 * strength / 16.0
        weights[5] = weights[1]
        weights[0] = 1.0 / 64.0 - strength / 32.0
        weights[6] = weights[0]
        for edge_row in (2, points - 3):
            weights[:, edge_row] = 0.0
            weights[3, edge_row] = 5.0 / 8.0 + 3.0 * strength / 4.0
            weights[2, edge_row] = 0.25 + strength / 2.0
            weights[4, edge_row] = 0.25 + strength / 2.0
            weights[1, edge_row] = -1.0 / 16.0 + strength / 8.0
            weights[5, edge_row] = -1.0 / 16.0 + strength / 8.0
        for edge_row in (1, points - 2):
            weights[:, edge_row] = 0.0
            weights[3, edge_row] = 0.5 + strength
            weights[2, edge_row] = 0.25 + strength / 2.0
            weights[4, edge_row] = 0.25 + strength / 2.0
        for edge_row in (0, points - 1):
            lower[edge_row] = 0.0
            upper[edge_row] = 0.0
            weights[:, edge_row] = 0.0
            weights[3, edge_row] = 1.0
    return (lower, middle, upper, weights)

def inverse_metric(points):
    places = 2.0 * np.arange(points) / (points - 1) - 1.0
    growth = np.exp(STRETCH * places)
    cosh_values = 0.5 * (growth + 1.0 / growth)
    edge_growth = np.exp(STRETCH)
    tanh_value = (edge_growth - 1.0 / edge_growth) / (edge_growth + 1.0 / edge_growth)
    return tanh_value * cosh_values ** 2 / (0.64 * STRETCH)

def stencil_sum(padded, weights, rim_rows):
    rows_here = padded.shape[1] - 2 * rim_rows
    summed = jnp.zeros((padded.shape[0], rows_here, padded.shape[2]), jnp.float32)
    for offset in range(-rim_rows, rim_rows + 1):
        summed = summed + weights[:, 3 + offset, :, None] * padded[:, rim_rows + offset:rim_rows + offset + rows_here]
    return summed

def wall_apply(field_lines, system_kind):
    points = field_lines.shape[0]
    lower, middle, upper, weights = system_rows(system_kind, points)
    padded = jnp.pad(field_lines[None], ((0, 0), (3, 3), (0, 0)))
    right_side = stencil_sum(padded, jnp.asarray(weights[None], jnp.float32), 3)[0]
    return lax.linalg.tridiagonal_solve(jnp.asarray(lower, jnp.float32), jnp.asarray(middle, jnp.float32), jnp.asarray(upper, jnp.float32), right_side)

def periodic_slope(fields, axis_at, spacing):
    points = fields.shape[axis_at]
    near_weight, far_weight = slope_weights()
    wave_numbers = np.arange(points // 2 + 1)
    angles = 2.0 * np.pi * wave_numbers / points
    modified = (2.0 * near_weight * np.sin(angles) + 2.0 * far_weight * np.sin(2.0 * angles)) / (1.0 + 2.0 * ALPHA_SLOPE * np.cos(angles)) / spacing
    modified[points // 2] = 0.0
    modified[0] = 0.0
    broadcast_shape = [1] * fields.ndim
    broadcast_shape[axis_at] = points // 2 + 1
    factor = jnp.asarray(modified.reshape(broadcast_shape), jnp.float32)
    spectrum = jnp.fft.rfft(fields, axis=axis_at)
    return jnp.fft.irfft(spectrum * (1j * factor), n=points, axis=axis_at).astype(jnp.float32)

def recover_basic_quantities(mass_per_volume, mass_flux_vector, total_heat_content):
    fluid_speed_vector = mass_flux_vector / mass_per_volume[None]
    kinetic = 0.5 * jnp.sum(fluid_speed_vector * mass_flux_vector, axis=0)
    thermo_push = (GAMMA_GAS - 1.0) * (total_heat_content - kinetic)
    thermo_warmth = thermo_push / mass_per_volume
    return (fluid_speed_vector, thermo_push, thermo_warmth)

def flux_along(direction, mass_flux_vector, total_heat_content, fluid_speed_vector, thermo_push, gradients):
    divergence = gradients[0][0] + gradients[1][1] + gradients[2][2]
    conduct = VISCOSITY * GAMMA_GAS / ((GAMMA_GAS - 1.0) * PRANDTL)
    rows_out = [mass_flux_vector[direction]]
    energy_flux = (total_heat_content + thermo_push) * fluid_speed_vector[direction]
    for component in range(3):
        stress = VISCOSITY * (gradients[direction][component] + gradients[component][direction])
        if component == direction:
            stress = stress - 2.0 / 3.0 * VISCOSITY * divergence
            rows_out.append(mass_flux_vector[component] * fluid_speed_vector[direction] + thermo_push - stress)
        else:
            rows_out.append(mass_flux_vector[component] * fluid_speed_vector[direction] - stress)
        energy_flux = energy_flux - fluid_speed_vector[component] * stress
    energy_flux = energy_flux - conduct * gradients[direction][3]
    rows_out.append(energy_flux)
    return jnp.stack(rows_out)

def reference(mass_per_volume, mass_flux_vector, total_heat_content):
    points, span_cells, stream_cells = mass_per_volume.shape
    line_count = span_cells * stream_cells
    fluid_speed_vector, thermo_push, thermo_warmth = recover_basic_quantities(mass_per_volume, mass_flux_vector, total_heat_content)
    basic_quantities = jnp.concatenate([fluid_speed_vector, thermo_warmth[None]], axis=0)
    state_all = jnp.concatenate([mass_per_volume[None], mass_flux_vector, total_heat_content[None]], axis=0)
    metric = jnp.asarray(inverse_metric(points), jnp.float32)[:, None, None]
    smoothed = jnp.stack([wall_apply(state_all[member].reshape(points, line_count), 'smooth').reshape(points, span_cells, stream_cells) for member in range(5)])
    wall_grad = jnp.stack([wall_apply(basic_quantities[member].reshape(points, line_count), 'slope').reshape(points, span_cells, stream_cells) * metric for member in range(4)])
    gradients = [periodic_slope(basic_quantities, 3, STREAM_STEP), wall_grad, periodic_slope(basic_quantities, 2, SPAN_STEP)]
    stream_term = periodic_slope(flux_along(0, mass_flux_vector, total_heat_content, fluid_speed_vector, thermo_push, gradients), 3, STREAM_STEP)
    flux_wall = flux_along(1, mass_flux_vector, total_heat_content, fluid_speed_vector, thermo_push, gradients)
    wall_term = jnp.stack([wall_apply(flux_wall[member].reshape(points, line_count), 'slope').reshape(points, span_cells, stream_cells) * metric for member in range(5)])
    span_term = periodic_slope(flux_along(2, mass_flux_vector, total_heat_content, fluid_speed_vector, thermo_push, gradients), 2, SPAN_STEP)
    time_rate = -(stream_term + wall_term + span_term)
    row_numbers = jnp.arange(points)
    at_wall = (row_numbers == 0) | (row_numbers == points - 1)
    held_rows = jnp.where(at_wall[None, :, None, None], 0.0, time_rate[1:4])
    time_rate = jnp.concatenate([time_rate[:1], held_rows, time_rate[4:]], axis=0)
    return (time_rate, smoothed)
```

```python
import functools

import jax
import jax.numpy as jnp
import ml_dtypes
import numpy as np
from jax import lax
from jax.experimental import pallas as pl
from jax.experimental.pallas import tpu as pltpu
from jax.sharding import PartitionSpec as P

GAMMA_GAS = 1.4
PRANDTL = 0.72
VISCOSITY = 0.25
ALPHA_FILTER = 0.499
ALPHA_SLOPE = 0.498
STRETCH = 1.2
STREAM_STEP = 1.0
SPAN_STEP = 0.5
CONDUCT = VISCOSITY * GAMMA_GAS / ((GAMMA_GAS - 1.0) * PRANDTL)
MESH = pl.DeviceIdType.MESH


def slope_weights():
    near_weight = (2.0 + ALPHA_SLOPE) / 3.0
    far_weight = (4.0 * ALPHA_SLOPE - 1.0) / 12.0
    return (near_weight, far_weight)


def system_rows(system_kind, points):
    lower = np.zeros(points)
    middle = np.ones(points)
    upper = np.zeros(points)
    weights = np.zeros((7, points))
    if system_kind == "slope":
        near_weight, far_weight = slope_weights()
        lower[:] = ALPHA_SLOPE
        upper[:] = ALPHA_SLOPE
        weights[1] = -far_weight
        weights[2] = -near_weight
        weights[4] = near_weight
        weights[5] = far_weight
        for edge_row in (1, points - 2):
            lower[edge_row] = 0.25
            upper[edge_row] = 0.25
            weights[:, edge_row] = 0.0
            weights[2, edge_row] = -0.75
            weights[4, edge_row] = 0.75
        lower[0] = 0.0
        upper[0] = 2.0
        weights[:, 0] = 0.0
        weights[3, 0] = -2.5
        weights[4, 0] = 2.0
        weights[5, 0] = 0.5
        lower[points - 1] = 2.0
        upper[points - 1] = 0.0
        weights[:, points - 1] = 0.0
        weights[3, points - 1] = 2.5
        weights[2, points - 1] = -2.0
        weights[1, points - 1] = -0.5
    else:
        strength = ALPHA_FILTER
        lower[:] = strength
        upper[:] = strength
        weights[3] = 11.0 / 16.0 + 5.0 * strength / 8.0
        weights[2] = 15.0 / 64.0 + 17.0 * strength / 32.0
        weights[4] = weights[2]
        weights[1] = -3.0 / 32.0 + 3.0 * strength / 16.0
        weights[5] = weights[1]
        weights[0] = 1.0 / 64.0 - strength / 32.0
        weights[6] = weights[0]
        for edge_row in (2, points - 3):
            weights[:, edge_row] = 0.0
            weights[3, edge_row] = 5.0 / 8.0 + 3.0 * strength / 4.0
            weights[2, edge_row] = 0.25 + strength / 2.0
            weights[4, edge_row] = 0.25 + strength / 2.0
            weights[1, edge_row] = -1.0 / 16.0 + strength / 8.0
            weights[5, edge_row] = -1.0 / 16.0 + strength / 8.0
        for edge_row in (1, points - 2):
            weights[:, edge_row] = 0.0
            weights[3, edge_row] = 0.5 + strength
            weights[2, edge_row] = 0.25 + strength / 2.0
            weights[4, edge_row] = 0.25 + strength / 2.0
        for edge_row in (0, points - 1):
            lower[edge_row] = 0.0
            upper[edge_row] = 0.0
            weights[:, edge_row] = 0.0
            weights[3, edge_row] = 1.0
    return (lower, middle, upper, weights)


def inverse_metric(points):
    places = 2.0 * np.arange(points) / (points - 1) - 1.0
    growth = np.exp(STRETCH * places)
    cosh_values = 0.5 * (growth + 1.0 / growth)
    edge_growth = np.exp(STRETCH)
    tanh_value = (edge_growth - 1.0 / edge_growth) / (edge_growth + 1.0 / edge_growth)
    return tanh_value * cosh_values**2 / (0.64 * STRETCH)


def periodic_matrix(points, spacing):
    near_weight, far_weight = slope_weights()
    wave_numbers = np.arange(1, points // 2)
    angles = 2.0 * np.pi * wave_numbers / points
    modified = (2.0 * near_weight * np.sin(angles) + 2.0 * far_weight * np.sin(2.0 * angles)) / (
        1.0 + 2.0 * ALPHA_SLOPE * np.cos(angles)
    )
    phases = np.arange(points)[:, None] * wave_numbers[None, :] % points
    circulant = -2.0 / (points * spacing) * (np.sin(2.0 * np.pi * phases / points) @ modified)
    shifts = (np.arange(points)[:, None] - np.arange(points)[None, :]) % points
    return circulant[shifts].T


def wall_tables(system_kind, points, rows):
    lower, middle, upper, weights = system_rows(system_kind, points)
    system = np.diag(middle) + np.diag(lower[1:], -1) + np.diag(upper[:-1], 1)
    source = np.zeros((points, points))
    for offset in range(-3, 4):
        for row in range(max(0, -offset), min(points, points - offset)):
            source[row, row + offset] = weights[3 + offset, row]
    band = np.zeros((points, points))
    if system_kind == "slope":
        ratio = slope_weights()[1] / ALPHA_SLOPE
        for row in range(2, points - 2):
            band[row, row + 1] = ratio
            band[row, row - 1] = -ratio
    else:
        mid = points // 2
        strength = ALPHA_FILTER
        two = weights[0, mid] / strength
        one = (weights[1, mid] - two) / strength
        zero = (weights[2, mid] - strength * two - one) / strength
        for row in range(3, points - 3):
            for offset, value in ((0, zero), (1, one), (2, two)):
                band[row, row + offset] = value
                band[row, row - offset] = value
    rest = np.linalg.solve(system, source - system @ band)
    down_ratio = np.zeros(points)
    carried = 0.0
    for row in range(points):
        down_ratio[row] = upper[row] / (middle[row] - lower[row] * carried)
        carried = down_ratio[row]
    up_ratio = np.zeros(points)
    carried = 0.0
    for row in range(points - 1, -1, -1):
        up_ratio[row] = lower[row] / (middle[row] - upper[row] * carried)
        carried = up_ratio[row]
    scale = inverse_metric(points) if system_kind == "slope" else np.ones(points)
    blocks = points // rows
    local = np.zeros((blocks, rows, rows))
    up = np.zeros((blocks, rows))
    down = np.zeros((blocks, rows))
    to_up = np.zeros((blocks, rows))
    to_down = np.zeros((blocks, rows))
    up_gain = np.zeros(blocks)
    down_gain = np.zeros(blocks)
    rim = np.zeros((blocks, 6))
    for block in range(blocks):
        first, last = block * rows, block * rows + rows - 1
        window = slice(first, last + 1)
        local[block] = (rest + band)[window, window] * scale[window, None]
        up[block] = np.cumprod(np.concatenate([[1.0], -up_ratio[first + 1 : last + 1]]))
        up[block] *= scale[window]
        down[block] = np.cumprod(np.concatenate([[1.0], -down_ratio[first:last][::-1]]))[::-1]
        down[block] *= scale[window]
        if block < blocks - 1:
            to_up[block] = rest[last + 1, window]
            up_gain[block] = np.prod(-up_ratio[first + 1 : last + 2])
            rim[block, 3] = band[last, last + 1] * scale[last]
            rim[block, 4] = band[last, last + 2] * scale[last]
            rim[block, 5] = band[last - 1, last + 1] * scale[last - 1]
        if block > 0:
            to_down[block] = rest[first - 1, window]
            down_gain[block] = np.prod(-down_ratio[first - 1 : last])
            rim[block, 0] = band[first, first - 1] * scale[first]
            rim[block, 1] = band[first, first - 2] * scale[first]
            rim[block, 2] = band[first + 1, first - 1] * scale[first + 1]
    return local, up, down, to_up, to_down, up_gain, down_gain, rim


def table_layout(rows):
    sizes = (("local", rows * rows), ("up", rows), ("down", rows), ("to_up", rows), ("to_down", rows), ("rim", 6))
    places, at = {}, 0
    for kind in ("slope", "smooth"):
        for name, size in sizes:
            places[kind, name] = at
            at += size
    places["keep"] = at
    return places, at + rows


def device_table(points, rows):
    places, width = table_layout(rows)
    blocks = points // rows
    table = np.zeros((blocks, width), np.float32)
    gains = {}
    for kind in ("slope", "smooth"):
        local, up, down, to_up, to_down, up_gain, down_gain, rim = wall_tables(kind, points, rows)
        gains[kind] = (up_gain, down_gain)
        named = dict(local=local, up=up, down=down, to_up=to_up, to_down=to_down, rim=rim)
        for name, value in named.items():
            flat = value.reshape(blocks, -1)
            at = places[kind, name]
            table[:, at : at + flat.shape[1]] = flat
    table[:, places["keep"] :] = 1.0
    table[0, places["keep"]] = 0.0
    table[-1, -1] = 0.0
    return table.reshape(-1), gains


def gain_table(kinds, gains, blocks, tiles, each):
    count = len(kinds)
    table = np.zeros((blocks, blocks, each), np.float32)
    for owner in range(blocks):
        for slot in range(each):
            quantity = (owner * each + slot) // tiles
            if quantity >= 2 * count:
                continue
            chain = gains[kinds[quantity % count]][quantity // count]
            table[owner, :, slot] = chain if quantity < count else chain[::-1]
    return table.reshape(-1)


def split_pair(matrix):
    high = matrix.astype(np.float32).astype(ml_dtypes.bfloat16)
    low = (matrix - high.astype(np.float64)).astype(np.float32).astype(ml_dtypes.bfloat16)
    return high, low


def stream_table(points):
    high, low = split_pair(periodic_matrix(points, STREAM_STEP))
    return np.block([[high, low], [high, np.zeros_like(low)]])


def span_table(points):
    own = points // 2
    rows = periodic_matrix(points, SPAN_STEP).T[:own]
    high, low = split_pair(rows)
    return np.block([[high, high], [low, np.zeros_like(low)]])


def halves(value):
    high = value.astype(jnp.bfloat16)
    return high, (value - high.astype(jnp.float32)).astype(jnp.bfloat16)


def fused_body(
    count, rho, mom, ene, tab, gain_a, gain_b, xmat, zmat,
    rate, smooth,
    span_out, span_in, gx, gy, gz, fx, fy, fspan_out, fspan_in,
    rim_out, rim_in, frim_out, frim_in,
    va, ra, oa, sa, vb, rb, ob, sb, vc, rc, oc, sc,
    s_span, r_span, s_rim, r_rim,
    s_a, r_a, s_ao, r_ao, s_b, r_b, s_bo, r_bo, s_c, r_c, s_co, r_co,
):
    rows, span, _ = rho.shape
    tiles = span // 8
    me, core = lax.axis_index("gy"), lax.axis_index("pa")
    places, width = table_layout(rows)
    base = me * width

    def entry(kind, name, at):
        return tab[base + places[kind, name] + at]

    def remote(src, dst, send, recv, target, target_core):
        return pltpu.make_async_remote_copy(
            src_ref=src, dst_ref=dst, send_sem=send, recv_sem=recv,
            device_id=(target, target_core), device_id_type=MESH,
        )

    barrier = pltpu.get_barrier_semaphore()

    @pl.loop(1, count)
    def _(step):
        pl.semaphore_signal(
            barrier, inc=1, device_id=(lax.rem(me + step, count), core), device_id_type=MESH
        )

    pl.semaphore_signal(barrier, inc=1, device_id=(me, 1 - core), device_id_type=MESH)

    for depth in range(2):
        for side, row in ((0, rows - 1 - depth), (1, depth)):
            rim_out[side, depth, 0] = rho[row]
            for c in range(3):
                rim_out[side, depth, 1 + c] = mom[c, row]
            rim_out[side, depth, 4] = ene[row]

    @pl.when(me == 0)
    def _():
        rim_in[0] = jnp.ones(rim_in.shape[1:], jnp.float32)
        frim_in[0] = jnp.ones(frim_in.shape[1:], jnp.float32)

    @pl.when(me == count - 1)
    def _():
        rim_in[1] = jnp.ones(rim_in.shape[1:], jnp.float32)
        frim_in[1] = jnp.ones(frim_in.shape[1:], jnp.float32)

    def primitives(d, m0, m1, m2, e):
        inv = 1.0 / d
        u, v, w = m0 * inv, m1 * inv, m2 * inv
        push = (GAMMA_GAS - 1.0) * (e - 0.5 * (u * m0 + v * m1 + w * m2))
        return u, v, w, push * inv

    @pl.loop(0, tiles)
    def _(t):
        z = pl.ds(pl.multiple_of(t * 8, 8), 8)
        ups, downs = [None] * 4, [None] * 4
        for y in range(rows):
            m2 = mom[2, y, z]
            values = primitives(rho[y, z], mom[0, y, z], mom[1, y, z], m2, ene[y, z])
            a, b = entry("slope", "to_up", y), entry("slope", "to_down", y)
            for f in range(4):
                span_out[f, y, z] = values[f]
                ups[f] = a * values[f] if y == 0 else ups[f] + a * values[f]
                downs[f] = b * values[f] if y == 0 else downs[f] + b * values[f]
            span_out[4, y, z] = m2
        for f in range(4):
            va[f * tiles + t] = ups[f]
            va[(4 + f) * tiles + t] = downs[f]

    pl.semaphore_wait(barrier, count)

    def rim_send(source, into, slot):
        def make(side, target):
            return remote(source(side), into(side), s_rim.at[slot, side], r_rim.at[slot, side], target, core)

        @pl.when(me < count - 1)
        def _():
            make(0, me + 1).start()

        @pl.when(me > 0)
        def _():
            make(1, me - 1).start()

    def rim_wait(source, into, slot):
        def make(side, target):
            return remote(source(side), into(side), s_rim.at[slot, side], r_rim.at[slot, side], target, core)

        @pl.when(me < count - 1)
        def _():
            make(0, me + 1).wait_send()
            make(1, me + 1).wait_recv()

        @pl.when(me > 0)
        def _():
            make(1, me - 1).wait_send()
            make(0, me - 1).wait_recv()

    def spread(src, dst, send, recv):
        each = src.shape[0] // count

        @pl.loop(1, count)
        def _(step):
            to = lax.rem(me + step, count)
            remote(
                src.at[pl.ds(to * each, each)], dst.at[pl.ds(me * each, each)],
                send.at[step], recv.at[step], to, core,
            ).start()

        dst[pl.ds(me * each, each)] = src[pl.ds(me * each, each)]

    def spread_wait(src, dst, send, recv):
        each = src.shape[0] // count

        @pl.loop(1, count)
        def _(step):
            to = lax.rem(me + step, count)
            fro = lax.rem(me + count - step, count)
            remote(
                src.at[pl.ds(to * each, each)], dst.at[pl.ds(me * each, each)],
                send.at[step], recv.at[step], to, core,
            ).wait_send()
            remote(
                src.at[pl.ds(to * each, each)], dst.at[pl.ds(fro * each, each)],
                send.at[step], recv.at[step], to, core,
            ).wait_recv()

    def scan(src, out, back, gains, fields, send, recv):
        each = src.shape[0] // count
        turned = jnp.minimum((me * each) // (fields * tiles), 1)

        def lap(i, carry):
            j = i + turned * (count - 1 - 2 * i)
            at = pl.ds(j * each, each)
            out[at] = jnp.stack(carry)

            @pl.when(j != me)
            def _():
                step = lax.rem(j - me + count, count)
                remote(
                    out.at[at], back.at[pl.ds(me * each, each)],
                    send.at[step], recv.at[step], j, core,
                ).start()

            @pl.when(j == me)
            def _():
                back[at] = out[at]

            return tuple(
                gains[(me * count + i) * each + k] * carry[k] + src[j * each + k] for k in range(each)
            )

        lax.fori_loop(0, count, lap, tuple(jnp.zeros((8, 128), jnp.float32) for _ in range(each)))

    rim_a = (lambda side: rim_out.at[side, 0], lambda side: rim_in.at[side, 0], 0)
    rim_b = (lambda side: rim_out.at[side, 1], lambda side: rim_in.at[side, 1], 1)
    rim_c = (lambda side: frim_out.at[side], lambda side: frim_in.at[side], 2)
    span_copy = remote(span_out, span_in, s_span.at[0], r_span.at[0], me, 1 - core)
    fspan_copy = remote(fspan_out, fspan_in, s_span.at[1], r_span.at[1], me, 1 - core)

    spread(va, ra, s_a, r_a)
    rim_send(*rim_a)
    span_copy.start()

    def local_rows(kind, load, store, z):
        values = [load(y) for y in range(rows)]
        for y in range(rows):
            total = entry(kind, "local", y * rows) * values[0]
            for k in range(1, rows):
                total = total + entry(kind, "local", y * rows + k) * values[k]
            store(y, total)

    def block_loop(fields, size, body):
        per = span // size

        @pl.loop(0, fields * per)
        def _(i):
            body(i // per, pl.ds(pl.multiple_of((i % per) * size, size), size))

    def slope_block(src, dst):
        def body(f, z):
            def store(y, total):
                dst[f, y, z] = total

            local_rows("slope", lambda y: src[f, y, z], store, z)

        return body

    def stream_rows(value):
        high, low = halves(value)
        product = jnp.dot(
            jnp.concatenate([high, low], axis=1), xmat[...], preferred_element_type=jnp.float32
        )
        return product[:, :128] + product[:, 128:]

    def stream_loop(fields, load, store):
        @pl.loop(0, fields * rows // 4)
        def _(i):
            f, y = i // (rows // 4), (i % (rows // 4)) * 4
            block = jnp.concatenate([load(f, y + k) for k in range(4)], axis=0)
            product = stream_rows(block)
            for k in range(4):
                store(f, y + k, product[k * span : (k + 1) * span])

    def span_loop(fields, own, other, store):
        @pl.loop(0, fields * rows // 2)
        def _(i):
            f, y = i // (rows // 2), (i % (rows // 2)) * 2
            parts = [
                halves(jnp.concatenate([ref[f, y], ref[f, y + 1]], axis=1)) for ref in (own, other)
            ]
            stacked = jnp.concatenate([parts[0][0], parts[1][0], parts[0][1], parts[1][1]], axis=0)
            product = jnp.dot(zmat[...], stacked, preferred_element_type=jnp.float32)
            product = product[:span] + product[span:]
            store(f, y, product[:, :128])
            store(f, y + 1, product[:, 128:])

    def store_gx(f, y, value):
        gx[f, y] = value

    def store_gz(f, y, value):
        gz[f, y] = value

    stream_loop(4, lambda f, y: span_out[f, y], store_gx)
    block_loop(4, 16, slope_block(span_out, gy))

    @pl.loop(0, tiles)
    def _(t):
        z = pl.ds(pl.multiple_of(t * 8, 8), 8)
        ups, downs = [None] * 6, [None] * 6
        for y in range(rows):
            middle = mom[1, y, z]
            values = (rho[y, z], mom[0, y, z], middle, mom[2, y, z], ene[y, z], middle)
            pairs = [
                (entry(kind, "to_up", y), entry(kind, "to_down", y)) for kind in ("smooth", "slope")
            ]
            for f in range(6):
                a, b = pairs[f // 5]
                ups[f] = a * values[f] if y == 0 else ups[f] + a * values[f]
                downs[f] = b * values[f] if y == 0 else downs[f] + b * values[f]
        for f in range(6):
            vb[f * tiles + t] = ups[f]
            vb[(6 + f) * tiles + t] = downs[f]

    spread_wait(va, ra, s_a, r_a)
    scan(ra, oa, sa, gain_a, 4, s_ao, r_ao)
    spread(vb, rb, s_b, r_b)

    span_copy.wait()
    span_loop(5, span_out, span_in, store_gz)

    rim_wait(*rim_a)
    for side, row in ((0, 0), (1, rows - 1)):
        weight = entry("slope", "rim", 3 * side)
        values = primitives(*(rim_in[side, 0, f] for f in range(5)))
        for f in range(4):
            gy[f, row] += weight * values[f]
    rim_send(*rim_b)

    spread_wait(oa, sa, s_ao, r_ao)

    @pl.loop(0, tiles)
    def _(t):
        z = pl.ds(pl.multiple_of(t * 8, 8), 8)
        ups, downs = [None] * 4, [None] * 4
        from_up = [sa[f * tiles + t] for f in range(4)]
        from_down = [sa[(4 + f) * tiles + t] for f in range(4)]
        for y in range(rows):
            a, b = entry("slope", "up", y), entry("slope", "down", y)
            u = [span_out[f, y, z] for f in range(4)]
            m = [mom[c, y, z] for c in range(3)]
            e = ene[y, z]
            push = rho[y, z] * u[3]
            grad = (
                [gx[f, y, z] for f in range(4)],
                [gy[f, y, z] + a * from_up[f] + b * from_down[f] for f in range(4)],
                [gz[f, y, z] for f in range(4)],
            )
            spread_out = (2.0 / 3.0 * VISCOSITY) * (grad[0][0] + grad[1][1] + grad[2][2])
            stress = [[None] * 3 for _ in range(3)]
            for c in range(3):
                stress[c][c] = (2.0 * VISCOSITY) * grad[c][c] - spread_out
                for d in range(c):
                    stress[c][d] = stress[d][c] = VISCOSITY * (grad[d][c] + grad[c][d])
            heat = e + push
            a, b = entry("slope", "to_up", y), entry("slope", "to_down", y)
            for d, out in ((0, fx), (1, fy), (2, fspan_out)):
                energy = heat * u[d] - CONDUCT * grad[d][3]
                for c in range(3):
                    energy = energy - u[c] * stress[c][d]
                values = []
                for c in range(3):
                    value = m[c] * u[d] - stress[c][d]
                    values.append(value + push if c == d else value)
                values.append(energy)
                for f in range(4):
                    out[f, y, z] = values[f]
                    if d == 1:
                        ups[f] = a * values[f] if y == 0 else ups[f] + a * values[f]
                        downs[f] = b * values[f] if y == 0 else downs[f] + b * values[f]
                        if y == rows - 1:
                            frim_out[0, f, z] = values[f]
                        if y == 0:
                            frim_out[1, f, z] = values[f]
        for f in range(4):
            vc[f * tiles + t] = ups[f]
            vc[(4 + f) * tiles + t] = downs[f]

    spread(vc, rc, s_c, r_c)
    rim_send(*rim_c)
    fspan_copy.start()

    spread_wait(vb, rb, s_b, r_b)
    scan(rb, ob, sb, gain_b, 6, s_bo, r_bo)

    def store_fx(f, y, value):
        gx[f, y] = value

    stream_loop(4, lambda f, y: fx[f, y], store_fx)
    block_loop(4, 16, slope_block(fy, gy))

    spread_wait(vc, rc, s_c, r_c)
    scan(rc, oc, sc, gain_a, 4, s_co, r_co)

    def store_mass(f, y, value):
        rate[0, y] = value

    stream_loop(1, lambda f, y: mom[0, y], store_mass)

    def mass_block(f, z):
        def store(y, total):
            rate[0, y, z] = -(rate[0, y, z] + total + gz[4, y, z])

        local_rows("slope", lambda y: mom[1, y, z], store, z)

    block_loop(1, 16, mass_block)

    def smooth_block(read, write):
        def body(f, z):
            def store(y, total):
                write[y, z] = total

            local_rows("smooth", lambda y: read[y, z], store, z)

        return body

    block_loop(1, 16, smooth_block(rho, smooth.at[0]))

    def smooth_mom(f, z):
        def store(y, total):
            smooth[1 + f, y, z] = total

        local_rows("smooth", lambda y: mom[f, y, z], store, z)

    block_loop(3, 16, smooth_mom)
    block_loop(1, 16, smooth_block(ene, smooth.at[4]))
    rim_wait(*rim_b)
    for side, edge, inner in ((0, 0, 1), (1, rows - 1, rows - 2)):
        near, far, second = (entry("smooth", "rim", 3 * side + k) for k in range(3))
        for f in range(5):
            smooth[f, edge] += near * rim_in[side, 0, f] + far * rim_in[side, 1, f]
            smooth[f, inner] += second * rim_in[side, 0, f]
        rate[0, edge] -= entry("slope", "rim", 3 * side) * rim_in[side, 0, 2]

    spread_wait(ob, sb, s_bo, r_bo)

    @pl.loop(0, tiles)
    def _(t):
        z = pl.ds(pl.multiple_of(t * 8, 8), 8)
        from_up = [sb[f * tiles + t] for f in range(6)]
        from_down = [sb[(6 + f) * tiles + t] for f in range(6)]
        for y in range(rows):
            a, b = entry("smooth", "up", y), entry("smooth", "down", y)
            for f in range(5):
                smooth[f, y, z] += a * from_up[f] + b * from_down[f]
            a, b = entry("slope", "up", y), entry("slope", "down", y)
            rate[0, y, z] -= a * from_up[5] + b * from_down[5]

    fspan_copy.wait()
    span_loop(4, fspan_out, fspan_in, store_gz)
    rim_wait(*rim_c)
    for side, row in ((0, 0), (1, rows - 1)):
        weight = entry("slope", "rim", 3 * side)
        for f in range(4):
            gy[f, row] += weight * frim_in[side, f]

    spread_wait(oc, sc, s_co, r_co)

    @pl.loop(0, tiles)
    def _(t):
        z = pl.ds(pl.multiple_of(t * 8, 8), 8)
        from_up = [sc[f * tiles + t] for f in range(4)]
        from_down = [sc[(4 + f) * tiles + t] for f in range(4)]
        for y in range(rows):
            a, b = entry("slope", "up", y), entry("slope", "down", y)
            keep = tab[base + places["keep"] + y]
            for f in range(4):
                total = gx[f, y, z] + gz[f, y, z] + gy[f, y, z] + a * from_up[f] + b * from_down[f]
                rate[1 + f, y, z] = -(total * keep) if f < 3 else -total


def per_device(mass_per_volume, mass_flux_vector, total_heat_content):
    rows, span, stream = mass_per_volume.shape
    count = lax.axis_size("gy")
    tiles = span // 8
    table, gains = device_table(rows * count, rows)
    each_a = -(-8 * tiles // count)
    each_b = -(-12 * tiles // count)
    gain_a = gain_table(["slope"] * 4, gains, count, tiles, each_a)
    gain_b = gain_table(["smooth"] * 5 + ["slope"], gains, count, tiles, each_b)
    field = (rows, span, stream)

    def vmem(*shape):
        return pltpu.VMEM(shape, jnp.float32)

    lines_a = [vmem(count * each_a, 8, stream)] * 4
    lines_b = [vmem(count * each_b, 8, stream)] * 4
    whole = pl.BlockSpec(memory_space=pltpu.VMEM)
    scalar = pl.BlockSpec(memory_space=pltpu.SMEM)
    dma = pltpu.SemaphoreType.DMA
    out = jax.ShapeDtypeStruct((5,) + field, jnp.float32)
    return pl.pallas_call(
        functools.partial(fused_body, count),
        out_shape=(out, out),
        in_specs=[whole] * 3 + [scalar] * 3 + [whole] * 2,
        out_specs=(whole, whole),
        scratch_shapes=[
            vmem(5, *field), vmem(5, *field), vmem(4, *field), vmem(4, *field), vmem(5, *field),
            vmem(4, *field), vmem(4, *field), vmem(4, *field), vmem(4, *field),
            vmem(2, 2, 5, span, stream), vmem(2, 2, 5, span, stream),
            vmem(2, 4, span, stream), vmem(2, 4, span, stream),
            *lines_a, *lines_b, *lines_a,
            dma((2,)), dma((2,)), dma((3, 2)), dma((3, 2)),
            *[dma((count,))] * 12,
        ],
        compiler_params=pltpu.CompilerParams(
            collective_id=0, has_side_effects=True, vmem_limit_bytes=48 * 1024 * 1024
        ),
    )(
        mass_per_volume, mass_flux_vector, total_heat_content,
        jnp.asarray(table), jnp.asarray(gain_a), jnp.asarray(gain_b),
        jnp.asarray(stream_table(stream)), jnp.asarray(span_table(2 * span)),
    )


def solution(mesh):
    placed = (P("gy", "pa", None), P(None, "gy", "pa", None), P("gy", "pa", None))
    return jax.shard_map(
        per_device,
        mesh=mesh,
        in_specs=placed,
        out_specs=(P(None, "gy", "pa", None), P(None, "gy", "pa", None)),
        check_vma=False,
    )
```

```python
import functools

import jax
import jax.numpy as jnp
import ml_dtypes
import numpy as np
from jax import lax
from jax.experimental import pallas as pl
from jax.experimental.pallas import tpu as pltpu
from jax.sharding import PartitionSpec as P

GAMMA_GAS = 1.4
PRANDTL = 0.72
VISCOSITY = 0.25
ALPHA_FILTER = 0.499
ALPHA_SLOPE = 0.498
STRETCH = 1.2
STREAM_STEP = 1.0
SPAN_STEP = 0.5
CONDUCT = VISCOSITY * GAMMA_GAS / ((GAMMA_GAS - 1.0) * PRANDTL)
MESH = pl.DeviceIdType.MESH


def slope_weights():
    near_weight = (2.0 + ALPHA_SLOPE) / 3.0
    far_weight = (4.0 * ALPHA_SLOPE - 1.0) / 12.0
    return (near_weight, far_weight)


def system_rows(system_kind, points):
    lower = np.zeros(points)
    middle = np.ones(points)
    upper = np.zeros(points)
    weights = np.zeros((7, points))
    if system_kind == "slope":
        near_weight, far_weight = slope_weights()
        lower[:] = ALPHA_SLOPE
        upper[:] = ALPHA_SLOPE
        weights[1] = -far_weight
        weights[2] = -near_weight
        weights[4] = near_weight
        weights[5] = far_weight
        for edge_row in (1, points - 2):
            lower[edge_row] = 0.25
            upper[edge_row] = 0.25
            weights[:, edge_row] = 0.0
            weights[2, edge_row] = -0.75
            weights[4, edge_row] = 0.75
        lower[0] = 0.0
        upper[0] = 2.0
        weights[:, 0] = 0.0
        weights[3, 0] = -2.5
        weights[4, 0] = 2.0
        weights[5, 0] = 0.5
        lower[points - 1] = 2.0
        upper[points - 1] = 0.0
        weights[:, points - 1] = 0.0
        weights[3, points - 1] = 2.5
        weights[2, points - 1] = -2.0
        weights[1, points - 1] = -0.5
    else:
        strength = ALPHA_FILTER
        lower[:] = strength
        upper[:] = strength
        weights[3] = 11.0 / 16.0 + 5.0 * strength / 8.0
        weights[2] = 15.0 / 64.0 + 17.0 * strength / 32.0
        weights[4] = weights[2]
        weights[1] = -3.0 / 32.0 + 3.0 * strength / 16.0
        weights[5] = weights[1]
        weights[0] = 1.0 / 64.0 - strength / 32.0
        weights[6] = weights[0]
        for edge_row in (2, points - 3):
            weights[:, edge_row] = 0.0
            weights[3, edge_row] = 5.0 / 8.0 + 3.0 * strength / 4.0
            weights[2, edge_row] = 0.25 + strength / 2.0
            weights[4, edge_row] = 0.25 + strength / 2.0
            weights[1, edge_row] = -1.0 / 16.0 + strength / 8.0
            weights[5, edge_row] = -1.0 / 16.0 + strength / 8.0
        for edge_row in (1, points - 2):
            weights[:, edge_row] = 0.0
            weights[3, edge_row] = 0.5 + strength
            weights[2, edge_row] = 0.25 + strength / 2.0
            weights[4, edge_row] = 0.25 + strength / 2.0
        for edge_row in (0, points - 1):
            lower[edge_row] = 0.0
            upper[edge_row] = 0.0
            weights[:, edge_row] = 0.0
            weights[3, edge_row] = 1.0
    return (lower, middle, upper, weights)


def inverse_metric(points):
    places = 2.0 * np.arange(points) / (points - 1) - 1.0
    growth = np.exp(STRETCH * places)
    cosh_values = 0.5 * (growth + 1.0 / growth)
    edge_growth = np.exp(STRETCH)
    tanh_value = (edge_growth - 1.0 / edge_growth) / (edge_growth + 1.0 / edge_growth)
    return tanh_value * cosh_values**2 / (0.64 * STRETCH)


def periodic_matrix(points, spacing):
    near_weight, far_weight = slope_weights()
    wave_numbers = np.arange(1, points // 2)
    angles = 2.0 * np.pi * wave_numbers / points
    modified = (2.0 * near_weight * np.sin(angles) + 2.0 * far_weight * np.sin(2.0 * angles)) / (
        1.0 + 2.0 * ALPHA_SLOPE * np.cos(angles)
    )
    phases = np.arange(points)[:, None] * wave_numbers[None, :] % points
    circulant = -2.0 / (points * spacing) * (np.sin(2.0 * np.pi * phases / points) @ modified)
    shifts = (np.arange(points)[:, None] - np.arange(points)[None, :]) % points
    return circulant[shifts].T


def wall_tables(system_kind, points, rows):
    lower, middle, upper, weights = system_rows(system_kind, points)
    system = np.diag(middle) + np.diag(lower[1:], -1) + np.diag(upper[:-1], 1)
    source = np.zeros((points, points))
    for offset in range(-3, 4):
        for row in range(max(0, -offset), min(points, points - offset)):
            source[row, row + offset] = weights[3 + offset, row]
    band = np.zeros((points, points))
    if system_kind == "slope":
        ratio = slope_weights()[1] / ALPHA_SLOPE
        for row in range(2, points - 2):
            band[row, row + 1] = ratio
            band[row, row - 1] = -ratio
    else:
        mid = points // 2
        strength = ALPHA_FILTER
        two = weights[0, mid] / strength
        one = (weights[1, mid] - two) / strength
        zero = (weights[2, mid] - strength * two - one) / strength
        for row in range(3, points - 3):
            for offset, value in ((0, zero), (1, one), (2, two)):
                band[row, row + offset] = value
                band[row, row - offset] = value
    rest = np.linalg.solve(system, source - system @ band)
    down_ratio = np.zeros(points)
    carried = 0.0
    for row in range(points):
        down_ratio[row] = upper[row] / (middle[row] - lower[row] * carried)
        carried = down_ratio[row]
    up_ratio = np.zeros(points)
    carried = 0.0
    for row in range(points - 1, -1, -1):
        up_ratio[row] = lower[row] / (middle[row] - upper[row] * carried)
        carried = up_ratio[row]
    scale = inverse_metric(points) if system_kind == "slope" else np.ones(points)
    blocks = points // rows
    local = np.zeros((blocks, rows, rows))
    up = np.zeros((blocks, rows))
    down = np.zeros((blocks, rows))
    to_up = np.zeros((blocks, rows))
    to_down = np.zeros((blocks, rows))
    up_gain = np.zeros(blocks)
    down_gain = np.zeros(blocks)
    rim = np.zeros((blocks, 6))
    for block in range(blocks):
        first, last = block * rows, block * rows + rows - 1
        window = slice(first, last + 1)
        local[block] = (rest + band)[window, window] * scale[window, None]
        up[block] = np.cumprod(np.concatenate([[1.0], -up_ratio[first + 1 : last + 1]]))
        up[block] *= scale[window]
        down[block] = np.cumprod(np.concatenate([[1.0], -down_ratio[first:last][::-1]]))[::-1]
        down[block] *= scale[window]
        if block < blocks - 1:
            to_up[block] = rest[last + 1, window]
            up_gain[block] = np.prod(-up_ratio[first + 1 : last + 2])
            rim[block, 3] = band[last, last + 1] * scale[last]
            rim[block, 4] = band[last, last + 2] * scale[last]
            rim[block, 5] = band[last - 1, last + 1] * scale[last - 1]
        if block > 0:
            to_down[block] = rest[first - 1, window]
            down_gain[block] = np.prod(-down_ratio[first - 1 : last])
            rim[block, 0] = band[first, first - 1] * scale[first]
            rim[block, 1] = band[first, first - 2] * scale[first]
            rim[block, 2] = band[first + 1, first - 1] * scale[first + 1]
    return local, up, down, to_up, to_down, up_gain, down_gain, rim


def table_layout(rows):
    sizes = (("local", rows * rows), ("up", rows), ("down", rows), ("to_up", rows), ("to_down", rows), ("rim", 6))
    places, at = {}, 0
    for kind in ("slope", "smooth"):
        for name, size in sizes:
            places[kind, name] = at
            at += size
    places["keep"] = at
    return places, at + rows


def device_table(points, rows):
    places, width = table_layout(rows)
    blocks = points // rows
    table = np.zeros((blocks, width), np.float32)
    gains = {}
    for kind in ("slope", "smooth"):
        local, up, down, to_up, to_down, up_gain, down_gain, rim = wall_tables(kind, points, rows)
        gains[kind] = (up_gain, down_gain)
        named = dict(local=local, up=up, down=down, to_up=to_up, to_down=to_down, rim=rim)
        for name, value in named.items():
            flat = value.reshape(blocks, -1)
            at = places[kind, name]
            table[:, at : at + flat.shape[1]] = flat
    table[:, places["keep"] :] = 1.0
    table[0, places["keep"]] = 0.0
    table[-1, -1] = 0.0
    return table.reshape(-1), gains


def scan_groups(count):
    outer = 4 if count % 4 == 0 else 1
    return outer, count // outer


def gain_tables(kinds, gains, count, tiles, each):
    outer, inner = scan_groups(count)
    fields = len(kinds)
    wide = outer * each
    near = np.zeros((count, inner, wide), np.float32)
    far = np.zeros((count, outer, each), np.float32)

    def chain(tile):
        quantity = min(tile // tiles, 2 * fields - 1)
        back = quantity // fields
        return gains[kinds[quantity % fields]][back].reshape(outer, inner), back

    for group in range(outer):
        for place in range(inner):
            owner = group * inner + place
            for slot in range(wide):
                values, back = chain(place * wide + slot)
                near[owner, :, slot] = values[group][::-1] if back else values[group]
            for slot in range(each):
                values, back = chain((place * outer + group) * each + slot)
                product = values.prod(axis=1)
                far[owner, :, slot] = product[::-1] if back else product
    return near.reshape(-1), far.reshape(-1)


def split_pair(matrix):
    high = matrix.astype(np.float32).astype(ml_dtypes.bfloat16)
    low = (matrix - high.astype(np.float64)).astype(np.float32).astype(ml_dtypes.bfloat16)
    return high, low


def stream_table(points):
    high, low = split_pair(periodic_matrix(points, STREAM_STEP))
    return np.block([[high, low], [high, np.zeros_like(low)]])


def span_table(points):
    own = points // 2
    rows = periodic_matrix(points, SPAN_STEP).T[:own]
    high, low = split_pair(rows)
    return np.block([[high, high], [low, np.zeros_like(low)]])


def halves(value):
    high = value.astype(jnp.bfloat16)
    return high, (value - high.astype(jnp.float32)).astype(jnp.bfloat16)


def fused_body(
    count, starts, rho_hbm, mom_hbm, ene_hbm, tab, mats_hbm,
    rate, smooth,
    rho, mom, ene, mats,
    span_out, span_in, gx, gy, gz, fx, fy, fspan_out, fspan_in,
    rim_out, rim_in, frim_out, frim_in,
    va, ra, oa, sa, vb, rb, ob, sb, vc, rc, oc, sc,
    ta, rta, ota, sta, tb, rtb, otb, stb, tc, rtc, otc, stc,
    s_load, s_span, r_span, s_rim, r_rim, s_line, r_line,
):
    rows, span, _ = rho.shape
    tiles = span // 8
    me, core = lax.axis_index("gy"), lax.axis_index("pa")
    outer, inner = scan_groups(count)
    group, place = me // inner, lax.rem(me, inner)
    places, width = table_layout(rows)
    base = me * width

    def entry(kind, name, at):
        return tab[base + places[kind, name] + at]

    def remote(src, dst, send, recv, target, target_core):
        return pltpu.make_async_remote_copy(
            src_ref=src, dst_ref=dst, send_sem=send, recv_sem=recv,
            device_id=(target, target_core), device_id_type=MESH,
        )

    loads = [
        pltpu.make_async_copy(source, target, s_load.at[at])
        for at, (source, target) in enumerate(
            ((rho_hbm, rho), (mom_hbm, mom), (ene_hbm, ene), (mats_hbm, mats))
        )
    ]
    for load in loads:
        load.start()

    barrier = pltpu.get_barrier_semaphore()

    @pl.loop(1, count)
    def _(step):
        pl.semaphore_signal(
            barrier, inc=1, device_id=(lax.rem(me + step, count), core), device_id_type=MESH
        )

    pl.semaphore_signal(barrier, inc=1, device_id=(me, 1 - core), device_id_type=MESH)

    for load in loads:
        load.wait()

    for depth in range(2):
        for side, row in ((0, rows - 1 - depth), (1, depth)):
            rim_out[side, depth, 0] = rho[row]
            for c in range(3):
                rim_out[side, depth, 1 + c] = mom[c, row]
            rim_out[side, depth, 4] = ene[row]

    @pl.when(me == 0)
    def _():
        rim_in[0] = jnp.ones(rim_in.shape[1:], jnp.float32)
        frim_in[0] = jnp.ones(frim_in.shape[1:], jnp.float32)

    @pl.when(me == count - 1)
    def _():
        rim_in[1] = jnp.ones(rim_in.shape[1:], jnp.float32)
        frim_in[1] = jnp.ones(frim_in.shape[1:], jnp.float32)

    def primitives(d, m0, m1, m2, e):
        inv = 1.0 / d
        u, v, w = m0 * inv, m1 * inv, m2 * inv
        push = (GAMMA_GAS - 1.0) * (e - 0.5 * (u * m0 + v * m1 + w * m2))
        return u, v, w, push * inv

    @pl.loop(0, tiles)
    def _(t):
        z = pl.ds(pl.multiple_of(t * 8, 8), 8)
        ups, downs = [None] * 4, [None] * 4
        for y in range(rows):
            m2 = mom[2, y, z]
            values = primitives(rho[y, z], mom[0, y, z], mom[1, y, z], m2, ene[y, z])
            a, b = entry("slope", "to_up", y), entry("slope", "to_down", y)
            for f in range(4):
                span_out[f, y, z] = values[f]
                ups[f] = a * values[f] if y == 0 else ups[f] + a * values[f]
                downs[f] = b * values[f] if y == 0 else downs[f] + b * values[f]
            span_out[4, y, z] = m2
        for f in range(4):
            va[f * tiles + t] = ups[f]
            va[(4 + f) * tiles + t] = downs[f]

    pl.semaphore_wait(barrier, count)

    def rim_send(source, into, slot):
        def make(side, target):
            return remote(source(side), into(side), s_rim.at[slot, side], r_rim.at[slot, side], target, core)

        @pl.when(me < count - 1)
        def _():
            make(0, me + 1).start()

        @pl.when(me > 0)
        def _():
            make(1, me - 1).start()

    def rim_wait(source, into, slot):
        def make(side, target):
            return remote(source(side), into(side), s_rim.at[slot, side], r_rim.at[slot, side], target, core)

        @pl.when(me < count - 1)
        def _():
            make(0, me + 1).wait_send()
            make(1, me + 1).wait_recv()

        @pl.when(me > 0)
        def _():
            make(1, me - 1).wait_send()
            make(0, me - 1).wait_recv()

    def in_group(at):
        return group * inner + at

    def across(at):
        return at * inner + place

    def spread(src, dst, line, size, mine, device):
        each = src.shape[0] // size
        own = pl.ds(mine * each, each)

        @pl.loop(1, size)
        def _(step):
            to = lax.rem(mine + step, size)
            remote(
                src.at[pl.ds(to * each, each)], dst.at[own],
                s_line.at[line, step], r_line.at[line, step], device(to), core,
            ).start()

        dst[own] = src[own]

    def spread_wait(src, dst, line, size, mine, device):
        each = src.shape[0] // size

        @pl.loop(1, size)
        def _(step):
            to = lax.rem(mine + step, size)
            fro = lax.rem(mine + size - step, size)
            remote(
                src.at[pl.ds(to * each, each)], dst.at[pl.ds(mine * each, each)],
                s_line.at[line, step], r_line.at[line, step], device(to), core,
            ).wait_send()
            remote(
                src.at[pl.ds(to * each, each)], dst.at[pl.ds(fro * each, each)],
                s_line.at[line, step], r_line.at[line, step], device(to), core,
            ).wait_recv()

    def scan(src, first, gain_at, turned, size, emit):
        each = src.shape[0] // size

        def lap(i, carry):
            j = i + turned * (size - 1 - 2 * i)
            emit(j, carry)
            return tuple(
                tab[gain_at + i * each + k] * carry[k] + src[j * each + k] for k in range(each)
            )

        return lax.fori_loop(0, size, lap, first)

    def sender(out, back, line, size, mine, device):
        each = out.shape[0] // size

        def emit(j, carry):
            at = pl.ds(j * each, each)
            for k in range(each):
                out[j * each + k] = carry[k]

            @pl.when(j != mine)
            def _():
                step = lax.rem(j - mine + size, size)
                remote(
                    out.at[at], back.at[pl.ds(mine * each, each)],
                    s_line.at[line, step], r_line.at[line, step], device(j), core,
                ).start()

            @pl.when(j == mine)
            def _():
                back[at] = out[at]

        return emit

    class Lines:
        def __init__(self, at, fields, near, far, values, got, out, back, total, tgot, tout, tback):
            self.values, self.got, self.out, self.back = values, got, out, back
            self.total, self.tgot, self.tout, self.tback = total, tgot, tout, tback
            self.line = 4 * at
            self.each = values.shape[0] // count
            wide = outer * self.each
            self.wide = wide
            self.turned = jnp.minimum((place * wide) // (fields * tiles), 1)
            self.near = near + me * (inner * wide)
            self.far = far + me * (outer * self.each)
            ring, column = (inner, place, in_group), (outer, group, across)
            self.hops = (
                (values, got, self.line, *ring),
                (total, tgot, self.line + 1, *column),
                (tout, tback, self.line + 2, *column),
                (out, back, self.line + 3, *ring),
            )

        def start(self):
            spread(*self.hops[0])

        def wait(self, hop):
            spread_wait(*self.hops[hop])

        def gather(self):
            self.wait(0)
            zeros = tuple(jnp.zeros((8, 128), jnp.float32) for _ in range(self.wide))
            total = scan(self.got, zeros, self.near, self.turned, inner, lambda j, carry: None)
            for k in range(self.wide):
                self.total[k] = total[k]
            spread(*self.hops[1])

        def cross(self):
            self.wait(1)
            zeros = tuple(jnp.zeros((8, 128), jnp.float32) for _ in range(self.each))
            scan(self.tgot, zeros, self.far, self.turned, outer, sender(*self.hops[2]))

        def give(self):
            self.wait(2)
            first = tuple(self.tback[k] for k in range(self.wide))
            scan(self.got, first, self.near, self.turned, inner, sender(*self.hops[3]))

        def finish(self):
            self.wait(3)

    near_a, far_a, near_b, far_b = starts
    lines_a = Lines(0, 4, near_a, far_a, va, ra, oa, sa, ta, rta, ota, sta)
    lines_b = Lines(1, 6, near_b, far_b, vb, rb, ob, sb, tb, rtb, otb, stb)
    lines_c = Lines(2, 4, near_a, far_a, vc, rc, oc, sc, tc, rtc, otc, stc)

    rim_a = (lambda side: rim_out.at[side, 0], lambda side: rim_in.at[side, 0], 0)
    rim_b = (lambda side: rim_out.at[side, 1], lambda side: rim_in.at[side, 1], 1)
    rim_c = (lambda side: frim_out.at[side], lambda side: frim_in.at[side], 2)
    span_copy = remote(span_out, span_in, s_span.at[0], r_span.at[0], me, 1 - core)
    fspan_copy = remote(fspan_out, fspan_in, s_span.at[1], r_span.at[1], me, 1 - core)

    lines_a.start()
    rim_send(*rim_a)
    span_copy.start()

    def local_rows(kind, load, store, z):
        values = [load(y) for y in range(rows)]
        for y in range(rows):
            total = entry(kind, "local", y * rows) * values[0]
            for k in range(1, rows):
                total = total + entry(kind, "local", y * rows + k) * values[k]
            store(y, total)

    def block_loop(fields, size, body):
        per = span // size

        @pl.loop(0, fields * per)
        def _(i):
            body(i // per, pl.ds(pl.multiple_of((i % per) * size, size), size))

    def slope_block(src, dst):
        def body(f, z):
            def store(y, total):
                dst[f, y, z] = total

            local_rows("slope", lambda y: src[f, y, z], store, z)

        return body

    def stream_rows(value):
        high, low = halves(value)
        product = jnp.dot(
            jnp.concatenate([high, low], axis=1), mats[pl.ds(0, 256)], preferred_element_type=jnp.float32
        )
        return product[:, :128] + product[:, 128:]

    def stream_loop(fields, load, store):
        @pl.loop(0, fields * rows // 4)
        def _(i):
            f, y = i // (rows // 4), (i % (rows // 4)) * 4
            block = jnp.concatenate([load(f, y + k) for k in range(4)], axis=0)
            product = stream_rows(block)
            for k in range(4):
                store(f, y + k, product[k * span : (k + 1) * span])

    def span_loop(fields, own, other, store):
        @pl.loop(0, fields * rows // 2)
        def _(i):
            f, y = i // (rows // 2), (i % (rows // 2)) * 2
            parts = [
                halves(jnp.concatenate([ref[f, y], ref[f, y + 1]], axis=1)) for ref in (own, other)
            ]
            stacked = jnp.concatenate([parts[0][0], parts[1][0], parts[0][1], parts[1][1]], axis=0)
            product = jnp.dot(mats[pl.ds(256, 128)], stacked, preferred_element_type=jnp.float32)
            product = product[:span] + product[span:]
            store(f, y, product[:, :128])
            store(f, y + 1, product[:, 128:])

    def store_gx(f, y, value):
        gx[f, y] = value

    def store_gz(f, y, value):
        gz[f, y] = value

    stream_loop(4, lambda f, y: span_out[f, y], store_gx)
    lines_a.gather()

    @pl.loop(0, tiles)
    def _(t):
        z = pl.ds(pl.multiple_of(t * 8, 8), 8)
        ups, downs = [None] * 6, [None] * 6
        for y in range(rows):
            middle = mom[1, y, z]
            values = (rho[y, z], mom[0, y, z], middle, mom[2, y, z], ene[y, z], middle)
            pairs = [
                (entry(kind, "to_up", y), entry(kind, "to_down", y)) for kind in ("smooth", "slope")
            ]
            for f in range(6):
                a, b = pairs[f // 5]
                ups[f] = a * values[f] if y == 0 else ups[f] + a * values[f]
                downs[f] = b * values[f] if y == 0 else downs[f] + b * values[f]
        for f in range(6):
            vb[f * tiles + t] = ups[f]
            vb[(6 + f) * tiles + t] = downs[f]

    lines_b.start()
    lines_a.cross()
    block_loop(4, 16, slope_block(span_out, gy))
    lines_a.give()
    lines_b.gather()
    rim_send(*rim_b)

    span_copy.wait()
    span_loop(5, span_out, span_in, store_gz)

    rim_wait(*rim_a)
    for side, row in ((0, 0), (1, rows - 1)):
        weight = entry("slope", "rim", 3 * side)
        values = primitives(*(rim_in[side, 0, f] for f in range(5)))
        for f in range(4):
            gy[f, row] += weight * values[f]

    lines_a.finish()

    @pl.loop(0, tiles)
    def _(t):
        z = pl.ds(pl.multiple_of(t * 8, 8), 8)
        ups, downs = [None] * 4, [None] * 4
        from_up = [sa[f * tiles + t] for f in range(4)]
        from_down = [sa[(4 + f) * tiles + t] for f in range(4)]
        for y in range(rows):
            a, b = entry("slope", "up", y), entry("slope", "down", y)
            u = [span_out[f, y, z] for f in range(4)]
            m = [mom[c, y, z] for c in range(3)]
            e = ene[y, z]
            push = rho[y, z] * u[3]
            grad = (
                [gx[f, y, z] for f in range(4)],
                [gy[f, y, z] + a * from_up[f] + b * from_down[f] for f in range(4)],
                [gz[f, y, z] for f in range(4)],
            )
            spread_out = (2.0 / 3.0 * VISCOSITY) * (grad[0][0] + grad[1][1] + grad[2][2])
            stress = [[None] * 3 for _ in range(3)]
            for c in range(3):
                stress[c][c] = (2.0 * VISCOSITY) * grad[c][c] - spread_out
                for d in range(c):
                    stress[c][d] = stress[d][c] = VISCOSITY * (grad[d][c] + grad[c][d])
            heat = e + push
            a, b = entry("slope", "to_up", y), entry("slope", "to_down", y)
            for d, out in ((0, fx), (1, fy), (2, fspan_out)):
                energy = heat * u[d] - CONDUCT * grad[d][3]
                for c in range(3):
                    energy = energy - u[c] * stress[c][d]
                values = []
                for c in range(3):
                    value = m[c] * u[d] - stress[c][d]
                    values.append(value + push if c == d else value)
                values.append(energy)
                for f in range(4):
                    out[f, y, z] = values[f]
                    if d == 1:
                        ups[f] = a * values[f] if y == 0 else ups[f] + a * values[f]
                        downs[f] = b * values[f] if y == 0 else downs[f] + b * values[f]
                        if y == rows - 1:
                            frim_out[0, f, z] = values[f]
                        if y == 0:
                            frim_out[1, f, z] = values[f]
        for f in range(4):
            vc[f * tiles + t] = ups[f]
            vc[(4 + f) * tiles + t] = downs[f]

    lines_c.start()
    rim_send(*rim_c)
    fspan_copy.start()

    lines_b.cross()

    def store_fx(f, y, value):
        gx[f, y] = value

    stream_loop(4, lambda f, y: fx[f, y], store_fx)
    lines_c.gather()
    block_loop(4, 16, slope_block(fy, gy))
    lines_c.cross()
    lines_b.give()

    def store_mass(f, y, value):
        rate[0, y] = value

    stream_loop(1, lambda f, y: mom[0, y], store_mass)

    def mass_block(f, z):
        def store(y, total):
            rate[0, y, z] = -(rate[0, y, z] + total + gz[4, y, z])

        local_rows("slope", lambda y: mom[1, y, z], store, z)

    block_loop(1, 16, mass_block)

    lines_c.give()

    def smooth_block(read, write):
        def body(f, z):
            def store(y, total):
                write[y, z] = total

            local_rows("smooth", lambda y: read[y, z], store, z)

        return body

    block_loop(1, 16, smooth_block(rho, smooth.at[0]))

    def smooth_mom(f, z):
        def store(y, total):
            smooth[1 + f, y, z] = total

        local_rows("smooth", lambda y: mom[f, y, z], store, z)

    block_loop(3, 16, smooth_mom)
    block_loop(1, 16, smooth_block(ene, smooth.at[4]))
    rim_wait(*rim_b)
    for side, edge, inner in ((0, 0, 1), (1, rows - 1, rows - 2)):
        near, far, second = (entry("smooth", "rim", 3 * side + k) for k in range(3))
        for f in range(5):
            smooth[f, edge] += near * rim_in[side, 0, f] + far * rim_in[side, 1, f]
            smooth[f, inner] += second * rim_in[side, 0, f]
        rate[0, edge] -= entry("slope", "rim", 3 * side) * rim_in[side, 0, 2]

    lines_b.finish()

    @pl.loop(0, tiles)
    def _(t):
        z = pl.ds(pl.multiple_of(t * 8, 8), 8)
        from_up = [sb[f * tiles + t] for f in range(6)]
        from_down = [sb[(6 + f) * tiles + t] for f in range(6)]
        for y in range(rows):
            a, b = entry("smooth", "up", y), entry("smooth", "down", y)
            for f in range(5):
                smooth[f, y, z] += a * from_up[f] + b * from_down[f]
            a, b = entry("slope", "up", y), entry("slope", "down", y)
            rate[0, y, z] -= a * from_up[5] + b * from_down[5]

    fspan_copy.wait()
    span_loop(4, fspan_out, fspan_in, store_gz)
    rim_wait(*rim_c)
    for side, row in ((0, 0), (1, rows - 1)):
        weight = entry("slope", "rim", 3 * side)
        for f in range(4):
            gy[f, row] += weight * frim_in[side, f]

    lines_c.finish()

    @pl.loop(0, tiles)
    def _(t):
        z = pl.ds(pl.multiple_of(t * 8, 8), 8)
        from_up = [sc[f * tiles + t] for f in range(4)]
        from_down = [sc[(4 + f) * tiles + t] for f in range(4)]
        for y in range(rows):
            a, b = entry("slope", "up", y), entry("slope", "down", y)
            keep = tab[base + places["keep"] + y]
            for f in range(4):
                total = gx[f, y, z] + gz[f, y, z] + gy[f, y, z] + a * from_up[f] + b * from_down[f]
                rate[1 + f, y, z] = -(total * keep) if f < 3 else -total


def per_device(mass_per_volume, mass_flux_vector, total_heat_content):
    rows, span, stream = mass_per_volume.shape
    count = lax.axis_size("gy")
    tiles = span // 8
    table, gains = device_table(rows * count, rows)
    each_a = -(-8 * tiles // count)
    each_b = -(-12 * tiles // count)
    pieces = [table]
    for kinds, each in ((["slope"] * 4, each_a), (["smooth"] * 5 + ["slope"], each_b)):
        pieces += gain_tables(kinds, gains, count, tiles, each)
    starts = tuple(int(at) for at in np.cumsum([piece.size for piece in pieces[:-1]]))
    field = (rows, span, stream)
    mats = np.concatenate([stream_table(stream), span_table(2 * span)])
    outer, inner = scan_groups(count)

    def vmem(*shape):
        return pltpu.VMEM(shape, jnp.float32)

    lines_a = [vmem(count * each_a, 8, stream)] * 4
    lines_b = [vmem(count * each_b, 8, stream)] * 4
    totals_a = [vmem(outer * each_a, 8, stream)] * 4
    totals_b = [vmem(outer * each_b, 8, stream)] * 4
    whole = pl.BlockSpec(memory_space=pltpu.VMEM)
    scalar = pl.BlockSpec(memory_space=pltpu.SMEM)
    outside = pl.BlockSpec(memory_space=pl.ANY)
    dma = pltpu.SemaphoreType.DMA
    out = jax.ShapeDtypeStruct((5,) + field, jnp.float32)
    return pl.pallas_call(
        functools.partial(fused_body, count, starts),
        out_shape=(out, out),
        in_specs=[outside] * 3 + [scalar, outside],
        out_specs=(whole, whole),
        scratch_shapes=[
            vmem(*field), vmem(3, *field), vmem(*field), pltpu.VMEM(mats.shape, jnp.bfloat16),
            vmem(5, *field), vmem(5, *field), vmem(4, *field), vmem(4, *field), vmem(5, *field),
            vmem(4, *field), vmem(4, *field), vmem(4, *field), vmem(4, *field),
            vmem(2, 2, 5, span, stream), vmem(2, 2, 5, span, stream),
            vmem(2, 4, span, stream), vmem(2, 4, span, stream),
            *lines_a, *lines_b, *lines_a,
            *totals_a, *totals_b, *totals_a,
            dma((4,)), dma((2,)), dma((2,)), dma((3, 2)), dma((3, 2)),
            dma((12, max(inner, outer))), dma((12, max(inner, outer))),
        ],
        compiler_params=pltpu.CompilerParams(
            collective_id=0, has_side_effects=True, vmem_limit_bytes=56 * 1024 * 1024
        ),
    )(
        mass_per_volume, mass_flux_vector, total_heat_content,
        jnp.asarray(np.concatenate(pieces)), jnp.asarray(mats),
    )


def solution(mesh):
    placed = (P("gy", "pa", None), P(None, "gy", "pa", None), P("gy", "pa", None))
    return jax.shard_map(
        per_device,
        mesh=mesh,
        in_specs=placed,
        out_specs=(P(None, "gy", "pa", None), P(None, "gy", "pa", None)),
        check_vma=False,
    )
```

```python
import functools

import jax
import jax.numpy as jnp
import ml_dtypes
import numpy as np
from jax import lax
from jax.experimental import pallas as pl
from jax.experimental.pallas import tpu as pltpu
from jax.sharding import PartitionSpec as P

GAMMA_GAS = 1.4
PRANDTL = 0.72
VISCOSITY = 0.25
ALPHA_FILTER = 0.499
ALPHA_SLOPE = 0.498
STRETCH = 1.2
STREAM_STEP = 1.0
SPAN_STEP = 0.5
CONDUCT = VISCOSITY * GAMMA_GAS / ((GAMMA_GAS - 1.0) * PRANDTL)
MESH = pl.DeviceIdType.MESH


def slope_weights():
    near_weight = (2.0 + ALPHA_SLOPE) / 3.0
    far_weight = (4.0 * ALPHA_SLOPE - 1.0) / 12.0
    return (near_weight, far_weight)


def system_rows(system_kind, points):
    lower = np.zeros(points)
    middle = np.ones(points)
    upper = np.zeros(points)
    weights = np.zeros((7, points))
    if system_kind == "slope":
        near_weight, far_weight = slope_weights()
        lower[:] = ALPHA_SLOPE
        upper[:] = ALPHA_SLOPE
        weights[1] = -far_weight
        weights[2] = -near_weight
        weights[4] = near_weight
        weights[5] = far_weight
        for edge_row in (1, points - 2):
            lower[edge_row] = 0.25
            upper[edge_row] = 0.25
            weights[:, edge_row] = 0.0
            weights[2, edge_row] = -0.75
            weights[4, edge_row] = 0.75
        lower[0] = 0.0
        upper[0] = 2.0
        weights[:, 0] = 0.0
        weights[3, 0] = -2.5
        weights[4, 0] = 2.0
        weights[5, 0] = 0.5
        lower[points - 1] = 2.0
        upper[points - 1] = 0.0
        weights[:, points - 1] = 0.0
        weights[3, points - 1] = 2.5
        weights[2, points - 1] = -2.0
        weights[1, points - 1] = -0.5
    else:
        strength = ALPHA_FILTER
        lower[:] = strength
        upper[:] = strength
        weights[3] = 11.0 / 16.0 + 5.0 * strength / 8.0
        weights[2] = 15.0 / 64.0 + 17.0 * strength / 32.0
        weights[4] = weights[2]
        weights[1] = -3.0 / 32.0 + 3.0 * strength / 16.0
        weights[5] = weights[1]
        weights[0] = 1.0 / 64.0 - strength / 32.0
        weights[6] = weights[0]
        for edge_row in (2, points - 3):
            weights[:, edge_row] = 0.0
            weights[3, edge_row] = 5.0 / 8.0 + 3.0 * strength / 4.0
            weights[2, edge_row] = 0.25 + strength / 2.0
            weights[4, edge_row] = 0.25 + strength / 2.0
            weights[1, edge_row] = -1.0 / 16.0 + strength / 8.0
            weights[5, edge_row] = -1.0 / 16.0 + strength / 8.0
        for edge_row in (1, points - 2):
            weights[:, edge_row] = 0.0
            weights[3, edge_row] = 0.5 + strength
            weights[2, edge_row] = 0.25 + strength / 2.0
            weights[4, edge_row] = 0.25 + strength / 2.0
        for edge_row in (0, points - 1):
            lower[edge_row] = 0.0
            upper[edge_row] = 0.0
            weights[:, edge_row] = 0.0
            weights[3, edge_row] = 1.0
    return (lower, middle, upper, weights)


def inverse_metric(points):
    places = 2.0 * np.arange(points) / (points - 1) - 1.0
    growth = np.exp(STRETCH * places)
    cosh_values = 0.5 * (growth + 1.0 / growth)
    edge_growth = np.exp(STRETCH)
    tanh_value = (edge_growth - 1.0 / edge_growth) / (edge_growth + 1.0 / edge_growth)
    return tanh_value * cosh_values**2 / (0.64 * STRETCH)


def periodic_matrix(points, spacing):
    near_weight, far_weight = slope_weights()
    wave_numbers = np.arange(1, points // 2)
    angles = 2.0 * np.pi * wave_numbers / points
    modified = (2.0 * near_weight * np.sin(angles) + 2.0 * far_weight * np.sin(2.0 * angles)) / (
        1.0 + 2.0 * ALPHA_SLOPE * np.cos(angles)
    )
    phases = np.arange(points)[:, None] * wave_numbers[None, :] % points
    circulant = -2.0 / (points * spacing) * (np.sin(2.0 * np.pi * phases / points) @ modified)
    shifts = (np.arange(points)[:, None] - np.arange(points)[None, :]) % points
    return circulant[shifts].T


def wall_tables(system_kind, points, rows):
    lower, middle, upper, weights = system_rows(system_kind, points)
    system = np.diag(middle) + np.diag(lower[1:], -1) + np.diag(upper[:-1], 1)
    source = np.zeros((points, points))
    for offset in range(-3, 4):
        for row in range(max(0, -offset), min(points, points - offset)):
            source[row, row + offset] = weights[3 + offset, row]
    band = np.zeros((points, points))
    if system_kind == "slope":
        ratio = slope_weights()[1] / ALPHA_SLOPE
        for row in range(2, points - 2):
            band[row, row + 1] = ratio
            band[row, row - 1] = -ratio
    else:
        mid = points // 2
        strength = ALPHA_FILTER
        two = weights[0, mid] / strength
        one = (weights[1, mid] - two) / strength
        zero = (weights[2, mid] - strength * two - one) / strength
        for row in range(3, points - 3):
            for offset, value in ((0, zero), (1, one), (2, two)):
                band[row, row + offset] = value
                band[row, row - offset] = value
    rest = np.linalg.solve(system, source - system @ band)
    down_ratio = np.zeros(points)
    carried = 0.0
    for row in range(points):
        down_ratio[row] = upper[row] / (middle[row] - lower[row] * carried)
        carried = down_ratio[row]
    up_ratio = np.zeros(points)
    carried = 0.0
    for row in range(points - 1, -1, -1):
        up_ratio[row] = lower[row] / (middle[row] - upper[row] * carried)
        carried = up_ratio[row]
    scale = inverse_metric(points) if system_kind == "slope" else np.ones(points)
    blocks = points // rows
    local = np.zeros((blocks, rows, rows))
    up = np.zeros((blocks, rows))
    down = np.zeros((blocks, rows))
    to_up = np.zeros((blocks, rows))
    to_down = np.zeros((blocks, rows))
    up_gain = np.zeros(blocks)
    down_gain = np.zeros(blocks)
    rim = np.zeros((blocks, 6))
    next_row = np.zeros((blocks, 12))
    near, far = slope_weights()
    for block in range(blocks):
        first, last = block * rows, block * rows + rows - 1
        window = slice(first, last + 1)
        local[block] = (rest + band)[window, window] * scale[window, None]
        up[block] = np.cumprod(np.concatenate([[1.0], -up_ratio[first + 1 : last + 1]]))
        up[block] *= scale[window]
        down[block] = np.cumprod(np.concatenate([[1.0], -down_ratio[first:last][::-1]]))[::-1]
        down[block] *= scale[window]
        if block < blocks - 1:
            to_up[block] = rest[last + 1, window]
            up_gain[block] = np.prod(-up_ratio[first + 1 : last + 2])
            rim[block, 3] = band[last, last + 1] * scale[last]
            rim[block, 4] = band[last, last + 2] * scale[last]
            rim[block, 5] = band[last - 1, last + 1] * scale[last - 1]
            unit = scale[last + 1] / ALPHA_SLOPE
            next_row[block, 6:] = unit * np.array(
                [near, -near, far, -far, -1.0 / scale[last], -ALPHA_SLOPE / scale[last - 1]]
            )
        if block > 0:
            to_down[block] = rest[first - 1, window]
            down_gain[block] = np.prod(-down_ratio[first - 1 : last])
            rim[block, 0] = band[first, first - 1] * scale[first]
            rim[block, 1] = band[first, first - 2] * scale[first]
            rim[block, 2] = band[first + 1, first - 1] * scale[first + 1]
            unit = scale[first - 1] / ALPHA_SLOPE
            next_row[block, :6] = unit * np.array(
                [-near, near, -far, far, -1.0 / scale[first], -ALPHA_SLOPE / scale[first + 1]]
            )
    return local, up, down, to_up, to_down, up_gain, down_gain, rim, next_row


def table_layout(rows):
    sizes = (("local", rows * rows), ("up", rows), ("down", rows), ("to_up", rows), ("to_down", rows), ("rim", 6), ("next", 12))
    places, at = {}, 0
    for kind in ("slope", "smooth"):
        for name, size in sizes:
            places[kind, name] = at
            at += size
    places["keep"] = at
    return places, at + rows


def device_table(points, rows):
    places, width = table_layout(rows)
    blocks = points // rows
    table = np.zeros((blocks, width), np.float32)
    gains = {}
    for kind in ("slope", "smooth"):
        local, up, down, to_up, to_down, up_gain, down_gain, rim, beyond = wall_tables(kind, points, rows)
        gains[kind] = (up_gain, down_gain)
        named = dict(local=local, up=up, down=down, to_up=to_up, to_down=to_down, rim=rim, next=beyond)
        for name, value in named.items():
            flat = value.reshape(blocks, -1)
            at = places[kind, name]
            table[:, at : at + flat.shape[1]] = flat
    table[:, places["keep"] :] = 1.0
    table[0, places["keep"]] = 0.0
    table[-1, -1] = 0.0
    return table.reshape(-1), gains


def scan_groups(count):
    outer = 4 if count % 4 == 0 else 1
    return outer, count // outer


def gain_tables(kinds, gains, count, tiles, each):
    outer, inner = scan_groups(count)
    fields = len(kinds)
    wide = outer * each
    near = np.zeros((count, inner, wide), np.float32)
    far = np.zeros((count, outer, each), np.float32)

    def chain(tile):
        quantity = min(tile // tiles, 2 * fields - 1)
        back = quantity // fields
        return gains[kinds[quantity % fields]][back].reshape(outer, inner), back

    for group in range(outer):
        for place in range(inner):
            owner = group * inner + place
            for slot in range(wide):
                values, back = chain(place * wide + slot)
                near[owner, :, slot] = values[group][::-1] if back else values[group]
            for slot in range(each):
                values, back = chain((place * outer + group) * each + slot)
                product = values.prod(axis=1)
                far[owner, :, slot] = product[::-1] if back else product
    return near.reshape(-1), far.reshape(-1)


def split_pair(matrix):
    high = matrix.astype(np.float32).astype(ml_dtypes.bfloat16)
    low = (matrix - high.astype(np.float64)).astype(np.float32).astype(ml_dtypes.bfloat16)
    return high, low


def stream_table(points):
    high, low = split_pair(periodic_matrix(points, STREAM_STEP))
    return np.block([[high, low], [high, np.zeros_like(low)]])


def span_table(points):
    own = points // 2
    rows = periodic_matrix(points, SPAN_STEP).T[:own]
    high, low = split_pair(rows)
    return np.block([[high, high], [low, np.zeros_like(low)]])


def halves(value):
    high = value.astype(jnp.bfloat16)
    return high, (value - high.astype(jnp.float32)).astype(jnp.bfloat16)


def fused_body(
    count, starts, rho_hbm, mom_hbm, ene_hbm, tab, mats_hbm,
    rate_hbm, smooth_hbm,
    rate, smooth, rho, mom, ene, mats,
    span_out, span_in, gx, gy, gz, fx, fy, gf, fspan_out, fspan_in,
    rim_out, rim_in, edge_out, edge_in, edge_x, edge_z,
    va, ra, oa, sa, vb, rb, ob, sb, vc, rc, oc, sc,
    ta, rta, ota, sta, tb, rtb, otb, stb, tc, rtc, otc, stc,
    s_load, s_span, r_span, s_rim, r_rim, s_line, r_line,
):
    rows, span, _ = rho.shape
    tiles = span // 8
    me, core = lax.axis_index("gy"), lax.axis_index("pa")
    outer, inner = scan_groups(count)
    group, place = me // inner, lax.rem(me, inner)
    places, width = table_layout(rows)
    base = me * width

    def entry(kind, name, at):
        return tab[base + places[kind, name] + at]

    def remote(src, dst, send, recv, target, target_core):
        return pltpu.make_async_remote_copy(
            src_ref=src, dst_ref=dst, send_sem=send, recv_sem=recv,
            device_id=(target, target_core), device_id_type=MESH,
        )

    loads = [
        pltpu.make_async_copy(source, target, s_load.at[at])
        for at, (source, target) in enumerate(
            ((rho_hbm, rho), (mom_hbm, mom), (ene_hbm, ene), (mats_hbm, mats))
        )
    ]
    for load in loads:
        load.start()

    barrier = pltpu.get_barrier_semaphore()

    @pl.loop(1, count)
    def _(step):
        pl.semaphore_signal(
            barrier, inc=1, device_id=(lax.rem(me + step, count), core), device_id_type=MESH
        )

    pl.semaphore_signal(barrier, inc=1, device_id=(me, 1 - core), device_id_type=MESH)

    for load in loads:
        load.wait()

    for depth in range(2):
        for side, row in ((0, rows - 1 - depth), (1, depth)):
            rim_out[side, depth, 0] = rho[row]
            for c in range(3):
                rim_out[side, depth, 1 + c] = mom[c, row]
            rim_out[side, depth, 4] = ene[row]

    @pl.when(me == 0)
    def _():
        rim_in[0] = jnp.ones(rim_in.shape[1:], jnp.float32)

    @pl.when(me == count - 1)
    def _():
        rim_in[1] = jnp.ones(rim_in.shape[1:], jnp.float32)

    def primitives(d, m0, m1, m2, e):
        inv = 1.0 / d
        u, v, w = m0 * inv, m1 * inv, m2 * inv
        push = (GAMMA_GAS - 1.0) * (e - 0.5 * (u * m0 + v * m1 + w * m2))
        return u, v, w, push * inv

    @pl.loop(0, tiles)
    def _(t):
        z = pl.ds(pl.multiple_of(t * 8, 8), 8)
        ups, downs = [None] * 4, [None] * 4
        for y in range(rows):
            m2 = mom[2, y, z]
            values = primitives(rho[y, z], mom[0, y, z], mom[1, y, z], m2, ene[y, z])
            a, b = entry("slope", "to_up", y), entry("slope", "to_down", y)
            for f in range(4):
                span_out[f, y, z] = values[f]
                ups[f] = a * values[f] if y == 0 else ups[f] + a * values[f]
                downs[f] = b * values[f] if y == 0 else downs[f] + b * values[f]
            span_out[4, y, z] = m2
        for f in range(4):
            va[f * tiles + t] = ups[f]
            va[(4 + f) * tiles + t] = downs[f]

    pl.semaphore_wait(barrier, count)

    def rim_send(source, into, slot):
        def make(side, target):
            return remote(source(side), into(side), s_rim.at[slot, side], r_rim.at[slot, side], target, core)

        @pl.when(me < count - 1)
        def _():
            make(0, me + 1).start()

        @pl.when(me > 0)
        def _():
            make(1, me - 1).start()

    def rim_wait(source, into, slot):
        def make(side, target):
            return remote(source(side), into(side), s_rim.at[slot, side], r_rim.at[slot, side], target, core)

        @pl.when(me < count - 1)
        def _():
            make(0, me + 1).wait_send()
            make(1, me + 1).wait_recv()

        @pl.when(me > 0)
        def _():
            make(1, me - 1).wait_send()
            make(0, me - 1).wait_recv()

    def in_group(at):
        return group * inner + at

    def across(at):
        return at * inner + place

    def spread(src, dst, line, size, mine, device):
        each = src.shape[0] // size
        own = pl.ds(mine * each, each)

        @pl.loop(1, size)
        def _(step):
            to = lax.rem(mine + step, size)
            remote(
                src.at[pl.ds(to * each, each)], dst.at[own],
                s_line.at[line, step], r_line.at[line, step], device(to), core,
            ).start()

        dst[own] = src[own]

    def spread_wait(src, dst, line, size, mine, device):
        each = src.shape[0] // size

        @pl.loop(1, size)
        def _(step):
            to = lax.rem(mine + step, size)
            fro = lax.rem(mine + size - step, size)
            remote(
                src.at[pl.ds(to * each, each)], dst.at[pl.ds(mine * each, each)],
                s_line.at[line, step], r_line.at[line, step], device(to), core,
            ).wait_send()
            remote(
                src.at[pl.ds(to * each, each)], dst.at[pl.ds(fro * each, each)],
                s_line.at[line, step], r_line.at[line, step], device(to), core,
            ).wait_recv()

    def scan(src, first, gain_at, turned, size, emit):
        each = src.shape[0] // size

        def lap(i, carry):
            j = i + turned * (size - 1 - 2 * i)
            emit(j, carry)
            return tuple(
                tab[gain_at + i * each + k] * carry[k] + src[j * each + k] for k in range(each)
            )

        return lax.fori_loop(0, size, lap, first)

    def sender(out, back, line, size, mine, device):
        each = out.shape[0] // size

        def emit(j, carry):
            at = pl.ds(j * each, each)
            for k in range(each):
                out[j * each + k] = carry[k]

            @pl.when(j != mine)
            def _():
                step = lax.rem(j - mine + size, size)
                remote(
                    out.at[at], back.at[pl.ds(mine * each, each)],
                    s_line.at[line, step], r_line.at[line, step], device(j), core,
                ).start()

            @pl.when(j == mine)
            def _():
                back[at] = out[at]

        return emit

    class Lines:
        def __init__(self, at, fields, near, far, values, got, out, back, total, tgot, tout, tback):
            self.values, self.got, self.out, self.back = values, got, out, back
            self.total, self.tgot, self.tout, self.tback = total, tgot, tout, tback
            self.line = 4 * at
            self.each = values.shape[0] // count
            wide = outer * self.each
            self.wide = wide
            self.turned = jnp.minimum((place * wide) // (fields * tiles), 1)
            self.near = near + me * (inner * wide)
            self.far = far + me * (outer * self.each)
            ring, column = (inner, place, in_group), (outer, group, across)
            self.hops = (
                (values, got, self.line, *ring),
                (total, tgot, self.line + 1, *column),
                (tout, tback, self.line + 2, *column),
                (out, back, self.line + 3, *ring),
            )

        def start(self):
            spread(*self.hops[0])

        def wait(self, hop):
            spread_wait(*self.hops[hop])

        def gather(self):
            self.wait(0)
            zeros = tuple(jnp.zeros((8, 128), jnp.float32) for _ in range(self.wide))
            total = scan(self.got, zeros, self.near, self.turned, inner, lambda j, carry: None)
            for k in range(self.wide):
                self.total[k] = total[k]
            spread(*self.hops[1])

        def cross(self):
            self.wait(1)
            zeros = tuple(jnp.zeros((8, 128), jnp.float32) for _ in range(self.each))
            scan(self.tgot, zeros, self.far, self.turned, outer, sender(*self.hops[2]))

        def give(self):
            self.wait(2)
            first = tuple(self.tback[k] for k in range(self.wide))
            scan(self.got, first, self.near, self.turned, inner, sender(*self.hops[3]))

        def finish(self):
            self.wait(3)

    near_a, far_a, near_b, far_b = starts
    lines_a = Lines(0, 4, near_a, far_a, va, ra, oa, sa, ta, rta, ota, sta)
    lines_b = Lines(1, 6, near_b, far_b, vb, rb, ob, sb, tb, rtb, otb, stb)
    lines_c = Lines(2, 4, near_a, far_a, vc, rc, oc, sc, tc, rtc, otc, stc)

    rim_a = (lambda side: rim_out.at[side, 0], lambda side: rim_in.at[side, 0], 0)
    rim_b = (lambda side: rim_out.at[side, 1], lambda side: rim_in.at[side, 1], 1)
    span_copy = remote(span_out, span_in, s_span.at[0], r_span.at[0], me, 1 - core)
    fspan_copy = remote(fspan_out, fspan_in, s_span.at[1], r_span.at[1], me, 1 - core)
    edge_copy = remote(edge_out, edge_in, s_span.at[2], r_span.at[2], me, 1 - core)

    lines_a.start()
    span_copy.start()

    def local_rows(kind, load, store, z):
        values = [load(y) for y in range(rows)]
        for y in range(rows):
            total = entry(kind, "local", y * rows) * values[0]
            for k in range(1, rows):
                total = total + entry(kind, "local", y * rows + k) * values[k]
            store(y, total)

    def block_loop(fields, size, body):
        per = span // size

        @pl.loop(0, fields * per)
        def _(i):
            body(i // per, pl.ds(pl.multiple_of((i % per) * size, size), size))

    def slope_block(src, dst):
        def body(f, z):
            def store(y, total):
                dst[f, y, z] = total

            local_rows("slope", lambda y: src[f, y, z], store, z)

        return body

    def stream_rows(value):
        high, low = halves(value)
        product = jnp.dot(
            jnp.concatenate([high, low], axis=1), mats[pl.ds(0, 256)], preferred_element_type=jnp.float32
        )
        return product[:, :128] + product[:, 128:]

    def stream_loop(fields, load, store):
        @pl.loop(0, fields * rows // 4)
        def _(i):
            f, y = i // (rows // 4), (i % (rows // 4)) * 4
            block = jnp.concatenate([load(f, y + k) for k in range(4)], axis=0)
            product = stream_rows(block)
            for k in range(4):
                store(f, y + k, product[k * span : (k + 1) * span])

    def span_pair(own, other):
        parts = [halves(jnp.concatenate(pair, axis=1)) for pair in (own, other)]
        stacked = jnp.concatenate([parts[0][0], parts[1][0], parts[0][1], parts[1][1]], axis=0)
        product = jnp.dot(mats[pl.ds(256, 128)], stacked, preferred_element_type=jnp.float32)
        product = product[:span] + product[span:]
        return product[:, :128], product[:, 128:]

    def span_loop(fields, own, other, store):
        @pl.loop(0, fields * rows // 2)
        def _(i):
            f, y = i // (rows // 2), (i % (rows // 2)) * 2
            pair = span_pair((own[f, y], own[f, y + 1]), (other[f, y], other[f, y + 1]))
            store(f, y, pair[0])
            store(f, y + 1, pair[1])

    def store_gx(f, y, value):
        gx[f, y] = value

    def store_gz(f, y, value):
        gz[f, y] = value

    stream_loop(4, lambda f, y: span_out[f, y], store_gx)
    lines_a.gather()
    rim_send(*rim_a)

    @pl.loop(0, tiles)
    def _(t):
        z = pl.ds(pl.multiple_of(t * 8, 8), 8)
        ups, downs = [None] * 6, [None] * 6
        for y in range(rows):
            middle = mom[1, y, z]
            values = (rho[y, z], mom[0, y, z], middle, mom[2, y, z], ene[y, z], middle)
            pairs = [
                (entry(kind, "to_up", y), entry(kind, "to_down", y)) for kind in ("smooth", "slope")
            ]
            for f in range(6):
                a, b = pairs[f // 5]
                ups[f] = a * values[f] if y == 0 else ups[f] + a * values[f]
                downs[f] = b * values[f] if y == 0 else downs[f] + b * values[f]
        for f in range(6):
            vb[f * tiles + t] = ups[f]
            vb[(6 + f) * tiles + t] = downs[f]

    lines_a.cross()
    block_loop(4, 16, slope_block(span_out, gy))
    lines_a.give()
    lines_b.start()

    span_copy.wait()
    span_loop(5, span_out, span_in, store_gz)

    rim_wait(*rim_a)
    for side, row in ((0, 0), (1, rows - 1)):
        weight = entry("slope", "rim", 3 * side)
        values = primitives(*(rim_in[side, 0, f] for f in range(5)))
        for f in range(4):
            edge_out[side, f] = values[f]
            gy[f, row] += weight * values[f]
    edge_copy.start()

    lines_a.finish()
    rim_send(*rim_b)

    def stress_of(grad, d):
        row = [VISCOSITY * (grad[d][c] + grad[c][d]) for c in range(3)]
        spread_out = (2.0 / 3.0 * VISCOSITY) * (grad[0][0] + grad[1][1] + grad[2][2])
        row[d] = (2.0 * VISCOSITY) * grad[d][d] - spread_out
        return row

    def flux_of(d, u, m, e, push, grad):
        stress = stress_of(grad, d)
        energy = (e + push) * u[d] - CONDUCT * grad[d][3]
        values = []
        for c in range(3):
            energy = energy - u[c] * stress[c]
            value = m[c] * u[d] - stress[c]
            values.append(value + push if c == d else value)
        return values + [energy]

    def cell(y, z):
        u = [span_out[f, y, z] for f in range(4)]
        return u, [mom[c, y, z] for c in range(3)], ene[y, z], rho[y, z] * u[3]

    @pl.loop(0, tiles)
    def _(t):
        z = pl.ds(pl.multiple_of(t * 8, 8), 8)
        ups, downs = [None] * 4, [None] * 4
        from_up = [sa[f * tiles + t] for f in range(4)]
        from_down = [sa[(4 + f) * tiles + t] for f in range(4)]
        for y in range(rows):
            a, b = entry("slope", "up", y), entry("slope", "down", y)
            wall = [gy[f, y, z] + a * from_up[f] + b * from_down[f] for f in range(4)]
            for f in range(4):
                gy[f, y, z] = wall[f]
            grad = ([gx[f, y, z] for f in range(3)], wall, [gz[f, y, z] for f in range(3)])
            values = flux_of(1, *cell(y, z), grad)
            a, b = entry("slope", "to_up", y), entry("slope", "to_down", y)
            for f in range(4):
                fy[f, y, z] = values[f]
                ups[f] = a * values[f] if y == 0 else ups[f] + a * values[f]
                downs[f] = b * values[f] if y == 0 else downs[f] + b * values[f]
        for f in range(4):
            vc[f * tiles + t] = ups[f]
            vc[(4 + f) * tiles + t] = downs[f]

    lines_c.start()

    @pl.loop(0, tiles)
    def _(t):
        z = pl.ds(pl.multiple_of(t * 8, 8), 8)
        for y in range(rows):
            grad = [[ref[f, y, z] for f in range(4)] for ref in (gx, gy, gz)]
            state = cell(y, z)
            for d, out in ((2, fspan_out), (0, fx)):
                values = flux_of(d, *state, grad)
                for f in range(4):
                    out[f, y, z] = values[f]

    fspan_copy.start()
    lines_b.gather()
    lines_c.gather()

    def store_fx(f, y, value):
        gx[f, y] = value

    stream_loop(4, lambda f, y: fx[f, y], store_fx)
    lines_c.cross()
    lines_b.cross()
    block_loop(4, 16, slope_block(fy, gf))
    lines_c.give()
    lines_b.give()

    def store_mass(f, y, value):
        rate[0, y] = value

    stream_loop(1, lambda f, y: mom[0, y], store_mass)

    def mass_block(f, z):
        def store(y, total):
            rate[0, y, z] = -(rate[0, y, z] + total + gz[4, y, z])

        local_rows("slope", lambda y: mom[1, y, z], store, z)

    block_loop(1, 16, mass_block)

    def smooth_block(read, write):
        def body(f, z):
            def store(y, total):
                write[y, z] = total

            local_rows("smooth", lambda y: read[y, z], store, z)

        return body

    block_loop(1, 16, smooth_block(rho, smooth.at[0]))

    def smooth_mom(f, z):
        def store(y, total):
            smooth[1 + f, y, z] = total

        local_rows("smooth", lambda y: mom[f, y, z], store, z)

    block_loop(3, 16, smooth_mom)
    block_loop(1, 16, smooth_block(ene, smooth.at[4]))
    rim_wait(*rim_b)
    for side, edge, inner in ((0, 0, 1), (1, rows - 1, rows - 2)):
        near, far, second = (entry("smooth", "rim", 3 * side + k) for k in range(3))
        for f in range(5):
            smooth[f, edge] += near * rim_in[side, 0, f] + far * rim_in[side, 1, f]
            smooth[f, inner] += second * rim_in[side, 0, f]
        rate[0, edge] -= entry("slope", "rim", 3 * side) * rim_in[side, 0, 2]

    lines_b.finish()

    @pl.loop(0, tiles)
    def _(t):
        z = pl.ds(pl.multiple_of(t * 8, 8), 8)
        from_up = [sb[f * tiles + t] for f in range(6)]
        from_down = [sb[(6 + f) * tiles + t] for f in range(6)]
        for y in range(rows):
            a, b = entry("smooth", "up", y), entry("smooth", "down", y)
            for f in range(5):
                smooth[f, y, z] += a * from_up[f] + b * from_down[f]
            a, b = entry("slope", "up", y), entry("slope", "down", y)
            rate[0, y, z] -= a * from_up[5] + b * from_down[5]

    smooth_flush = pltpu.make_async_copy(smooth, smooth_hbm, s_load.at[4])
    smooth_flush.start()

    edge_copy.wait()

    @pl.loop(0, 2)
    def _(side):
        product = stream_rows(jnp.concatenate([edge_out[side, f] for f in range(4)], axis=0))
        for f in range(4):
            edge_x[side, f] = product[f * span : (f + 1) * span]
        for f in (0, 2):
            pair = span_pair(
                (edge_out[side, f], edge_out[side, f + 1]), (edge_in[side, f], edge_in[side, f + 1])
            )
            edge_z[side, f] = pair[0]
            edge_z[side, f + 1] = pair[1]

    @pl.loop(0, tiles)
    def _(t):
        z = pl.ds(pl.multiple_of(t * 8, 8), 8)
        for side, row, step in ((0, 0, 1), (1, rows - 1, -1)):
            weights = [entry("slope", "next", 6 * side + k) for k in range(6)]
            u = [edge_out[side, f, z] for f in range(4)]
            past = primitives(*(rim_in[side, 1, f, z] for f in range(5)))
            wall = [
                weights[0] * u[f] + weights[1] * span_out[f, row + step, z]
                + weights[2] * past[f] + weights[3] * span_out[f, row + 2 * step, z]
                + weights[4] * gy[f, row, z] + weights[5] * gy[f, row + step, z]
                for f in range(4)
            ]
            grad = (
                [edge_x[side, f, z] for f in range(3)], wall, [edge_z[side, f, z] for f in range(3)]
            )
            m = [rim_in[side, 0, 1 + c, z] for c in range(3)]
            values = flux_of(1, u, m, rim_in[side, 0, 4, z], rim_in[side, 0, 0, z] * u[3], grad)
            weight = entry("slope", "rim", 3 * side)
            for f in range(4):
                gf[f, row, z] += weight * values[f]

    fspan_copy.wait()
    span_loop(4, fspan_out, fspan_in, store_gz)

    lines_c.finish()

    @pl.loop(0, tiles)
    def _(t):
        z = pl.ds(pl.multiple_of(t * 8, 8), 8)
        from_up = [sc[f * tiles + t] for f in range(4)]
        from_down = [sc[(4 + f) * tiles + t] for f in range(4)]
        for y in range(rows):
            a, b = entry("slope", "up", y), entry("slope", "down", y)
            keep = tab[base + places["keep"] + y]
            for f in range(4):
                total = gx[f, y, z] + gz[f, y, z] + gf[f, y, z] + a * from_up[f] + b * from_down[f]
                rate[1 + f, y, z] = -(total * keep) if f < 3 else -total

    rate_flush = pltpu.make_async_copy(rate, rate_hbm, s_load.at[5])
    rate_flush.start()
    rate_flush.wait()
    smooth_flush.wait()


def results_body(rate_from, smooth_from, rate_to, smooth_to, sems):
    copies = [
        pltpu.make_async_copy(source.at[f], target.at[f], sems.at[at, f])
        for at, (source, target) in enumerate(((rate_from, rate_to), (smooth_from, smooth_to)))
        for f in range(5)
    ]
    for copy in copies:
        copy.start()
    for copy in copies:
        copy.wait()


def per_device(mass_per_volume, mass_flux_vector, total_heat_content):
    rows, span, stream = mass_per_volume.shape
    count = lax.axis_size("gy")
    tiles = span // 8
    table, gains = device_table(rows * count, rows)
    each_a = -(-8 * tiles // count)
    each_b = -(-12 * tiles // count)
    pieces = [table]
    for kinds, each in ((["slope"] * 4, each_a), (["smooth"] * 5 + ["slope"], each_b)):
        pieces += gain_tables(kinds, gains, count, tiles, each)
    starts = tuple(int(at) for at in np.cumsum([piece.size for piece in pieces[:-1]]))
    field = (rows, span, stream)
    mats = np.concatenate([stream_table(stream), span_table(2 * span)])
    outer, inner = scan_groups(count)

    def vmem(*shape):
        return pltpu.VMEM(shape, jnp.float32)

    lines_a = [vmem(count * each_a, 8, stream)] * 4
    lines_b = [vmem(count * each_b, 8, stream)] * 4
    totals_a = [vmem(outer * each_a, 8, stream)] * 4
    totals_b = [vmem(outer * each_b, 8, stream)] * 4
    scalar = pl.BlockSpec(memory_space=pltpu.SMEM)
    outside = pl.BlockSpec(memory_space=pl.ANY)
    dma = pltpu.SemaphoreType.DMA
    out = jax.ShapeDtypeStruct((5,) + field, jnp.float32)
    results = pl.pallas_call(
        functools.partial(fused_body, count, starts),
        out_shape=(out, out),
        in_specs=[outside] * 3 + [scalar, outside],
        out_specs=(outside, outside),
        scratch_shapes=[
            vmem(5, *field), vmem(5, *field),
            vmem(*field), vmem(3, *field), vmem(*field), pltpu.VMEM(mats.shape, jnp.bfloat16),
            vmem(5, *field), vmem(5, *field), vmem(4, *field), vmem(4, *field), vmem(5, *field),
            *[vmem(4, *field)] * 5,
            vmem(2, 2, 5, span, stream), vmem(2, 2, 5, span, stream),
            *[vmem(2, 4, span, stream)] * 4,
            *lines_a, *lines_b, *lines_a,
            *totals_a, *totals_b, *totals_a,
            dma((6,)), dma((3,)), dma((3,)), dma((2, 2)), dma((2, 2)),
            dma((12, max(inner, outer))), dma((12, max(inner, outer))),
        ],
        compiler_params=pltpu.CompilerParams(
            collective_id=0, has_side_effects=True, vmem_limit_bytes=56 * 1024 * 1024
        ),
    )(
        mass_per_volume, mass_flux_vector, total_heat_content,
        jnp.asarray(np.concatenate(pieces)), jnp.asarray(mats),
    )
    return pl.pallas_call(
        results_body,
        out_shape=(out, out),
        in_specs=[outside] * 2,
        out_specs=(outside, outside),
        scratch_shapes=[dma((2, 5))],
    )(*results)


def solution(mesh):
    placed = (P("gy", "pa", None), P(None, "gy", "pa", None), P("gy", "pa", None))
    return jax.shard_map(
        per_device,
        mesh=mesh,
        in_specs=placed,
        out_specs=(P(None, "gy", "pa", None), P(None, "gy", "pa", None)),
        check_vma=False,
    )
```

```python
import functools

import jax
import jax.numpy as jnp
import ml_dtypes
import numpy as np
from jax import lax
from jax.experimental import pallas as pl
from jax.experimental.pallas import tpu as pltpu
from jax.sharding import PartitionSpec as P

GAMMA_GAS = 1.4
PRANDTL = 0.72
VISCOSITY = 0.25
ALPHA_FILTER = 0.499
ALPHA_SLOPE = 0.498
STRETCH = 1.2
STREAM_STEP = 1.0
SPAN_STEP = 0.5
CONDUCT = VISCOSITY * GAMMA_GAS / ((GAMMA_GAS - 1.0) * PRANDTL)
MESH = pl.DeviceIdType.MESH


def slope_weights():
    near_weight = (2.0 + ALPHA_SLOPE) / 3.0
    far_weight = (4.0 * ALPHA_SLOPE - 1.0) / 12.0
    return (near_weight, far_weight)


def system_rows(system_kind, points):
    lower = np.zeros(points)
    middle = np.ones(points)
    upper = np.zeros(points)
    weights = np.zeros((7, points))
    if system_kind == "slope":
        near_weight, far_weight = slope_weights()
        lower[:] = ALPHA_SLOPE
        upper[:] = ALPHA_SLOPE
        weights[1] = -far_weight
        weights[2] = -near_weight
        weights[4] = near_weight
        weights[5] = far_weight
        for edge_row in (1, points - 2):
            lower[edge_row] = 0.25
            upper[edge_row] = 0.25
            weights[:, edge_row] = 0.0
            weights[2, edge_row] = -0.75
            weights[4, edge_row] = 0.75
        lower[0] = 0.0
        upper[0] = 2.0
        weights[:, 0] = 0.0
        weights[3, 0] = -2.5
        weights[4, 0] = 2.0
        weights[5, 0] = 0.5
        lower[points - 1] = 2.0
        upper[points - 1] = 0.0
        weights[:, points - 1] = 0.0
        weights[3, points - 1] = 2.5
        weights[2, points - 1] = -2.0
        weights[1, points - 1] = -0.5
    else:
        strength = ALPHA_FILTER
        lower[:] = strength
        upper[:] = strength
        weights[3] = 11.0 / 16.0 + 5.0 * strength / 8.0
        weights[2] = 15.0 / 64.0 + 17.0 * strength / 32.0
        weights[4] = weights[2]
        weights[1] = -3.0 / 32.0 + 3.0 * strength / 16.0
        weights[5] = weights[1]
        weights[0] = 1.0 / 64.0 - strength / 32.0
        weights[6] = weights[0]
        for edge_row in (2, points - 3):
            weights[:, edge_row] = 0.0
            weights[3, edge_row] = 5.0 / 8.0 + 3.0 * strength / 4.0
            weights[2, edge_row] = 0.25 + strength / 2.0
            weights[4, edge_row] = 0.25 + strength / 2.0
            weights[1, edge_row] = -1.0 / 16.0 + strength / 8.0
            weights[5, edge_row] = -1.0 / 16.0 + strength / 8.0
        for edge_row in (1, points - 2):
            weights[:, edge_row] = 0.0
            weights[3, edge_row] = 0.5 + strength
            weights[2, edge_row] = 0.25 + strength / 2.0
            weights[4, edge_row] = 0.25 + strength / 2.0
        for edge_row in (0, points - 1):
            lower[edge_row] = 0.0
            upper[edge_row] = 0.0
            weights[:, edge_row] = 0.0
            weights[3, edge_row] = 1.0
    return (lower, middle, upper, weights)


def inverse_metric(points):
    places = 2.0 * np.arange(points) / (points - 1) - 1.0
    growth = np.exp(STRETCH * places)
    cosh_values = 0.5 * (growth + 1.0 / growth)
    edge_growth = np.exp(STRETCH)
    tanh_value = (edge_growth - 1.0 / edge_growth) / (edge_growth + 1.0 / edge_growth)
    return tanh_value * cosh_values**2 / (0.64 * STRETCH)


def periodic_matrix(points, spacing):
    near_weight, far_weight = slope_weights()
    wave_numbers = np.arange(1, points // 2)
    angles = 2.0 * np.pi * wave_numbers / points
    modified = (2.0 * near_weight * np.sin(angles) + 2.0 * far_weight * np.sin(2.0 * angles)) / (
        1.0 + 2.0 * ALPHA_SLOPE * np.cos(angles)
    )
    phases = np.arange(points)[:, None] * wave_numbers[None, :] % points
    circulant = -2.0 / (points * spacing) * (np.sin(2.0 * np.pi * phases / points) @ modified)
    shifts = (np.arange(points)[:, None] - np.arange(points)[None, :]) % points
    return circulant[shifts].T


def wall_tables(system_kind, points, rows):
    lower, middle, upper, weights = system_rows(system_kind, points)
    system = np.diag(middle) + np.diag(lower[1:], -1) + np.diag(upper[:-1], 1)
    source = np.zeros((points, points))
    for offset in range(-3, 4):
        for row in range(max(0, -offset), min(points, points - offset)):
            source[row, row + offset] = weights[3 + offset, row]
    band = np.zeros((points, points))
    if system_kind == "slope":
        ratio = slope_weights()[1] / ALPHA_SLOPE
        for row in range(2, points - 2):
            band[row, row + 1] = ratio
            band[row, row - 1] = -ratio
    else:
        mid = points // 2
        strength = ALPHA_FILTER
        two = weights[0, mid] / strength
        one = (weights[1, mid] - two) / strength
        zero = (weights[2, mid] - strength * two - one) / strength
        for row in range(3, points - 3):
            for offset, value in ((0, zero), (1, one), (2, two)):
                band[row, row + offset] = value
                band[row, row - offset] = value
    rest = np.linalg.solve(system, source - system @ band)
    down_ratio = np.zeros(points)
    carried = 0.0
    for row in range(points):
        down_ratio[row] = upper[row] / (middle[row] - lower[row] * carried)
        carried = down_ratio[row]
    up_ratio = np.zeros(points)
    carried = 0.0
    for row in range(points - 1, -1, -1):
        up_ratio[row] = lower[row] / (middle[row] - upper[row] * carried)
        carried = up_ratio[row]
    scale = inverse_metric(points) if system_kind == "slope" else np.ones(points)
    blocks = points // rows
    local = np.zeros((blocks, rows, rows))
    up = np.zeros((blocks, rows))
    down = np.zeros((blocks, rows))
    to_up = np.zeros((blocks, rows))
    to_down = np.zeros((blocks, rows))
    up_gain = np.zeros(blocks)
    down_gain = np.zeros(blocks)
    rim = np.zeros((blocks, 6))
    next_row = np.zeros((blocks, 12))
    near, far = slope_weights()
    for block in range(blocks):
        first, last = block * rows, block * rows + rows - 1
        window = slice(first, last + 1)
        local[block] = (rest + band)[window, window] * scale[window, None]
        up[block] = np.cumprod(np.concatenate([[1.0], -up_ratio[first + 1 : last + 1]]))
        up[block] *= scale[window]
        down[block] = np.cumprod(np.concatenate([[1.0], -down_ratio[first:last][::-1]]))[::-1]
        down[block] *= scale[window]
        if block < blocks - 1:
            to_up[block] = rest[last + 1, window]
            up_gain[block] = np.prod(-up_ratio[first + 1 : last + 2])
            rim[block, 3] = band[last, last + 1] * scale[last]
            rim[block, 4] = band[last, last + 2] * scale[last]
            rim[block, 5] = band[last - 1, last + 1] * scale[last - 1]
            unit = scale[last + 1] / ALPHA_SLOPE
            next_row[block, 6:] = unit * np.array(
                [near, -near, far, -far, -1.0 / scale[last], -ALPHA_SLOPE / scale[last - 1]]
            )
        if block > 0:
            to_down[block] = rest[first - 1, window]
            down_gain[block] = np.prod(-down_ratio[first - 1 : last])
            rim[block, 0] = band[first, first - 1] * scale[first]
            rim[block, 1] = band[first, first - 2] * scale[first]
            rim[block, 2] = band[first + 1, first - 1] * scale[first + 1]
            unit = scale[first - 1] / ALPHA_SLOPE
            next_row[block, :6] = unit * np.array(
                [-near, near, -far, far, -1.0 / scale[first], -ALPHA_SLOPE / scale[first + 1]]
            )
    return local, up, down, to_up, to_down, up_gain, down_gain, rim, next_row


def table_layout(rows):
    sizes = (("local", rows * rows), ("up", rows), ("down", rows), ("to_up", rows), ("to_down", rows), ("rim", 6), ("next", 12))
    places, at = {}, 0
    for kind in ("slope", "smooth"):
        for name, size in sizes:
            places[kind, name] = at
            at += size
    places["keep"] = at
    return places, at + rows


def device_table(points, rows):
    places, width = table_layout(rows)
    blocks = points // rows
    table = np.zeros((blocks, width), np.float32)
    gains = {}
    for kind in ("slope", "smooth"):
        local, up, down, to_up, to_down, up_gain, down_gain, rim, beyond = wall_tables(kind, points, rows)
        gains[kind] = (up_gain, down_gain)
        named = dict(local=local, up=up, down=down, to_up=to_up, to_down=to_down, rim=rim, next=beyond)
        for name, value in named.items():
            flat = value.reshape(blocks, -1)
            at = places[kind, name]
            table[:, at : at + flat.shape[1]] = flat
    table[:, places["keep"] :] = 1.0
    table[0, places["keep"]] = 0.0
    table[-1, -1] = 0.0
    return table.reshape(-1), gains


def scan_groups(count):
    outer = 4 if count % 4 == 0 else 1
    return outer, count // outer


def gain_tables(kinds, gains, count, tiles, each):
    outer, inner = scan_groups(count)
    fields = len(kinds)
    wide = outer * each
    near = np.zeros((count, inner, wide), np.float32)
    far = np.zeros((count, outer, each), np.float32)

    def chain(tile):
        quantity = min(tile // tiles, 2 * fields - 1)
        back = quantity // fields
        return gains[kinds[quantity % fields]][back].reshape(outer, inner), back

    for group in range(outer):
        for place in range(inner):
            owner = group * inner + place
            for slot in range(wide):
                values, back = chain(place * wide + slot)
                near[owner, :, slot] = values[group][::-1] if back else values[group]
            for slot in range(each):
                values, back = chain((place * outer + group) * each + slot)
                product = values.prod(axis=1)
                far[owner, :, slot] = product[::-1] if back else product
    return near.reshape(-1), far.reshape(-1)


def split_pair(matrix):
    high = matrix.astype(np.float32).astype(ml_dtypes.bfloat16)
    low = (matrix - high.astype(np.float64)).astype(np.float32).astype(ml_dtypes.bfloat16)
    return high, low


def stream_table(points):
    high, low = split_pair(periodic_matrix(points, STREAM_STEP))
    return np.block([[high, low], [high, np.zeros_like(low)]])


def span_table(points):
    own = points // 2
    rows = periodic_matrix(points, SPAN_STEP).T[:own]
    high, low = split_pair(rows)
    return np.block([[high, high], [low, np.zeros_like(low)]])


def halves(value):
    high = value.astype(jnp.bfloat16)
    return high, (value - high.astype(jnp.float32)).astype(jnp.bfloat16)


def fused_body(
    count, starts, rho_hbm, mom_hbm, ene_hbm, tab, mats_hbm,
    rate_hbm, smooth_hbm,
    rate, smooth, rho, mom, ene, mats,
    span_out, span_in, gx, gy, gz, fx, fy, gf, fspan_out, fspan_in,
    rim_out, rim_in, edge_out, edge_in, edge_x, edge_z,
    va, ra, oa, sa, vb, rb, ob, sb, vc, rc, oc, sc,
    ta, rta, ota, sta, tb, rtb, otb, stb, tc, rtc, otc, stc,
    s_load, s_span, r_span, s_rim, r_rim, s_line, r_line,
):
    rows, span, _ = rho.shape
    tiles = span // 8
    me, core = lax.axis_index("gy"), lax.axis_index("pa")
    outer, inner = scan_groups(count)
    group, place = me // inner, lax.rem(me, inner)
    places, width = table_layout(rows)
    base = me * width

    def entry(kind, name, at):
        return tab[base + places[kind, name] + at]

    def remote(src, dst, send, recv, target, target_core):
        return pltpu.make_async_remote_copy(
            src_ref=src, dst_ref=dst, send_sem=send, recv_sem=recv,
            device_id=(target, target_core), device_id_type=MESH,
        )

    loads = [
        pltpu.make_async_copy(source, target, s_load.at[at])
        for at, (source, target) in enumerate(
            ((rho_hbm, rho), (mom_hbm, mom), (ene_hbm, ene), (mats_hbm, mats))
        )
    ]
    for load in loads:
        load.start()

    barrier = pltpu.get_barrier_semaphore()

    @pl.loop(1, count)
    def _(step):
        pl.semaphore_signal(
            barrier, inc=1, device_id=(lax.rem(me + step, count), core), device_id_type=MESH
        )

    pl.semaphore_signal(barrier, inc=1, device_id=(me, 1 - core), device_id_type=MESH)

    for load in loads:
        load.wait()

    for depth in range(2):
        for side, row in ((0, rows - 1 - depth), (1, depth)):
            rim_out[side, depth, 0] = rho[row]
            for c in range(3):
                rim_out[side, depth, 1 + c] = mom[c, row]
            rim_out[side, depth, 4] = ene[row]

    @pl.when(me == 0)
    def _():
        rim_in[0] = jnp.ones(rim_in.shape[1:], jnp.float32)

    @pl.when(me == count - 1)
    def _():
        rim_in[1] = jnp.ones(rim_in.shape[1:], jnp.float32)

    def primitives(d, m0, m1, m2, e):
        inv = 1.0 / d
        u, v, w = m0 * inv, m1 * inv, m2 * inv
        push = (GAMMA_GAS - 1.0) * (e - 0.5 * (u * m0 + v * m1 + w * m2))
        return u, v, w, push * inv

    @pl.loop(0, tiles)
    def _(t):
        z = pl.ds(pl.multiple_of(t * 8, 8), 8)
        ups, downs = [None] * 4, [None] * 4
        for y in range(rows):
            m2 = mom[2, y, z]
            values = primitives(rho[y, z], mom[0, y, z], mom[1, y, z], m2, ene[y, z])
            a, b = entry("slope", "to_up", y), entry("slope", "to_down", y)
            for f in range(4):
                span_out[f, y, z] = values[f]
                ups[f] = a * values[f] if y == 0 else ups[f] + a * values[f]
                downs[f] = b * values[f] if y == 0 else downs[f] + b * values[f]
            span_out[4, y, z] = m2
        for f in range(4):
            va[f * tiles + t] = ups[f]
            va[(4 + f) * tiles + t] = downs[f]

    pl.semaphore_wait(barrier, count)

    def rim_send(source, into, slot):
        def make(side, target):
            return remote(source(side), into(side), s_rim.at[slot, side], r_rim.at[slot, side], target, core)

        @pl.when(me < count - 1)
        def _():
            make(0, me + 1).start()

        @pl.when(me > 0)
        def _():
            make(1, me - 1).start()

    def rim_wait(source, into, slot):
        def make(side, target):
            return remote(source(side), into(side), s_rim.at[slot, side], r_rim.at[slot, side], target, core)

        @pl.when(me < count - 1)
        def _():
            make(0, me + 1).wait_send()
            make(1, me + 1).wait_recv()

        @pl.when(me > 0)
        def _():
            make(1, me - 1).wait_send()
            make(0, me - 1).wait_recv()

    def in_group(at):
        return group * inner + at

    def across(at):
        return at * inner + place

    def spread(src, dst, line, size, mine, device):
        each = src.shape[0] // size
        own = pl.ds(mine * each, each)

        @pl.loop(1, size)
        def _(step):
            to = lax.rem(mine + step, size)
            remote(
                src.at[pl.ds(to * each, each)], dst.at[own],
                s_line.at[line, step], r_line.at[line, step], device(to), core,
            ).start()

        dst[own] = src[own]

    def spread_wait(src, dst, line, size, mine, device):
        each = src.shape[0] // size

        @pl.loop(1, size)
        def _(step):
            to = lax.rem(mine + step, size)
            fro = lax.rem(mine + size - step, size)
            remote(
                src.at[pl.ds(to * each, each)], dst.at[pl.ds(mine * each, each)],
                s_line.at[line, step], r_line.at[line, step], device(to), core,
            ).wait_send()
            remote(
                src.at[pl.ds(to * each, each)], dst.at[pl.ds(fro * each, each)],
                s_line.at[line, step], r_line.at[line, step], device(to), core,
            ).wait_recv()

    def scan(src, first, gain_at, turned, size, emit):
        each = src.shape[0] // size

        def lap(i, carry):
            j = i + turned * (size - 1 - 2 * i)
            emit(j, carry)
            return tuple(
                tab[gain_at + i * each + k] * carry[k] + src[j * each + k] for k in range(each)
            )

        return lax.fori_loop(0, size, lap, first)

    def sender(out, back, line, size, mine, device):
        each = out.shape[0] // size

        def emit(j, carry):
            at = pl.ds(j * each, each)
            for k in range(each):
                out[j * each + k] = carry[k]

            @pl.when(j != mine)
            def _():
                step = lax.rem(j - mine + size, size)
                remote(
                    out.at[at], back.at[pl.ds(mine * each, each)],
                    s_line.at[line, step], r_line.at[line, step], device(j), core,
                ).start()

            @pl.when(j == mine)
            def _():
                back[at] = out[at]

        return emit

    class Lines:
        def __init__(self, at, fields, near, far, values, got, out, back, total, tgot, tout, tback):
            self.values, self.got, self.out, self.back = values, got, out, back
            self.total, self.tgot, self.tout, self.tback = total, tgot, tout, tback
            self.line = 4 * at
            self.each = values.shape[0] // count
            wide = outer * self.each
            self.wide = wide
            self.turned = jnp.minimum((place * wide) // (fields * tiles), 1)
            self.near = near + me * (inner * wide)
            self.far = far + me * (outer * self.each)
            ring, column = (inner, place, in_group), (outer, group, across)
            self.hops = (
                (values, got, self.line, *ring),
                (total, tgot, self.line + 1, *column),
                (tout, tback, self.line + 2, *column),
                (out, back, self.line + 3, *ring),
            )

        def start(self):
            spread(*self.hops[0])

        def wait(self, hop):
            spread_wait(*self.hops[hop])

        def gather(self):
            self.wait(0)
            zeros = tuple(jnp.zeros((8, 128), jnp.float32) for _ in range(self.wide))
            total = scan(self.got, zeros, self.near, self.turned, inner, lambda j, carry: None)
            for k in range(self.wide):
                self.total[k] = total[k]
            spread(*self.hops[1])

        def cross(self):
            self.wait(1)
            zeros = tuple(jnp.zeros((8, 128), jnp.float32) for _ in range(self.each))
            scan(self.tgot, zeros, self.far, self.turned, outer, sender(*self.hops[2]))

        def give(self):
            self.wait(2)
            first = tuple(self.tback[k] for k in range(self.wide))
            scan(self.got, first, self.near, self.turned, inner, sender(*self.hops[3]))

        def finish(self):
            self.wait(3)

    near_a, far_a, near_b, far_b = starts
    lines_a = Lines(0, 4, near_a, far_a, va, ra, oa, sa, ta, rta, ota, sta)
    lines_b = Lines(1, 6, near_b, far_b, vb, rb, ob, sb, tb, rtb, otb, stb)
    lines_c = Lines(2, 4, near_a, far_a, vc, rc, oc, sc, tc, rtc, otc, stc)

    rim_a = (lambda side: rim_out.at[side, 0], lambda side: rim_in.at[side, 0], 0)
    rim_b = (lambda side: rim_out.at[side, 1], lambda side: rim_in.at[side, 1], 1)
    span_copy = remote(span_out, span_in, s_span.at[0], r_span.at[0], me, 1 - core)
    fspan_copy = remote(fspan_out, fspan_in, s_span.at[1], r_span.at[1], me, 1 - core)
    edge_copy = remote(edge_out, edge_in, s_span.at[2], r_span.at[2], me, 1 - core)

    lines_a.start()
    rim_send(*rim_a)
    span_copy.start()

    def local_rows(kind, load, store, z):
        values = [load(y) for y in range(rows)]
        for y in range(rows):
            total = entry(kind, "local", y * rows) * values[0]
            for k in range(1, rows):
                total = total + entry(kind, "local", y * rows + k) * values[k]
            store(y, total)

    def block_loop(fields, size, body):
        per = span // size

        @pl.loop(0, fields * per)
        def _(i):
            body(i // per, pl.ds(pl.multiple_of((i % per) * size, size), size))

    def slope_block(src, dst):
        def body(f, z):
            def store(y, total):
                dst[f, y, z] = total

            local_rows("slope", lambda y: src[f, y, z], store, z)

        return body

    def stream_rows(value):
        high, low = halves(value)
        product = jnp.dot(
            jnp.concatenate([high, low], axis=1), mats[pl.ds(0, 256)], preferred_element_type=jnp.float32
        )
        return product[:, :128] + product[:, 128:]

    def stream_loop(fields, load, store):
        @pl.loop(0, fields * rows // 4)
        def _(i):
            f, y = i // (rows // 4), (i % (rows // 4)) * 4
            block = jnp.concatenate([load(f, y + k) for k in range(4)], axis=0)
            product = stream_rows(block)
            for k in range(4):
                store(f, y + k, product[k * span : (k + 1) * span])

    def span_pair(own, other):
        parts = [halves(jnp.concatenate(pair, axis=1)) for pair in (own, other)]
        stacked = jnp.concatenate([parts[0][0], parts[1][0], parts[0][1], parts[1][1]], axis=0)
        product = jnp.dot(mats[pl.ds(256, 128)], stacked, preferred_element_type=jnp.float32)
        product = product[:span] + product[span:]
        return product[:, :128], product[:, 128:]

    def span_loop(fields, own, other, store):
        @pl.loop(0, fields * rows // 2)
        def _(i):
            f, y = i // (rows // 2), (i % (rows // 2)) * 2
            pair = span_pair((own[f, y], own[f, y + 1]), (other[f, y], other[f, y + 1]))
            store(f, y, pair[0])
            store(f, y + 1, pair[1])

    def store_gx(f, y, value):
        gx[f, y] = value

    def store_gz(f, y, value):
        gz[f, y] = value

    stream_loop(4, lambda f, y: span_out[f, y], store_gx)
    lines_a.gather()

    @pl.loop(0, tiles)
    def _(t):
        z = pl.ds(pl.multiple_of(t * 8, 8), 8)
        ups, downs = [None] * 6, [None] * 6
        for y in range(rows):
            middle = mom[1, y, z]
            values = (rho[y, z], mom[0, y, z], middle, mom[2, y, z], ene[y, z], middle)
            pairs = [
                (entry(kind, "to_up", y), entry(kind, "to_down", y)) for kind in ("smooth", "slope")
            ]
            for f in range(6):
                a, b = pairs[f // 5]
                ups[f] = a * values[f] if y == 0 else ups[f] + a * values[f]
                downs[f] = b * values[f] if y == 0 else downs[f] + b * values[f]
        for f in range(6):
            vb[f * tiles + t] = ups[f]
            vb[(6 + f) * tiles + t] = downs[f]

    lines_b.start()
    lines_a.cross()
    block_loop(4, 16, slope_block(span_out, gy))
    lines_a.give()

    span_copy.wait()
    span_loop(5, span_out, span_in, store_gz)

    rim_wait(*rim_a)
    for side, row in ((0, 0), (1, rows - 1)):
        weight = entry("slope", "rim", 3 * side)
        values = primitives(*(rim_in[side, 0, f] for f in range(5)))
        for f in range(4):
            edge_out[side, f] = values[f]
            gy[f, row] += weight * values[f]
    edge_copy.start()

    lines_b.gather()
    lines_a.finish()
    rim_send(*rim_b)

    def stress_of(grad, d):
        row = [VISCOSITY * (grad[d][c] + grad[c][d]) for c in range(3)]
        spread_out = (2.0 / 3.0 * VISCOSITY) * (grad[0][0] + grad[1][1] + grad[2][2])
        row[d] = (2.0 * VISCOSITY) * grad[d][d] - spread_out
        return row

    def flux_of(d, u, m, e, push, grad):
        stress = stress_of(grad, d)
        energy = (e + push) * u[d] - CONDUCT * grad[d][3]
        values = []
        for c in range(3):
            energy = energy - u[c] * stress[c]
            value = m[c] * u[d] - stress[c]
            values.append(value + push if c == d else value)
        return values + [energy]

    def cell(y, z):
        u = [span_out[f, y, z] for f in range(4)]
        return u, [mom[c, y, z] for c in range(3)], ene[y, z], rho[y, z] * u[3]

    @pl.loop(0, tiles)
    def _(t):
        z = pl.ds(pl.multiple_of(t * 8, 8), 8)
        ups, downs = [None] * 4, [None] * 4
        from_up = [sa[f * tiles + t] for f in range(4)]
        from_down = [sa[(4 + f) * tiles + t] for f in range(4)]
        for y in range(rows):
            a, b = entry("slope", "up", y), entry("slope", "down", y)
            wall = [gy[f, y, z] + a * from_up[f] + b * from_down[f] for f in range(4)]
            for f in range(4):
                gy[f, y, z] = wall[f]
            grad = ([gx[f, y, z] for f in range(3)], wall, [gz[f, y, z] for f in range(3)])
            values = flux_of(1, *cell(y, z), grad)
            a, b = entry("slope", "to_up", y), entry("slope", "to_down", y)
            for f in range(4):
                fy[f, y, z] = values[f]
                ups[f] = a * values[f] if y == 0 else ups[f] + a * values[f]
                downs[f] = b * values[f] if y == 0 else downs[f] + b * values[f]
        for f in range(4):
            vc[f * tiles + t] = ups[f]
            vc[(4 + f) * tiles + t] = downs[f]

    lines_c.start()

    @pl.loop(0, tiles)
    def _(t):
        z = pl.ds(pl.multiple_of(t * 8, 8), 8)
        for y in range(rows):
            grad = [[ref[f, y, z] for f in range(4)] for ref in (gx, gy, gz)]
            state = cell(y, z)
            for d, out in ((2, fspan_out), (0, fx)):
                values = flux_of(d, *state, grad)
                for f in range(4):
                    out[f, y, z] = values[f]

    fspan_copy.start()
    lines_b.cross()

    def store_fx(f, y, value):
        gx[f, y] = value

    stream_loop(4, lambda f, y: fx[f, y], store_fx)
    lines_c.gather()
    lines_b.give()
    block_loop(4, 16, slope_block(fy, gf))
    lines_c.cross()

    def store_mass(f, y, value):
        rate[0, y] = value

    stream_loop(1, lambda f, y: mom[0, y], store_mass)

    def mass_block(f, z):
        def store(y, total):
            rate[0, y, z] = -(rate[0, y, z] + total + gz[4, y, z])

        local_rows("slope", lambda y: mom[1, y, z], store, z)

    block_loop(1, 16, mass_block)

    def smooth_block(read, write):
        def body(f, z):
            def store(y, total):
                write[y, z] = total

            local_rows("smooth", lambda y: read[y, z], store, z)

        return body

    block_loop(1, 16, smooth_block(rho, smooth.at[0]))

    def smooth_mom(f, z):
        def store(y, total):
            smooth[1 + f, y, z] = total

        local_rows("smooth", lambda y: mom[f, y, z], store, z)

    block_loop(3, 16, smooth_mom)
    block_loop(1, 16, smooth_block(ene, smooth.at[4]))
    lines_c.give()
    rim_wait(*rim_b)
    for side, edge, inner in ((0, 0, 1), (1, rows - 1, rows - 2)):
        near, far, second = (entry("smooth", "rim", 3 * side + k) for k in range(3))
        for f in range(5):
            smooth[f, edge] += near * rim_in[side, 0, f] + far * rim_in[side, 1, f]
            smooth[f, inner] += second * rim_in[side, 0, f]
        rate[0, edge] -= entry("slope", "rim", 3 * side) * rim_in[side, 0, 2]

    edge_copy.wait()

    @pl.loop(0, 2)
    def _(side):
        product = stream_rows(jnp.concatenate([edge_out[side, f] for f in range(4)], axis=0))
        for f in range(4):
            edge_x[side, f] = product[f * span : (f + 1) * span]
        for f in (0, 2):
            pair = span_pair(
                (edge_out[side, f], edge_out[side, f + 1]), (edge_in[side, f], edge_in[side, f + 1])
            )
            edge_z[side, f] = pair[0]
            edge_z[side, f + 1] = pair[1]

    @pl.loop(0, tiles)
    def _(t):
        z = pl.ds(pl.multiple_of(t * 8, 8), 8)
        for side, row, step in ((0, 0, 1), (1, rows - 1, -1)):
            weights = [entry("slope", "next", 6 * side + k) for k in range(6)]
            u = [edge_out[side, f, z] for f in range(4)]
            past = primitives(*(rim_in[side, 1, f, z] for f in range(5)))
            wall = [
                weights[0] * u[f] + weights[1] * span_out[f, row + step, z]
                + weights[2] * past[f] + weights[3] * span_out[f, row + 2 * step, z]
                + weights[4] * gy[f, row, z] + weights[5] * gy[f, row + step, z]
                for f in range(4)
            ]
            grad = (
                [edge_x[side, f, z] for f in range(3)], wall, [edge_z[side, f, z] for f in range(3)]
            )
            m = [rim_in[side, 0, 1 + c, z] for c in range(3)]
            values = flux_of(1, u, m, rim_in[side, 0, 4, z], rim_in[side, 0, 0, z] * u[3], grad)
            weight = entry("slope", "rim", 3 * side)
            for f in range(4):
                gf[f, row, z] += weight * values[f]

    fspan_copy.wait()
    span_loop(4, fspan_out, fspan_in, store_gz)

    lines_b.finish()

    @pl.loop(0, tiles)
    def _(t):
        z = pl.ds(pl.multiple_of(t * 8, 8), 8)
        from_up = [sb[f * tiles + t] for f in range(6)]
        from_down = [sb[(6 + f) * tiles + t] for f in range(6)]
        for y in range(rows):
            a, b = entry("smooth", "up", y), entry("smooth", "down", y)
            for f in range(5):
                smooth[f, y, z] += a * from_up[f] + b * from_down[f]
            a, b = entry("slope", "up", y), entry("slope", "down", y)
            rate[0, y, z] -= a * from_up[5] + b * from_down[5]

    smooth_flush = pltpu.make_async_copy(smooth, smooth_hbm, s_load.at[4])
    smooth_flush.start()
    mass_flush = pltpu.make_async_copy(rate.at[0], rate_hbm.at[0], s_load.at[6])
    mass_flush.start()

    lines_c.finish()

    @pl.loop(0, tiles)
    def _(t):
        z = pl.ds(pl.multiple_of(t * 8, 8), 8)
        from_up = [sc[f * tiles + t] for f in range(4)]
        from_down = [sc[(4 + f) * tiles + t] for f in range(4)]
        for y in range(rows):
            a, b = entry("slope", "up", y), entry("slope", "down", y)
            keep = tab[base + places["keep"] + y]
            for f in range(4):
                total = gx[f, y, z] + gz[f, y, z] + gf[f, y, z] + a * from_up[f] + b * from_down[f]
                rate[1 + f, y, z] = -(total * keep) if f < 3 else -total

    rest = pl.ds(1, 4)
    rate_flush = pltpu.make_async_copy(rate.at[rest], rate_hbm.at[rest], s_load.at[5])
    rate_flush.start()
    rate_flush.wait()
    mass_flush.wait()
    smooth_flush.wait()


def results_body(rate_from, smooth_from, rate_to, smooth_to, held, sems):
    ins, outs = [], []
    for at, (source, target) in enumerate(((rate_from, rate_to), (smooth_from, smooth_to))):
        for f in range(5):
            ins.append(pltpu.make_async_copy(source.at[f], held.at[at, f], sems.at[0, at, f]))
            outs.append(pltpu.make_async_copy(held.at[at, f], target.at[f], sems.at[1, at, f]))
    for copy in ins:
        copy.start()
    for copy, after in zip(ins, outs):
        copy.wait()
        after.start()
    for after in outs:
        after.wait()


def per_device(mass_per_volume, mass_flux_vector, total_heat_content):
    rows, span, stream = mass_per_volume.shape
    count = lax.axis_size("gy")
    tiles = span // 8
    table, gains = device_table(rows * count, rows)
    each_a = -(-8 * tiles // count)
    each_b = -(-12 * tiles // count)
    pieces = [table]
    for kinds, each in ((["slope"] * 4, each_a), (["smooth"] * 5 + ["slope"], each_b)):
        pieces += gain_tables(kinds, gains, count, tiles, each)
    starts = tuple(int(at) for at in np.cumsum([piece.size for piece in pieces[:-1]]))
    field = (rows, span, stream)
    mats = np.concatenate([stream_table(stream), span_table(2 * span)])
    outer, inner = scan_groups(count)

    def vmem(*shape):
        return pltpu.VMEM(shape, jnp.float32)

    lines_a = [vmem(count * each_a, 8, stream)] * 4
    lines_b = [vmem(count * each_b, 8, stream)] * 4
    totals_a = [vmem(outer * each_a, 8, stream)] * 4
    totals_b = [vmem(outer * each_b, 8, stream)] * 4
    scalar = pl.BlockSpec(memory_space=pltpu.SMEM)
    outside = pl.BlockSpec(memory_space=pl.ANY)
    dma = pltpu.SemaphoreType.DMA
    out = jax.ShapeDtypeStruct((5,) + field, jnp.float32)
    results = pl.pallas_call(
        functools.partial(fused_body, count, starts),
        out_shape=(out, out),
        in_specs=[outside] * 3 + [scalar, outside],
        out_specs=(outside, outside),
        scratch_shapes=[
            vmem(5, *field), vmem(5, *field),
            vmem(*field), vmem(3, *field), vmem(*field), pltpu.VMEM(mats.shape, jnp.bfloat16),
            vmem(5, *field), vmem(5, *field), vmem(4, *field), vmem(4, *field), vmem(5, *field),
            *[vmem(4, *field)] * 5,
            vmem(2, 2, 5, span, stream), vmem(2, 2, 5, span, stream),
            *[vmem(2, 4, span, stream)] * 4,
            *lines_a, *lines_b, *lines_a,
            *totals_a, *totals_b, *totals_a,
            dma((7,)), dma((3,)), dma((3,)), dma((2, 2)), dma((2, 2)),
            dma((12, max(inner, outer))), dma((12, max(inner, outer))),
        ],
        compiler_params=pltpu.CompilerParams(
            collective_id=0, has_side_effects=True, vmem_limit_bytes=56 * 1024 * 1024
        ),
    )(
        mass_per_volume, mass_flux_vector, total_heat_content,
        jnp.asarray(np.concatenate(pieces)), jnp.asarray(mats),
    )
    return pl.pallas_call(
        results_body,
        out_shape=(out, out),
        in_specs=[outside] * 2,
        out_specs=(outside, outside),
        scratch_shapes=[vmem(2, 5, *field), dma((2, 2, 5))],
        compiler_params=pltpu.CompilerParams(vmem_limit_bytes=56 * 1024 * 1024),
    )(*results)


def solution(mesh):
    placed = (P("gy", "pa", None), P(None, "gy", "pa", None), P("gy", "pa", None))
    return jax.shard_map(
        per_device,
        mesh=mesh,
        in_specs=placed,
        out_specs=(P(None, "gy", "pa", None), P(None, "gy", "pa", None)),
        check_vma=False,
    )
```

```python
import functools

import jax
import jax.numpy as jnp
import ml_dtypes
import numpy as np
from jax import lax
from jax.experimental import pallas as pl
from jax.experimental.pallas import tpu as pltpu
from jax.sharding import PartitionSpec as P

GAMMA_GAS = 1.4
PRANDTL = 0.72
VISCOSITY = 0.25
ALPHA_FILTER = 0.499
ALPHA_SLOPE = 0.498
STRETCH = 1.2
STREAM_STEP = 1.0
SPAN_STEP = 0.5
CONDUCT = VISCOSITY * GAMMA_GAS / ((GAMMA_GAS - 1.0) * PRANDTL)
MESH = pl.DeviceIdType.MESH


def slope_weights():
    near_weight = (2.0 + ALPHA_SLOPE) / 3.0
    far_weight = (4.0 * ALPHA_SLOPE - 1.0) / 12.0
    return (near_weight, far_weight)


def system_rows(system_kind, points):
    lower = np.zeros(points)
    middle = np.ones(points)
    upper = np.zeros(points)
    weights = np.zeros((7, points))
    if system_kind == "slope":
        near_weight, far_weight = slope_weights()
        lower[:] = ALPHA_SLOPE
        upper[:] = ALPHA_SLOPE
        weights[1] = -far_weight
        weights[2] = -near_weight
        weights[4] = near_weight
        weights[5] = far_weight
        for edge_row in (1, points - 2):
            lower[edge_row] = 0.25
            upper[edge_row] = 0.25
            weights[:, edge_row] = 0.0
            weights[2, edge_row] = -0.75
            weights[4, edge_row] = 0.75
        lower[0] = 0.0
        upper[0] = 2.0
        weights[:, 0] = 0.0
        weights[3, 0] = -2.5
        weights[4, 0] = 2.0
        weights[5, 0] = 0.5
        lower[points - 1] = 2.0
        upper[points - 1] = 0.0
        weights[:, points - 1] = 0.0
        weights[3, points - 1] = 2.5
        weights[2, points - 1] = -2.0
        weights[1, points - 1] = -0.5
    else:
        strength = ALPHA_FILTER
        lower[:] = strength
        upper[:] = strength
        weights[3] = 11.0 / 16.0 + 5.0 * strength / 8.0
        weights[2] = 15.0 / 64.0 + 17.0 * strength / 32.0
        weights[4] = weights[2]
        weights[1] = -3.0 / 32.0 + 3.0 * strength / 16.0
        weights[5] = weights[1]
        weights[0] = 1.0 / 64.0 - strength / 32.0
        weights[6] = weights[0]
        for edge_row in (2, points - 3):
            weights[:, edge_row] = 0.0
            weights[3, edge_row] = 5.0 / 8.0 + 3.0 * strength / 4.0
            weights[2, edge_row] = 0.25 + strength / 2.0
            weights[4, edge_row] = 0.25 + strength / 2.0
            weights[1, edge_row] = -1.0 / 16.0 + strength / 8.0
            weights[5, edge_row] = -1.0 / 16.0 + strength / 8.0
        for edge_row in (1, points - 2):
            weights[:, edge_row] = 0.0
            weights[3, edge_row] = 0.5 + strength
            weights[2, edge_row] = 0.25 + strength / 2.0
            weights[4, edge_row] = 0.25 + strength / 2.0
        for edge_row in (0, points - 1):
            lower[edge_row] = 0.0
            upper[edge_row] = 0.0
            weights[:, edge_row] = 0.0
            weights[3, edge_row] = 1.0
    return (lower, middle, upper, weights)


def inverse_metric(points):
    places = 2.0 * np.arange(points) / (points - 1) - 1.0
    growth = np.exp(STRETCH * places)
    cosh_values = 0.5 * (growth + 1.0 / growth)
    edge_growth = np.exp(STRETCH)
    tanh_value = (edge_growth - 1.0 / edge_growth) / (edge_growth + 1.0 / edge_growth)
    return tanh_value * cosh_values**2 / (0.64 * STRETCH)


def periodic_matrix(points, spacing):
    near_weight, far_weight = slope_weights()
    wave_numbers = np.arange(1, points // 2)
    angles = 2.0 * np.pi * wave_numbers / points
    modified = (2.0 * near_weight * np.sin(angles) + 2.0 * far_weight * np.sin(2.0 * angles)) / (
        1.0 + 2.0 * ALPHA_SLOPE * np.cos(angles)
    )
    phases = np.arange(points)[:, None] * wave_numbers[None, :] % points
    circulant = -2.0 / (points * spacing) * (np.sin(2.0 * np.pi * phases / points) @ modified)
    shifts = (np.arange(points)[:, None] - np.arange(points)[None, :]) % points
    return circulant[shifts].T


def wall_tables(system_kind, points, rows):
    lower, middle, upper, weights = system_rows(system_kind, points)
    system = np.diag(middle) + np.diag(lower[1:], -1) + np.diag(upper[:-1], 1)
    source = np.zeros((points, points))
    for offset in range(-3, 4):
        for row in range(max(0, -offset), min(points, points - offset)):
            source[row, row + offset] = weights[3 + offset, row]
    band = np.zeros((points, points))
    if system_kind == "slope":
        ratio = slope_weights()[1] / ALPHA_SLOPE
        for row in range(2, points - 2):
            band[row, row + 1] = ratio
            band[row, row - 1] = -ratio
    else:
        mid = points // 2
        strength = ALPHA_FILTER
        two = weights[0, mid] / strength
        one = (weights[1, mid] - two) / strength
        zero = (weights[2, mid] - strength * two - one) / strength
        for row in range(3, points - 3):
            for offset, value in ((0, zero), (1, one), (2, two)):
                band[row, row + offset] = value
                band[row, row - offset] = value
    rest = np.linalg.solve(system, source - system @ band)
    down_ratio = np.zeros(points)
    carried = 0.0
    for row in range(points):
        down_ratio[row] = upper[row] / (middle[row] - lower[row] * carried)
        carried = down_ratio[row]
    up_ratio = np.zeros(points)
    carried = 0.0
    for row in range(points - 1, -1, -1):
        up_ratio[row] = lower[row] / (middle[row] - upper[row] * carried)
        carried = up_ratio[row]
    scale = inverse_metric(points) if system_kind == "slope" else np.ones(points)
    blocks = points // rows
    local = np.zeros((blocks, rows, rows))
    up = np.zeros((blocks, rows))
    down = np.zeros((blocks, rows))
    to_up = np.zeros((blocks, rows))
    to_down = np.zeros((blocks, rows))
    up_gain = np.zeros(blocks)
    down_gain = np.zeros(blocks)
    rim = np.zeros((blocks, 6))
    next_row = np.zeros((blocks, 12))
    near, far = slope_weights()
    for block in range(blocks):
        first, last = block * rows, block * rows + rows - 1
        window = slice(first, last + 1)
        local[block] = (rest + band)[window, window] * scale[window, None]
        up[block] = np.cumprod(np.concatenate([[1.0], -up_ratio[first + 1 : last + 1]]))
        up[block] *= scale[window]
        down[block] = np.cumprod(np.concatenate([[1.0], -down_ratio[first:last][::-1]]))[::-1]
        down[block] *= scale[window]
        if block < blocks - 1:
            to_up[block] = rest[last + 1, window]
            up_gain[block] = np.prod(-up_ratio[first + 1 : last + 2])
            rim[block, 3] = band[last, last + 1] * scale[last]
            rim[block, 4] = band[last, last + 2] * scale[last]
            rim[block, 5] = band[last - 1, last + 1] * scale[last - 1]
            unit = scale[last + 1] / ALPHA_SLOPE
            next_row[block, 6:] = unit * np.array(
                [near, -near, far, -far, -1.0 / scale[last], -ALPHA_SLOPE / scale[last - 1]]
            )
        if block > 0:
            to_down[block] = rest[first - 1, window]
            down_gain[block] = np.prod(-down_ratio[first - 1 : last])
            rim[block, 0] = band[first, first - 1] * scale[first]
            rim[block, 1] = band[first, first - 2] * scale[first]
            rim[block, 2] = band[first + 1, first - 1] * scale[first + 1]
            unit = scale[first - 1] / ALPHA_SLOPE
            next_row[block, :6] = unit * np.array(
                [-near, near, -far, far, -1.0 / scale[first], -ALPHA_SLOPE / scale[first + 1]]
            )
    return local, up, down, to_up, to_down, up_gain, down_gain, rim, next_row


def table_layout(rows):
    sizes = (("local", rows * rows), ("up", rows), ("down", rows), ("to_up", rows), ("to_down", rows), ("rim", 6), ("next", 12))
    places, at = {}, 0
    for kind in ("slope", "smooth"):
        for name, size in sizes:
            places[kind, name] = at
            at += size
    places["keep"] = at
    return places, at + rows


def device_table(points, rows):
    places, width = table_layout(rows)
    blocks = points // rows
    table = np.zeros((blocks, width), np.float32)
    gains = {}
    for kind in ("slope", "smooth"):
        local, up, down, to_up, to_down, up_gain, down_gain, rim, beyond = wall_tables(kind, points, rows)
        gains[kind] = (up_gain, down_gain)
        named = dict(local=local, up=up, down=down, to_up=to_up, to_down=to_down, rim=rim, next=beyond)
        for name, value in named.items():
            flat = value.reshape(blocks, -1)
            at = places[kind, name]
            table[:, at : at + flat.shape[1]] = flat
    table[:, places["keep"] :] = 1.0
    table[0, places["keep"]] = 0.0
    table[-1, -1] = 0.0
    return table.reshape(-1), gains


def scan_groups(count):
    outer = 4 if count % 4 == 0 else 1
    return outer, count // outer


def gain_tables(kinds, gains, count, tiles, each):
    outer, inner = scan_groups(count)
    fields = len(kinds)
    wide = outer * each
    near = np.zeros((count, inner, wide), np.float32)
    far = np.zeros((count, outer, each), np.float32)

    def chain(tile):
        quantity = min(tile // tiles, 2 * fields - 1)
        back = quantity // fields
        return gains[kinds[quantity % fields]][back].reshape(outer, inner), back

    for group in range(outer):
        for place in range(inner):
            owner = group * inner + place
            for slot in range(wide):
                values, back = chain(place * wide + slot)
                near[owner, :, slot] = values[group][::-1] if back else values[group]
            for slot in range(each):
                values, back = chain((place * outer + group) * each + slot)
                product = values.prod(axis=1)
                far[owner, :, slot] = product[::-1] if back else product
    return near.reshape(-1), far.reshape(-1)


def split_pair(matrix):
    high = matrix.astype(np.float32).astype(ml_dtypes.bfloat16)
    low = (matrix - high.astype(np.float64)).astype(np.float32).astype(ml_dtypes.bfloat16)
    return high, low


def stream_table(points):
    high, low = split_pair(periodic_matrix(points, STREAM_STEP))
    return np.block([[high, low], [high, np.zeros_like(low)]])


def span_table(points):
    own = points // 2
    rows = periodic_matrix(points, SPAN_STEP).T[:own]
    high, low = split_pair(rows)
    return np.block([[high, high], [low, np.zeros_like(low)]])


def halves(value):
    high = value.astype(jnp.bfloat16)
    return high, (value - high.astype(jnp.float32)).astype(jnp.bfloat16)


def fused_body(
    count, starts, rho_hbm, mom_hbm, ene_hbm, tab, mats_hbm,
    rate_hbm, smooth_hbm,
    rate, smooth, rho, mom, ene, mats,
    span_out, span_in, gx, gy, gz, fx, fy, gf, fspan_out, fspan_in,
    rim_out, rim_in, edge_out, edge_in, edge_x, edge_z,
    va, ra, oa, sa, vb, rb, ob, sb, vc, rc, oc, sc,
    ta, rta, ota, sta, tb, rtb, otb, stb, tc, rtc, otc, stc,
    s_load, s_span, r_span, s_rim, r_rim, s_line, r_line,
):
    rows, span, _ = rho.shape
    tiles = span // 8
    me, core = lax.axis_index("gy"), lax.axis_index("pa")
    outer, inner = scan_groups(count)
    group, place = me // inner, lax.rem(me, inner)
    places, width = table_layout(rows)
    base = me * width

    def entry(kind, name, at):
        return tab[base + places[kind, name] + at]

    def remote(src, dst, send, recv, target, target_core):
        return pltpu.make_async_remote_copy(
            src_ref=src, dst_ref=dst, send_sem=send, recv_sem=recv,
            device_id=(target, target_core), device_id_type=MESH,
        )

    loads = [
        pltpu.make_async_copy(source, target, s_load.at[at])
        for at, (source, target) in enumerate(
            ((rho_hbm, rho), (mom_hbm, mom), (ene_hbm, ene), (mats_hbm, mats))
        )
    ]
    for load in loads:
        load.start()

    barrier = pltpu.get_barrier_semaphore()

    @pl.loop(1, count)
    def _(step):
        pl.semaphore_signal(
            barrier, inc=1, device_id=(lax.rem(me + step, count), core), device_id_type=MESH
        )

    pl.semaphore_signal(barrier, inc=1, device_id=(me, 1 - core), device_id_type=MESH)

    for load in loads:
        load.wait()

    for depth in range(2):
        for side, row in ((0, rows - 1 - depth), (1, depth)):
            rim_out[side, depth, 0] = rho[row]
            for c in range(3):
                rim_out[side, depth, 1 + c] = mom[c, row]
            rim_out[side, depth, 4] = ene[row]

    @pl.when(me == 0)
    def _():
        rim_in[0] = jnp.ones(rim_in.shape[1:], jnp.float32)

    @pl.when(me == count - 1)
    def _():
        rim_in[1] = jnp.ones(rim_in.shape[1:], jnp.float32)

    def primitives(d, m0, m1, m2, e):
        inv = 1.0 / d
        u, v, w = m0 * inv, m1 * inv, m2 * inv
        push = (GAMMA_GAS - 1.0) * (e - 0.5 * (u * m0 + v * m1 + w * m2))
        return u, v, w, push * inv

    @pl.loop(0, tiles)
    def _(t):
        z = pl.ds(pl.multiple_of(t * 8, 8), 8)
        ups, downs = [None] * 4, [None] * 4
        for y in range(rows):
            m2 = mom[2, y, z]
            values = primitives(rho[y, z], mom[0, y, z], mom[1, y, z], m2, ene[y, z])
            a, b = entry("slope", "to_up", y), entry("slope", "to_down", y)
            for f in range(4):
                span_out[f, y, z] = values[f]
                ups[f] = a * values[f] if y == 0 else ups[f] + a * values[f]
                downs[f] = b * values[f] if y == 0 else downs[f] + b * values[f]
            span_out[4, y, z] = m2
        for f in range(4):
            va[f * tiles + t] = ups[f]
            va[(4 + f) * tiles + t] = downs[f]

    pl.semaphore_wait(barrier, count)

    def rim_send(source, into, slot):
        def make(side, target):
            return remote(source(side), into(side), s_rim.at[slot, side], r_rim.at[slot, side], target, core)

        @pl.when(me < count - 1)
        def _():
            make(0, me + 1).start()

        @pl.when(me > 0)
        def _():
            make(1, me - 1).start()

    def rim_wait(source, into, slot):
        def make(side, target):
            return remote(source(side), into(side), s_rim.at[slot, side], r_rim.at[slot, side], target, core)

        @pl.when(me < count - 1)
        def _():
            make(0, me + 1).wait_send()
            make(1, me + 1).wait_recv()

        @pl.when(me > 0)
        def _():
            make(1, me - 1).wait_send()
            make(0, me - 1).wait_recv()

    def in_group(at):
        return group * inner + at

    def across(at):
        return at * inner + place

    def spread(src, dst, line, size, mine, device):
        each = src.shape[0] // size
        own = pl.ds(mine * each, each)

        @pl.loop(1, size)
        def _(step):
            to = lax.rem(mine + step, size)
            remote(
                src.at[pl.ds(to * each, each)], dst.at[own],
                s_line.at[line, step], r_line.at[line, step], device(to), core,
            ).start()

        dst[own] = src[own]

    def spread_wait(src, dst, line, size, mine, device):
        each = src.shape[0] // size

        @pl.loop(1, size)
        def _(step):
            to = lax.rem(mine + step, size)
            fro = lax.rem(mine + size - step, size)
            remote(
                src.at[pl.ds(to * each, each)], dst.at[pl.ds(mine * each, each)],
                s_line.at[line, step], r_line.at[line, step], device(to), core,
            ).wait_send()
            remote(
                src.at[pl.ds(to * each, each)], dst.at[pl.ds(fro * each, each)],
                s_line.at[line, step], r_line.at[line, step], device(to), core,
            ).wait_recv()

    def scan(src, first, gain_at, turned, size, emit):
        each = src.shape[0] // size

        def lap(i, carry):
            j = i + turned * (size - 1 - 2 * i)
            emit(j, carry)
            return tuple(
                tab[gain_at + i * each + k] * carry[k] + src[j * each + k] for k in range(each)
            )

        return lax.fori_loop(0, size, lap, first)

    def sender(out, back, line, size, mine, device):
        each = out.shape[0] // size

        def emit(j, carry):
            at = pl.ds(j * each, each)
            for k in range(each):
                out[j * each + k] = carry[k]

            @pl.when(j != mine)
            def _():
                step = lax.rem(j - mine + size, size)
                remote(
                    out.at[at], back.at[pl.ds(mine * each, each)],
                    s_line.at[line, step], r_line.at[line, step], device(j), core,
                ).start()

            @pl.when(j == mine)
            def _():
                back[at] = out[at]

        return emit

    class Lines:
        def __init__(self, at, fields, near, far, values, got, out, back, total, tgot, tout, tback):
            self.values, self.got, self.out, self.back = values, got, out, back
            self.total, self.tgot, self.tout, self.tback = total, tgot, tout, tback
            self.line = 4 * at
            self.each = values.shape[0] // count
            wide = outer * self.each
            self.wide = wide
            self.turned = jnp.minimum((place * wide) // (fields * tiles), 1)
            self.near = near + me * (inner * wide)
            self.far = far + me * (outer * self.each)
            ring, column = (inner, place, in_group), (outer, group, across)
            self.hops = (
                (values, got, self.line, *ring),
                (total, tgot, self.line + 1, *column),
                (tout, tback, self.line + 2, *column),
                (out, back, self.line + 3, *ring),
            )

        def start(self):
            spread(*self.hops[0])

        def wait(self, hop):
            spread_wait(*self.hops[hop])

        def gather(self):
            self.wait(0)
            zeros = tuple(jnp.zeros((8, 128), jnp.float32) for _ in range(self.wide))
            total = scan(self.got, zeros, self.near, self.turned, inner, lambda j, carry: None)
            for k in range(self.wide):
                self.total[k] = total[k]
            spread(*self.hops[1])

        def cross(self):
            self.wait(1)
            zeros = tuple(jnp.zeros((8, 128), jnp.float32) for _ in range(self.each))
            scan(self.tgot, zeros, self.far, self.turned, outer, sender(*self.hops[2]))

        def give(self):
            self.wait(2)
            first = tuple(self.tback[k] for k in range(self.wide))
            scan(self.got, first, self.near, self.turned, inner, sender(*self.hops[3]))

        def finish(self):
            self.wait(3)

    near_a, far_a, near_b, far_b = starts
    lines_a = Lines(0, 4, near_a, far_a, va, ra, oa, sa, ta, rta, ota, sta)
    lines_b = Lines(1, 6, near_b, far_b, vb, rb, ob, sb, tb, rtb, otb, stb)
    lines_c = Lines(2, 4, near_a, far_a, vc, rc, oc, sc, tc, rtc, otc, stc)

    rim_a = (lambda side: rim_out.at[side, 0], lambda side: rim_in.at[side, 0], 0)
    rim_b = (lambda side: rim_out.at[side, 1], lambda side: rim_in.at[side, 1], 1)
    span_copy = remote(span_out, span_in, s_span.at[0], r_span.at[0], me, 1 - core)
    fspan_copy = remote(fspan_out, fspan_in, s_span.at[1], r_span.at[1], me, 1 - core)
    edge_copy = remote(edge_out, edge_in, s_span.at[2], r_span.at[2], me, 1 - core)

    lines_a.start()
    rim_send(*rim_a)
    span_copy.start()

    def local_rows(kind, load, store, z):
        values = [load(y) for y in range(rows)]
        for y in range(rows):
            total = entry(kind, "local", y * rows) * values[0]
            for k in range(1, rows):
                total = total + entry(kind, "local", y * rows + k) * values[k]
            store(y, total)

    def block_loop(fields, size, body):
        per = span // size

        @pl.loop(0, fields * per)
        def _(i):
            body(i // per, pl.ds(pl.multiple_of((i % per) * size, size), size))

    def slope_block(src, dst):
        def body(f, z):
            def store(y, total):
                dst[f, y, z] = total

            local_rows("slope", lambda y: src[f, y, z], store, z)

        return body

    def stream_rows(value):
        high, low = halves(value)
        product = jnp.dot(
            jnp.concatenate([high, low], axis=1), mats[pl.ds(0, 256)], preferred_element_type=jnp.float32
        )
        return product[:, :128] + product[:, 128:]

    def stream_loop(fields, load, store):
        @pl.loop(0, fields)
        def _(f):
            product = stream_rows(jnp.concatenate([load(f, y) for y in range(rows)], axis=0))
            for y in range(rows):
                store(f, y, product[y * span : (y + 1) * span])

    def span_pair(own, other):
        parts = [halves(jnp.concatenate(pair, axis=1)) for pair in (own, other)]
        stacked = jnp.concatenate([parts[0][0], parts[1][0], parts[0][1], parts[1][1]], axis=0)
        product = jnp.dot(mats[pl.ds(256, 128)], stacked, preferred_element_type=jnp.float32)
        product = product[:span] + product[span:]
        return product[:, :128], product[:, 128:]

    def span_loop(first, last, own, other, store):
        @pl.loop(first, last)
        def _(f):
            for y in range(0, rows, 2):
                pair = span_pair((own[f, y], own[f, y + 1]), (other[f, y], other[f, y + 1]))
                store(f, y, pair[0])
                store(f, y + 1, pair[1])

    def store_gx(f, y, value):
        gx[f, y] = value

    def store_gz(f, y, value):
        gz[f, y] = value

    stream_loop(4, lambda f, y: span_out[f, y], store_gx)
    lines_a.gather()

    @pl.loop(0, tiles)
    def _(t):
        z = pl.ds(pl.multiple_of(t * 8, 8), 8)
        ups, downs = [None] * 6, [None] * 6
        for y in range(rows):
            middle = mom[1, y, z]
            values = (rho[y, z], mom[0, y, z], middle, mom[2, y, z], ene[y, z], middle)
            pairs = [
                (entry(kind, "to_up", y), entry(kind, "to_down", y)) for kind in ("smooth", "slope")
            ]
            for f in range(6):
                a, b = pairs[f // 5]
                ups[f] = a * values[f] if y == 0 else ups[f] + a * values[f]
                downs[f] = b * values[f] if y == 0 else downs[f] + b * values[f]
        for f in range(6):
            vb[f * tiles + t] = ups[f]
            vb[(6 + f) * tiles + t] = downs[f]

    lines_b.start()
    lines_a.cross()
    block_loop(4, 32, slope_block(span_out, gy))
    lines_a.give()

    span_copy.wait()
    span_loop(0, 4, span_out, span_in, store_gz)

    rim_wait(*rim_a)
    for side, row in ((0, 0), (1, rows - 1)):
        weight = entry("slope", "rim", 3 * side)
        values = primitives(*(rim_in[side, 0, f] for f in range(5)))
        for f in range(4):
            edge_out[side, f] = values[f]
            gy[f, row] += weight * values[f]
    edge_copy.start()

    lines_b.gather()
    lines_a.finish()
    rim_send(*rim_b)

    def stress_of(grad, d):
        row = [VISCOSITY * (grad[d][c] + grad[c][d]) for c in range(3)]
        spread_out = (2.0 / 3.0 * VISCOSITY) * (grad[0][0] + grad[1][1] + grad[2][2])
        row[d] = (2.0 * VISCOSITY) * grad[d][d] - spread_out
        return row

    def flux_of(d, u, m, e, push, grad):
        stress = stress_of(grad, d)
        energy = (e + push) * u[d] - CONDUCT * grad[d][3]
        values = []
        for c in range(3):
            energy = energy - u[c] * stress[c]
            value = m[c] * u[d] - stress[c]
            values.append(value + push if c == d else value)
        return values + [energy]

    def cell(y, z):
        u = [span_out[f, y, z] for f in range(4)]
        return u, [mom[c, y, z] for c in range(3)], ene[y, z], rho[y, z] * u[3]

    @pl.loop(0, tiles)
    def _(t):
        z = pl.ds(pl.multiple_of(t * 8, 8), 8)
        ups, downs = [None] * 4, [None] * 4
        from_up = [sa[f * tiles + t] for f in range(4)]
        from_down = [sa[(4 + f) * tiles + t] for f in range(4)]
        for y in range(rows):
            a, b = entry("slope", "up", y), entry("slope", "down", y)
            wall = [gy[f, y, z] + a * from_up[f] + b * from_down[f] for f in range(4)]
            for f in range(4):
                gy[f, y, z] = wall[f]
            grad = ([gx[f, y, z] for f in range(3)], wall, [gz[f, y, z] for f in range(3)])
            values = flux_of(1, *cell(y, z), grad)
            a, b = entry("slope", "to_up", y), entry("slope", "to_down", y)
            for f in range(4):
                fy[f, y, z] = values[f]
                ups[f] = a * values[f] if y == 0 else ups[f] + a * values[f]
                downs[f] = b * values[f] if y == 0 else downs[f] + b * values[f]
        for f in range(4):
            vc[f * tiles + t] = ups[f]
            vc[(4 + f) * tiles + t] = downs[f]

    lines_c.start()

    @pl.loop(0, tiles)
    def _(t):
        z = pl.ds(pl.multiple_of(t * 8, 8), 8)
        for y in range(rows):
            grad = [[ref[f, y, z] for f in range(4)] for ref in (gx, gy, gz)]
            state = cell(y, z)
            for d, out in ((2, fspan_out), (0, fx)):
                values = flux_of(d, *state, grad)
                for f in range(4):
                    out[f, y, z] = values[f]

    fspan_copy.start()
    lines_b.cross()

    def store_fx(f, y, value):
        gx[f, y] = value

    stream_loop(4, lambda f, y: fx[f, y], store_fx)
    lines_c.gather()
    lines_b.give()
    block_loop(4, 32, slope_block(fy, gf))
    lines_c.cross()

    span_loop(4, 5, span_out, span_in, store_gz)

    def store_mass(f, y, value):
        rate[0, y] = value

    stream_loop(1, lambda f, y: mom[0, y], store_mass)

    def mass_block(f, z):
        def store(y, total):
            rate[0, y, z] = -(rate[0, y, z] + total + gz[4, y, z])

        local_rows("slope", lambda y: mom[1, y, z], store, z)

    block_loop(1, 32, mass_block)

    def smooth_block(read, write):
        def body(f, z):
            def store(y, total):
                write[y, z] = total

            local_rows("smooth", lambda y: read[y, z], store, z)

        return body

    block_loop(1, 32, smooth_block(rho, smooth.at[0]))

    def smooth_mom(f, z):
        def store(y, total):
            smooth[1 + f, y, z] = total

        local_rows("smooth", lambda y: mom[f, y, z], store, z)

    block_loop(3, 32, smooth_mom)
    block_loop(1, 32, smooth_block(ene, smooth.at[4]))
    lines_c.give()
    rim_wait(*rim_b)
    for side, edge, inner in ((0, 0, 1), (1, rows - 1, rows - 2)):
        near, far, second = (entry("smooth", "rim", 3 * side + k) for k in range(3))
        for f in range(5):
            smooth[f, edge] += near * rim_in[side, 0, f] + far * rim_in[side, 1, f]
            smooth[f, inner] += second * rim_in[side, 0, f]
        rate[0, edge] -= entry("slope", "rim", 3 * side) * rim_in[side, 0, 2]

    edge_copy.wait()

    @pl.loop(0, 2)
    def _(side):
        product = stream_rows(jnp.concatenate([edge_out[side, f] for f in range(4)], axis=0))
        for f in range(4):
            edge_x[side, f] = product[f * span : (f + 1) * span]
        for f in (0, 2):
            pair = span_pair(
                (edge_out[side, f], edge_out[side, f + 1]), (edge_in[side, f], edge_in[side, f + 1])
            )
            edge_z[side, f] = pair[0]
            edge_z[side, f + 1] = pair[1]

    @pl.loop(0, tiles)
    def _(t):
        z = pl.ds(pl.multiple_of(t * 8, 8), 8)
        for side, row, step in ((0, 0, 1), (1, rows - 1, -1)):
            weights = [entry("slope", "next", 6 * side + k) for k in range(6)]
            u = [edge_out[side, f, z] for f in range(4)]
            past = primitives(*(rim_in[side, 1, f, z] for f in range(5)))
            wall = [
                weights[0] * u[f] + weights[1] * span_out[f, row + step, z]
                + weights[2] * past[f] + weights[3] * span_out[f, row + 2 * step, z]
                + weights[4] * gy[f, row, z] + weights[5] * gy[f, row + step, z]
                for f in range(4)
            ]
            grad = (
                [edge_x[side, f, z] for f in range(3)], wall, [edge_z[side, f, z] for f in range(3)]
            )
            m = [rim_in[side, 0, 1 + c, z] for c in range(3)]
            values = flux_of(1, u, m, rim_in[side, 0, 4, z], rim_in[side, 0, 0, z] * u[3], grad)
            weight = entry("slope", "rim", 3 * side)
            for f in range(4):
                gf[f, row, z] += weight * values[f]

    fspan_copy.wait()
    span_loop(0, 4, fspan_out, fspan_in, store_gz)

    lines_b.finish()

    @pl.loop(0, tiles)
    def _(t):
        z = pl.ds(pl.multiple_of(t * 8, 8), 8)
        from_up = [sb[f * tiles + t] for f in range(6)]
        from_down = [sb[(6 + f) * tiles + t] for f in range(6)]
        for y in range(rows):
            a, b = entry("smooth", "up", y), entry("smooth", "down", y)
            for f in range(5):
                smooth[f, y, z] += a * from_up[f] + b * from_down[f]
            a, b = entry("slope", "up", y), entry("slope", "down", y)
            rate[0, y, z] -= a * from_up[5] + b * from_down[5]

    smooth_flush = pltpu.make_async_copy(smooth, smooth_hbm, s_load.at[4])
    smooth_flush.start()
    mass_flush = pltpu.make_async_copy(rate.at[0], rate_hbm.at[0], s_load.at[6])
    mass_flush.start()

    lines_c.finish()

    @pl.loop(0, tiles)
    def _(t):
        z = pl.ds(pl.multiple_of(t * 8, 8), 8)
        from_up = [sc[f * tiles + t] for f in range(4)]
        from_down = [sc[(4 + f) * tiles + t] for f in range(4)]
        for y in range(rows):
            a, b = entry("slope", "up", y), entry("slope", "down", y)
            keep = tab[base + places["keep"] + y]
            for f in range(4):
                total = gx[f, y, z] + gz[f, y, z] + gf[f, y, z] + a * from_up[f] + b * from_down[f]
                rate[1 + f, y, z] = -(total * keep) if f < 3 else -total

    rest = pl.ds(1, 4)
    rate_flush = pltpu.make_async_copy(rate.at[rest], rate_hbm.at[rest], s_load.at[5])
    rate_flush.start()
    rate_flush.wait()
    mass_flush.wait()
    smooth_flush.wait()


def results_body(rate_from, smooth_from, rate_to, smooth_to, held, sems):
    ins, outs = [], []
    for at, (source, target) in enumerate(((rate_from, rate_to), (smooth_from, smooth_to))):
        for f in range(5):
            ins.append(pltpu.make_async_copy(source.at[f], held.at[at, f], sems.at[0, at, f]))
            outs.append(pltpu.make_async_copy(held.at[at, f], target.at[f], sems.at[1, at, f]))
    for copy in ins:
        copy.start()
    for copy, after in zip(ins, outs):
        copy.wait()
        after.start()
    for after in outs:
        after.wait()


def per_device(mass_per_volume, mass_flux_vector, total_heat_content):
    rows, span, stream = mass_per_volume.shape
    count = lax.axis_size("gy")
    tiles = span // 8
    table, gains = device_table(rows * count, rows)
    each_a = -(-8 * tiles // count)
    each_b = -(-12 * tiles // count)
    pieces = [table]
    for kinds, each in ((["slope"] * 4, each_a), (["smooth"] * 5 + ["slope"], each_b)):
        pieces += gain_tables(kinds, gains, count, tiles, each)
    starts = tuple(int(at) for at in np.cumsum([piece.size for piece in pieces[:-1]]))
    field = (rows, span, stream)
    mats = np.concatenate([stream_table(stream), span_table(2 * span)])
    outer, inner = scan_groups(count)

    def vmem(*shape):
        return pltpu.VMEM(shape, jnp.float32)

    lines_a = [vmem(count * each_a, 8, stream)] * 4
    lines_b = [vmem(count * each_b, 8, stream)] * 4
    totals_a = [vmem(outer * each_a, 8, stream)] * 4
    totals_b = [vmem(outer * each_b, 8, stream)] * 4
    scalar = pl.BlockSpec(memory_space=pltpu.SMEM)
    outside = pl.BlockSpec(memory_space=pl.ANY)
    dma = pltpu.SemaphoreType.DMA
    out = jax.ShapeDtypeStruct((5,) + field, jnp.float32)
    results = pl.pallas_call(
        functools.partial(fused_body, count, starts),
        out_shape=(out, out),
        in_specs=[outside] * 3 + [scalar, outside],
        out_specs=(outside, outside),
        scratch_shapes=[
            vmem(5, *field), vmem(5, *field),
            vmem(*field), vmem(3, *field), vmem(*field), pltpu.VMEM(mats.shape, jnp.bfloat16),
            vmem(5, *field), vmem(5, *field), vmem(4, *field), vmem(4, *field), vmem(5, *field),
            *[vmem(4, *field)] * 5,
            vmem(2, 2, 5, span, stream), vmem(2, 2, 5, span, stream),
            *[vmem(2, 4, span, stream)] * 4,
            *lines_a, *lines_b, *lines_a,
            *totals_a, *totals_b, *totals_a,
            dma((7,)), dma((3,)), dma((3,)), dma((2, 2)), dma((2, 2)),
            dma((12, max(inner, outer))), dma((12, max(inner, outer))),
        ],
        compiler_params=pltpu.CompilerParams(
            collective_id=0, has_side_effects=True, vmem_limit_bytes=56 * 1024 * 1024
        ),
    )(
        mass_per_volume, mass_flux_vector, total_heat_content,
        jnp.asarray(np.concatenate(pieces)), jnp.asarray(mats),
    )
    return pl.pallas_call(
        results_body,
        out_shape=(out, out),
        in_specs=[outside] * 2,
        out_specs=(outside, outside),
        scratch_shapes=[vmem(2, 5, *field), dma((2, 2, 5))],
        compiler_params=pltpu.CompilerParams(vmem_limit_bytes=56 * 1024 * 1024),
    )(*results)


def solution(mesh):
    placed = (P("gy", "pa", None), P(None, "gy", "pa", None), P("gy", "pa", None))
    return jax.shard_map(
        per_device,
        mesh=mesh,
        in_specs=placed,
        out_specs=(P(None, "gy", "pa", None), P(None, "gy", "pa", None)),
        check_vma=False,
    )
```

```python
import functools

import jax
import jax.numpy as jnp
import ml_dtypes
import numpy as np
from jax import lax
from jax.experimental import pallas as pl
from jax.experimental.pallas import tpu as pltpu
from jax.sharding import PartitionSpec as P

GAMMA_GAS = 1.4
PRANDTL = 0.72
VISCOSITY = 0.25
ALPHA_FILTER = 0.499
ALPHA_SLOPE = 0.498
STRETCH = 1.2
STREAM_STEP = 1.0
SPAN_STEP = 0.5
CONDUCT = VISCOSITY * GAMMA_GAS / ((GAMMA_GAS - 1.0) * PRANDTL)
MESH = pl.DeviceIdType.MESH


def slope_weights():
    near_weight = (2.0 + ALPHA_SLOPE) / 3.0
    far_weight = (4.0 * ALPHA_SLOPE - 1.0) / 12.0
    return (near_weight, far_weight)


def system_rows(system_kind, points):
    lower = np.zeros(points)
    middle = np.ones(points)
    upper = np.zeros(points)
    weights = np.zeros((7, points))
    if system_kind == "slope":
        near_weight, far_weight = slope_weights()
        lower[:] = ALPHA_SLOPE
        upper[:] = ALPHA_SLOPE
        weights[1] = -far_weight
        weights[2] = -near_weight
        weights[4] = near_weight
        weights[5] = far_weight
        for edge_row in (1, points - 2):
            lower[edge_row] = 0.25
            upper[edge_row] = 0.25
            weights[:, edge_row] = 0.0
            weights[2, edge_row] = -0.75
            weights[4, edge_row] = 0.75
        lower[0] = 0.0
        upper[0] = 2.0
        weights[:, 0] = 0.0
        weights[3, 0] = -2.5
        weights[4, 0] = 2.0
        weights[5, 0] = 0.5
        lower[points - 1] = 2.0
        upper[points - 1] = 0.0
        weights[:, points - 1] = 0.0
        weights[3, points - 1] = 2.5
        weights[2, points - 1] = -2.0
        weights[1, points - 1] = -0.5
    else:
        strength = ALPHA_FILTER
        lower[:] = strength
        upper[:] = strength
        weights[3] = 11.0 / 16.0 + 5.0 * strength / 8.0
        weights[2] = 15.0 / 64.0 + 17.0 * strength / 32.0
        weights[4] = weights[2]
        weights[1] = -3.0 / 32.0 + 3.0 * strength / 16.0
        weights[5] = weights[1]
        weights[0] = 1.0 / 64.0 - strength / 32.0
        weights[6] = weights[0]
        for edge_row in (2, points - 3):
            weights[:, edge_row] = 0.0
            weights[3, edge_row] = 5.0 / 8.0 + 3.0 * strength / 4.0
            weights[2, edge_row] = 0.25 + strength / 2.0
            weights[4, edge_row] = 0.25 + strength / 2.0
            weights[1, edge_row] = -1.0 / 16.0 + strength / 8.0
            weights[5, edge_row] = -1.0 / 16.0 + strength / 8.0
        for edge_row in (1, points - 2):
            weights[:, edge_row] = 0.0
            weights[3, edge_row] = 0.5 + strength
            weights[2, edge_row] = 0.25 + strength / 2.0
            weights[4, edge_row] = 0.25 + strength / 2.0
        for edge_row in (0, points - 1):
            lower[edge_row] = 0.0
            upper[edge_row] = 0.0
            weights[:, edge_row] = 0.0
            weights[3, edge_row] = 1.0
    return (lower, middle, upper, weights)


def inverse_metric(points):
    places = 2.0 * np.arange(points) / (points - 1) - 1.0
    growth = np.exp(STRETCH * places)
    cosh_values = 0.5 * (growth + 1.0 / growth)
    edge_growth = np.exp(STRETCH)
    tanh_value = (edge_growth - 1.0 / edge_growth) / (edge_growth + 1.0 / edge_growth)
    return tanh_value * cosh_values**2 / (0.64 * STRETCH)


def periodic_matrix(points, spacing):
    near_weight, far_weight = slope_weights()
    wave_numbers = np.arange(1, points // 2)
    angles = 2.0 * np.pi * wave_numbers / points
    modified = (2.0 * near_weight * np.sin(angles) + 2.0 * far_weight * np.sin(2.0 * angles)) / (
        1.0 + 2.0 * ALPHA_SLOPE * np.cos(angles)
    )
    phases = np.arange(points)[:, None] * wave_numbers[None, :] % points
    circulant = -2.0 / (points * spacing) * (np.sin(2.0 * np.pi * phases / points) @ modified)
    shifts = (np.arange(points)[:, None] - np.arange(points)[None, :]) % points
    return circulant[shifts].T


def wall_tables(system_kind, points, rows):
    lower, middle, upper, weights = system_rows(system_kind, points)
    system = np.diag(middle) + np.diag(lower[1:], -1) + np.diag(upper[:-1], 1)
    source = np.zeros((points, points))
    for offset in range(-3, 4):
        for row in range(max(0, -offset), min(points, points - offset)):
            source[row, row + offset] = weights[3 + offset, row]
    band = np.zeros((points, points))
    if system_kind == "slope":
        ratio = slope_weights()[1] / ALPHA_SLOPE
        for row in range(2, points - 2):
            band[row, row + 1] = ratio
            band[row, row - 1] = -ratio
    else:
        mid = points // 2
        strength = ALPHA_FILTER
        two = weights[0, mid] / strength
        one = (weights[1, mid] - two) / strength
        zero = (weights[2, mid] - strength * two - one) / strength
        for row in range(3, points - 3):
            for offset, value in ((0, zero), (1, one), (2, two)):
                band[row, row + offset] = value
                band[row, row - offset] = value
    rest = np.linalg.solve(system, source - system @ band)
    down_ratio = np.zeros(points)
    carried = 0.0
    for row in range(points):
        down_ratio[row] = upper[row] / (middle[row] - lower[row] * carried)
        carried = down_ratio[row]
    up_ratio = np.zeros(points)
    carried = 0.0
    for row in range(points - 1, -1, -1):
        up_ratio[row] = lower[row] / (middle[row] - upper[row] * carried)
        carried = up_ratio[row]
    scale = inverse_metric(points) if system_kind == "slope" else np.ones(points)
    blocks = points // rows
    local = np.zeros((blocks, rows, rows))
    up = np.zeros((blocks, rows))
    down = np.zeros((blocks, rows))
    to_up = np.zeros((blocks, rows))
    to_down = np.zeros((blocks, rows))
    up_gain = np.zeros(blocks)
    down_gain = np.zeros(blocks)
    rim = np.zeros((blocks, 6))
    next_row = np.zeros((blocks, 12))
    near, far = slope_weights()
    for block in range(blocks):
        first, last = block * rows, block * rows + rows - 1
        window = slice(first, last + 1)
        local[block] = (rest + band)[window, window] * scale[window, None]
        up[block] = np.cumprod(np.concatenate([[1.0], -up_ratio[first + 1 : last + 1]]))
        up[block] *= scale[window]
        down[block] = np.cumprod(np.concatenate([[1.0], -down_ratio[first:last][::-1]]))[::-1]
        down[block] *= scale[window]
        if block < blocks - 1:
            to_up[block] = rest[last + 1, window]
            up_gain[block] = np.prod(-up_ratio[first + 1 : last + 2])
            rim[block, 3] = band[last, last + 1] * scale[last]
            rim[block, 4] = band[last, last + 2] * scale[last]
            rim[block, 5] = band[last - 1, last + 1] * scale[last - 1]
            unit = scale[last + 1] / ALPHA_SLOPE
            next_row[block, 6:] = unit * np.array(
                [near, -near, far, -far, -1.0 / scale[last], -ALPHA_SLOPE / scale[last - 1]]
            )
        if block > 0:
            to_down[block] = rest[first - 1, window]
            down_gain[block] = np.prod(-down_ratio[first - 1 : last])
            rim[block, 0] = band[first, first - 1] * scale[first]
            rim[block, 1] = band[first, first - 2] * scale[first]
            rim[block, 2] = band[first + 1, first - 1] * scale[first + 1]
            unit = scale[first - 1] / ALPHA_SLOPE
            next_row[block, :6] = unit * np.array(
                [-near, near, -far, far, -1.0 / scale[first], -ALPHA_SLOPE / scale[first + 1]]
            )
    return local, up, down, to_up, to_down, up_gain, down_gain, rim, next_row


def table_layout(rows):
    sizes = (("local", rows * rows), ("up", rows), ("down", rows), ("to_up", rows), ("to_down", rows), ("rim", 6), ("next", 12))
    places, at = {}, 0
    for kind in ("slope", "smooth"):
        for name, size in sizes:
            places[kind, name] = at
            at += size
    places["keep"] = at
    return places, at + rows


def device_table(points, rows):
    places, width = table_layout(rows)
    blocks = points // rows
    table = np.zeros((blocks, width), np.float32)
    gains = {}
    for kind in ("slope", "smooth"):
        local, up, down, to_up, to_down, up_gain, down_gain, rim, beyond = wall_tables(kind, points, rows)
        gains[kind] = (up_gain, down_gain)
        named = dict(local=local, up=up, down=down, to_up=to_up, to_down=to_down, rim=rim, next=beyond)
        for name, value in named.items():
            flat = value.reshape(blocks, -1)
            at = places[kind, name]
            table[:, at : at + flat.shape[1]] = flat
    table[:, places["keep"] :] = 1.0
    table[0, places["keep"]] = 0.0
    table[-1, -1] = 0.0
    return table.reshape(-1), gains


def scan_groups(count):
    outer = 4 if count % 4 == 0 else 1
    return outer, count // outer


def gain_tables(kinds, gains, count, tiles, each):
    outer, inner = scan_groups(count)
    fields = len(kinds)
    wide = outer * each
    near = np.zeros((count, inner, wide), np.float32)
    far = np.zeros((count, outer, each), np.float32)

    def chain(tile):
        quantity = min(tile // tiles, 2 * fields - 1)
        back = quantity // fields
        return gains[kinds[quantity % fields]][back].reshape(outer, inner), back

    for group in range(outer):
        for place in range(inner):
            owner = group * inner + place
            for slot in range(wide):
                values, back = chain(place * wide + slot)
                near[owner, :, slot] = values[group][::-1] if back else values[group]
            for slot in range(each):
                values, back = chain((place * outer + group) * each + slot)
                product = values.prod(axis=1)
                far[owner, :, slot] = product[::-1] if back else product
    return near.reshape(-1), far.reshape(-1)


def split_pair(matrix):
    high = matrix.astype(np.float32).astype(ml_dtypes.bfloat16)
    low = (matrix - high.astype(np.float64)).astype(np.float32).astype(ml_dtypes.bfloat16)
    return high, low


def stream_table(points):
    high, low = split_pair(periodic_matrix(points, STREAM_STEP))
    return np.block([[high, low], [high, np.zeros_like(low)]])


def span_table(points):
    own = points // 2
    rows = periodic_matrix(points, SPAN_STEP).T[:own]
    high, low = split_pair(rows)
    return np.block([[high, high], [low, np.zeros_like(low)]])


def halves(value):
    high = value.astype(jnp.bfloat16)
    return high, (value - high.astype(jnp.float32)).astype(jnp.bfloat16)


def fused_body(
    count, starts, rho_hbm, mom_hbm, ene_hbm, tab, mats_hbm,
    rate_hbm, smooth_hbm,
    rate, smooth, rho, mom, ene, mats,
    span_out, span_in, gx, gy, gz, fx, fy, gf, fspan_out, fspan_in,
    rim_out, rim_in, edge_out, edge_in, edge_x, edge_z,
    va, ra, oa, sa, vb, rb, ob, sb, vc, rc, oc, sc,
    ta, rta, ota, sta, tb, rtb, otb, stb, tc, rtc, otc, stc,
    s_load, s_span, r_span, s_rim, r_rim, s_line, r_line,
):
    rows, span, _ = rho.shape
    tiles = span // 8
    me, core = lax.axis_index("gy"), lax.axis_index("pa")
    outer, inner = scan_groups(count)
    group, place = me // inner, lax.rem(me, inner)
    places, width = table_layout(rows)
    base = me * width

    def entry(kind, name, at):
        return tab[base + places[kind, name] + at]

    def remote(src, dst, send, recv, target, target_core):
        return pltpu.make_async_remote_copy(
            src_ref=src, dst_ref=dst, send_sem=send, recv_sem=recv,
            device_id=(target, target_core), device_id_type=MESH,
        )

    loads = [
        pltpu.make_async_copy(source, target, s_load.at[at])
        for at, (source, target) in enumerate(
            ((rho_hbm, rho), (mom_hbm, mom), (ene_hbm, ene), (mats_hbm, mats))
        )
    ]
    for load in loads:
        load.start()

    barrier = pltpu.get_barrier_semaphore()

    @pl.loop(1, count)
    def _(step):
        pl.semaphore_signal(
            barrier, inc=1, device_id=(lax.rem(me + step, count), core), device_id_type=MESH
        )

    pl.semaphore_signal(barrier, inc=1, device_id=(me, 1 - core), device_id_type=MESH)

    for load in loads:
        load.wait()

    for depth in range(2):
        for side, row in ((0, rows - 1 - depth), (1, depth)):
            rim_out[side, depth, 0] = rho[row]
            for c in range(3):
                rim_out[side, depth, 1 + c] = mom[c, row]
            rim_out[side, depth, 4] = ene[row]

    @pl.when(me == 0)
    def _():
        rim_in[0] = jnp.ones(rim_in.shape[1:], jnp.float32)

    @pl.when(me == count - 1)
    def _():
        rim_in[1] = jnp.ones(rim_in.shape[1:], jnp.float32)

    def primitives(d, m0, m1, m2, e):
        inv = 1.0 / d
        u, v, w = m0 * inv, m1 * inv, m2 * inv
        push = (GAMMA_GAS - 1.0) * (e - 0.5 * (u * m0 + v * m1 + w * m2))
        return u, v, w, push * inv

    @pl.loop(0, tiles)
    def _(t):
        z = pl.ds(pl.multiple_of(t * 8, 8), 8)
        ups, downs = [None] * 4, [None] * 4
        for y in range(rows):
            m2 = mom[2, y, z]
            values = primitives(rho[y, z], mom[0, y, z], mom[1, y, z], m2, ene[y, z])
            a, b = entry("slope", "to_up", y), entry("slope", "to_down", y)
            for f in range(4):
                span_out[f, y, z] = values[f]
                ups[f] = a * values[f] if y == 0 else ups[f] + a * values[f]
                downs[f] = b * values[f] if y == 0 else downs[f] + b * values[f]
            span_out[4, y, z] = m2
        for f in range(4):
            va[f * tiles + t] = ups[f]
            va[(4 + f) * tiles + t] = downs[f]

    pl.semaphore_wait(barrier, count)

    def rim_send(source, into, slot):
        def make(side, target):
            return remote(source(side), into(side), s_rim.at[slot, side], r_rim.at[slot, side], target, core)

        @pl.when(me < count - 1)
        def _():
            make(0, me + 1).start()

        @pl.when(me > 0)
        def _():
            make(1, me - 1).start()

    def rim_wait(source, into, slot):
        def make(side, target):
            return remote(source(side), into(side), s_rim.at[slot, side], r_rim.at[slot, side], target, core)

        @pl.when(me < count - 1)
        def _():
            make(0, me + 1).wait_send()
            make(1, me + 1).wait_recv()

        @pl.when(me > 0)
        def _():
            make(1, me - 1).wait_send()
            make(0, me - 1).wait_recv()

    def in_group(at):
        return group * inner + at

    def across(at):
        return at * inner + place

    def spread(src, dst, line, size, mine, device):
        each = src.shape[0] // size
        own = pl.ds(mine * each, each)

        @pl.loop(1, size)
        def _(step):
            to = lax.rem(mine + step, size)
            remote(
                src.at[pl.ds(to * each, each)], dst.at[own],
                s_line.at[line, step], r_line.at[line, step], device(to), core,
            ).start()

        dst[own] = src[own]

    def spread_wait(src, dst, line, size, mine, device):
        each = src.shape[0] // size

        @pl.loop(1, size)
        def _(step):
            to = lax.rem(mine + step, size)
            fro = lax.rem(mine + size - step, size)
            remote(
                src.at[pl.ds(to * each, each)], dst.at[pl.ds(mine * each, each)],
                s_line.at[line, step], r_line.at[line, step], device(to), core,
            ).wait_send()
            remote(
                src.at[pl.ds(to * each, each)], dst.at[pl.ds(fro * each, each)],
                s_line.at[line, step], r_line.at[line, step], device(to), core,
            ).wait_recv()

    def scan(src, first, gain_at, turned, size, emit):
        each = src.shape[0] // size

        def lap(i, carry):
            j = i + turned * (size - 1 - 2 * i)
            emit(j, carry)
            return tuple(
                tab[gain_at + i * each + k] * carry[k] + src[j * each + k] for k in range(each)
            )

        return lax.fori_loop(0, size, lap, first)

    def sender(out, back, line, size, mine, device):
        each = out.shape[0] // size

        def emit(j, carry):
            at = pl.ds(j * each, each)
            for k in range(each):
                out[j * each + k] = carry[k]

            @pl.when(j != mine)
            def _():
                step = lax.rem(j - mine + size, size)
                remote(
                    out.at[at], back.at[pl.ds(mine * each, each)],
                    s_line.at[line, step], r_line.at[line, step], device(j), core,
                ).start()

            @pl.when(j == mine)
            def _():
                back[at] = out[at]

        return emit

    class Lines:
        def __init__(self, at, fields, near, far, values, got, out, back, total, tgot, tout, tback):
            self.values, self.got, self.out, self.back = values, got, out, back
            self.total, self.tgot, self.tout, self.tback = total, tgot, tout, tback
            self.line = 4 * at
            self.each = values.shape[0] // count
            wide = outer * self.each
            self.wide = wide
            self.turned = jnp.minimum((place * wide) // (fields * tiles), 1)
            self.near = near + me * (inner * wide)
            self.far = far + me * (outer * self.each)
            ring, column = (inner, place, in_group), (outer, group, across)
            self.hops = (
                (values, got, self.line, *ring),
                (total, tgot, self.line + 1, *column),
                (tout, tback, self.line + 2, *column),
                (out, back, self.line + 3, *ring),
            )

        def start(self):
            spread(*self.hops[0])

        def wait(self, hop):
            spread_wait(*self.hops[hop])

        def gather(self):
            self.wait(0)
            zeros = tuple(jnp.zeros((8, 128), jnp.float32) for _ in range(self.wide))
            total = scan(self.got, zeros, self.near, self.turned, inner, lambda j, carry: None)
            for k in range(self.wide):
                self.total[k] = total[k]
            spread(*self.hops[1])

        def cross(self):
            self.wait(1)
            zeros = tuple(jnp.zeros((8, 128), jnp.float32) for _ in range(self.each))
            scan(self.tgot, zeros, self.far, self.turned, outer, sender(*self.hops[2]))

        def give(self):
            self.wait(2)
            first = tuple(self.tback[k] for k in range(self.wide))
            scan(self.got, first, self.near, self.turned, inner, sender(*self.hops[3]))

        def finish(self):
            self.wait(3)

    near_a, far_a, near_b, far_b = starts
    lines_a = Lines(0, 4, near_a, far_a, va, ra, oa, sa, ta, rta, ota, sta)
    lines_b = Lines(1, 6, near_b, far_b, vb, rb, ob, sb, tb, rtb, otb, stb)
    lines_c = Lines(2, 4, near_a, far_a, vc, rc, oc, sc, tc, rtc, otc, stc)

    rim_a = (lambda side: rim_out.at[side, 0], lambda side: rim_in.at[side, 0], 0)
    rim_b = (lambda side: rim_out.at[side, 1], lambda side: rim_in.at[side, 1], 1)
    span_copy = remote(span_out, span_in, s_span.at[0], r_span.at[0], me, 1 - core)
    fspan_copy = remote(fspan_out, fspan_in, s_span.at[1], r_span.at[1], me, 1 - core)
    edge_copy = remote(edge_out, edge_in, s_span.at[2], r_span.at[2], me, 1 - core)

    lines_a.start()
    span_copy.start()

    def local_rows(kind, load, store, z):
        values = [load(y) for y in range(rows)]
        for y in range(rows):
            total = entry(kind, "local", y * rows) * values[0]
            for k in range(1, rows):
                total = total + entry(kind, "local", y * rows + k) * values[k]
            store(y, total)

    def block_loop(fields, size, body):
        per = span // size

        @pl.loop(0, fields * per)
        def _(i):
            body(i // per, pl.ds(pl.multiple_of((i % per) * size, size), size))

    def slope_block(src, dst):
        def body(f, z):
            def store(y, total):
                dst[f, y, z] = total

            local_rows("slope", lambda y: src[f, y, z], store, z)

        return body

    def stream_rows(value):
        high, low = halves(value)
        product = jnp.dot(
            jnp.concatenate([high, low], axis=1), mats[pl.ds(0, 256)], preferred_element_type=jnp.float32
        )
        return product[:, :128] + product[:, 128:]

    def stream_loop(fields, load, store):
        @pl.loop(0, fields)
        def _(f):
            product = stream_rows(jnp.concatenate([load(f, y) for y in range(rows)], axis=0))
            for y in range(rows):
                store(f, y, product[y * span : (y + 1) * span])

    def span_pair(own, other):
        parts = [halves(jnp.concatenate(pair, axis=1)) for pair in (own, other)]
        stacked = jnp.concatenate([parts[0][0], parts[1][0], parts[0][1], parts[1][1]], axis=0)
        product = jnp.dot(mats[pl.ds(256, 128)], stacked, preferred_element_type=jnp.float32)
        product = product[:span] + product[span:]
        return product[:, :128], product[:, 128:]

    def span_loop(first, last, own, other, store):
        @pl.loop(first, last)
        def _(f):
            for y in range(0, rows, 2):
                pair = span_pair((own[f, y], own[f, y + 1]), (other[f, y], other[f, y + 1]))
                store(f, y, pair[0])
                store(f, y + 1, pair[1])

    def store_gx(f, y, value):
        gx[f, y] = value

    def store_gz(f, y, value):
        gz[f, y] = value

    stream_loop(4, lambda f, y: span_out[f, y], store_gx)
    lines_a.gather()
    rim_send(*rim_a)

    @pl.loop(0, tiles)
    def _(t):
        z = pl.ds(pl.multiple_of(t * 8, 8), 8)
        ups, downs = [None] * 6, [None] * 6
        for y in range(rows):
            middle = mom[1, y, z]
            values = (rho[y, z], mom[0, y, z], middle, mom[2, y, z], ene[y, z], middle)
            pairs = [
                (entry(kind, "to_up", y), entry(kind, "to_down", y)) for kind in ("smooth", "slope")
            ]
            for f in range(6):
                a, b = pairs[f // 5]
                ups[f] = a * values[f] if y == 0 else ups[f] + a * values[f]
                downs[f] = b * values[f] if y == 0 else downs[f] + b * values[f]
        for f in range(6):
            vb[f * tiles + t] = ups[f]
            vb[(6 + f) * tiles + t] = downs[f]

    lines_a.cross()
    block_loop(4, 32, slope_block(span_out, gy))
    lines_a.give()
    lines_b.start()

    span_copy.wait()
    span_loop(0, 4, span_out, span_in, store_gz)

    rim_wait(*rim_a)
    for side, row in ((0, 0), (1, rows - 1)):
        weight = entry("slope", "rim", 3 * side)
        values = primitives(*(rim_in[side, 0, f] for f in range(5)))
        for f in range(4):
            edge_out[side, f] = values[f]
            gy[f, row] += weight * values[f]
    edge_copy.start()

    lines_a.finish()
    rim_send(*rim_b)

    def stress_of(grad, d):
        row = [VISCOSITY * (grad[d][c] + grad[c][d]) for c in range(3)]
        spread_out = (2.0 / 3.0 * VISCOSITY) * (grad[0][0] + grad[1][1] + grad[2][2])
        row[d] = (2.0 * VISCOSITY) * grad[d][d] - spread_out
        return row

    def flux_of(d, u, m, e, push, grad):
        stress = stress_of(grad, d)
        energy = (e + push) * u[d] - CONDUCT * grad[d][3]
        values = []
        for c in range(3):
            energy = energy - u[c] * stress[c]
            value = m[c] * u[d] - stress[c]
            values.append(value + push if c == d else value)
        return values + [energy]

    def cell(y, z):
        u = [span_out[f, y, z] for f in range(4)]
        return u, [mom[c, y, z] for c in range(3)], ene[y, z], rho[y, z] * u[3]

    @pl.loop(0, tiles)
    def _(t):
        z = pl.ds(pl.multiple_of(t * 8, 8), 8)
        ups, downs = [None] * 4, [None] * 4
        from_up = [sa[f * tiles + t] for f in range(4)]
        from_down = [sa[(4 + f) * tiles + t] for f in range(4)]
        for y in range(rows):
            a, b = entry("slope", "up", y), entry("slope", "down", y)
            wall = [gy[f, y, z] + a * from_up[f] + b * from_down[f] for f in range(4)]
            for f in range(4):
                gy[f, y, z] = wall[f]
            grad = ([gx[f, y, z] for f in range(3)], wall, [gz[f, y, z] for f in range(3)])
            values = flux_of(1, *cell(y, z), grad)
            a, b = entry("slope", "to_up", y), entry("slope", "to_down", y)
            for f in range(4):
                fy[f, y, z] = values[f]
                ups[f] = a * values[f] if y == 0 else ups[f] + a * values[f]
                downs[f] = b * values[f] if y == 0 else downs[f] + b * values[f]
        for f in range(4):
            vc[f * tiles + t] = ups[f]
            vc[(4 + f) * tiles + t] = downs[f]

    lines_c.start()
    lines_b.gather()

    @pl.loop(0, tiles)
    def _(t):
        z = pl.ds(pl.multiple_of(t * 8, 8), 8)
        for y in range(rows):
            grad = [[ref[f, y, z] for f in range(4)] for ref in (gx, gy, gz)]
            state = cell(y, z)
            for d, out in ((2, fspan_out), (0, fx)):
                values = flux_of(d, *state, grad)
                for f in range(4):
                    out[f, y, z] = values[f]

    fspan_copy.start()

    def store_fx(f, y, value):
        gx[f, y] = value

    stream_loop(4, lambda f, y: fx[f, y], store_fx)
    lines_b.cross()
    lines_c.gather()
    block_loop(4, 32, slope_block(fy, gf))
    lines_c.cross()
    lines_b.give()

    span_loop(4, 5, span_out, span_in, store_gz)

    def store_mass(f, y, value):
        rate[0, y] = value

    stream_loop(1, lambda f, y: mom[0, y], store_mass)

    def mass_block(f, z):
        def store(y, total):
            rate[0, y, z] = -(rate[0, y, z] + total + gz[4, y, z])

        local_rows("slope", lambda y: mom[1, y, z], store, z)

    block_loop(1, 32, mass_block)

    def smooth_block(read, write):
        def body(f, z):
            def store(y, total):
                write[y, z] = total

            local_rows("smooth", lambda y: read[y, z], store, z)

        return body

    block_loop(1, 32, smooth_block(rho, smooth.at[0]))

    def smooth_mom(f, z):
        def store(y, total):
            smooth[1 + f, y, z] = total

        local_rows("smooth", lambda y: mom[f, y, z], store, z)

    block_loop(3, 32, smooth_mom)
    block_loop(1, 32, smooth_block(ene, smooth.at[4]))
    lines_c.give()
    rim_wait(*rim_b)
    for side, edge, inner in ((0, 0, 1), (1, rows - 1, rows - 2)):
        near, far, second = (entry("smooth", "rim", 3 * side + k) for k in range(3))
        for f in range(5):
            smooth[f, edge] += near * rim_in[side, 0, f] + far * rim_in[side, 1, f]
            smooth[f, inner] += second * rim_in[side, 0, f]
        rate[0, edge] -= entry("slope", "rim", 3 * side) * rim_in[side, 0, 2]

    edge_copy.wait()

    @pl.loop(0, 2)
    def _(side):
        product = stream_rows(jnp.concatenate([edge_out[side, f] for f in range(4)], axis=0))
        for f in range(4):
            edge_x[side, f] = product[f * span : (f + 1) * span]
        for f in (0, 2):
            pair = span_pair(
                (edge_out[side, f], edge_out[side, f + 1]), (edge_in[side, f], edge_in[side, f + 1])
            )
            edge_z[side, f] = pair[0]
            edge_z[side, f + 1] = pair[1]

    @pl.loop(0, tiles)
    def _(t):
        z = pl.ds(pl.multiple_of(t * 8, 8), 8)
        for side, row, step in ((0, 0, 1), (1, rows - 1, -1)):
            weights = [entry("slope", "next", 6 * side + k) for k in range(6)]
            u = [edge_out[side, f, z] for f in range(4)]
            past = primitives(*(rim_in[side, 1, f, z] for f in range(5)))
            wall = [
                weights[0] * u[f] + weights[1] * span_out[f, row + step, z]
                + weights[2] * past[f] + weights[3] * span_out[f, row + 2 * step, z]
                + weights[4] * gy[f, row, z] + weights[5] * gy[f, row + step, z]
                for f in range(4)
            ]
            grad = (
                [edge_x[side, f, z] for f in range(3)], wall, [edge_z[side, f, z] for f in range(3)]
            )
            m = [rim_in[side, 0, 1 + c, z] for c in range(3)]
            values = flux_of(1, u, m, rim_in[side, 0, 4, z], rim_in[side, 0, 0, z] * u[3], grad)
            weight = entry("slope", "rim", 3 * side)
            for f in range(4):
                gf[f, row, z] += weight * values[f]

    fspan_copy.wait()
    span_loop(0, 4, fspan_out, fspan_in, store_gz)

    lines_b.finish()

    @pl.loop(0, tiles)
    def _(t):
        z = pl.ds(pl.multiple_of(t * 8, 8), 8)
        from_up = [sb[f * tiles + t] for f in range(6)]
        from_down = [sb[(6 + f) * tiles + t] for f in range(6)]
        for y in range(rows):
            a, b = entry("smooth", "up", y), entry("smooth", "down", y)
            for f in range(5):
                smooth[f, y, z] += a * from_up[f] + b * from_down[f]
            a, b = entry("slope", "up", y), entry("slope", "down", y)
            rate[0, y, z] -= a * from_up[5] + b * from_down[5]

    smooth_flush = pltpu.make_async_copy(smooth, smooth_hbm, s_load.at[4])
    smooth_flush.start()
    mass_flush = pltpu.make_async_copy(rate.at[0], rate_hbm.at[0], s_load.at[6])
    mass_flush.start()

    lines_c.finish()

    @pl.loop(0, tiles)
    def _(t):
        z = pl.ds(pl.multiple_of(t * 8, 8), 8)
        from_up = [sc[f * tiles + t] for f in range(4)]
        from_down = [sc[(4 + f) * tiles + t] for f in range(4)]
        for y in range(rows):
            a, b = entry("slope", "up", y), entry("slope", "down", y)
            keep = tab[base + places["keep"] + y]
            for f in range(4):
                total = gx[f, y, z] + gz[f, y, z] + gf[f, y, z] + a * from_up[f] + b * from_down[f]
                rate[1 + f, y, z] = -(total * keep) if f < 3 else -total

    rest = pl.ds(1, 4)
    rate_flush = pltpu.make_async_copy(rate.at[rest], rate_hbm.at[rest], s_load.at[5])
    rate_flush.start()
    rate_flush.wait()
    mass_flush.wait()
    smooth_flush.wait()


def results_body(rate_from, smooth_from, rate_to, smooth_to, held, sems):
    ins, outs = [], []
    for at, (source, target) in enumerate(((rate_from, rate_to), (smooth_from, smooth_to))):
        for f in range(5):
            ins.append(pltpu.make_async_copy(source.at[f], held.at[at, f], sems.at[0, at, f]))
            outs.append(pltpu.make_async_copy(held.at[at, f], target.at[f], sems.at[1, at, f]))
    for copy in ins:
        copy.start()
    for copy, after in zip(ins, outs):
        copy.wait()
        after.start()
    for after in outs:
        after.wait()


def per_device(mass_per_volume, mass_flux_vector, total_heat_content):
    rows, span, stream = mass_per_volume.shape
    count = lax.axis_size("gy")
    tiles = span // 8
    table, gains = device_table(rows * count, rows)
    each_a = -(-8 * tiles // count)
    each_b = -(-12 * tiles // count)
    pieces = [table]
    for kinds, each in ((["slope"] * 4, each_a), (["smooth"] * 5 + ["slope"], each_b)):
        pieces += gain_tables(kinds, gains, count, tiles, each)
    starts = tuple(int(at) for at in np.cumsum([piece.size for piece in pieces[:-1]]))
    field = (rows, span, stream)
    mats = np.concatenate([stream_table(stream), span_table(2 * span)])
    outer, inner = scan_groups(count)

    def vmem(*shape):
        return pltpu.VMEM(shape, jnp.float32)

    lines_a = [vmem(count * each_a, 8, stream)] * 4
    lines_b = [vmem(count * each_b, 8, stream)] * 4
    totals_a = [vmem(outer * each_a, 8, stream)] * 4
    totals_b = [vmem(outer * each_b, 8, stream)] * 4
    scalar = pl.BlockSpec(memory_space=pltpu.SMEM)
    outside = pl.BlockSpec(memory_space=pl.ANY)
    dma = pltpu.SemaphoreType.DMA
    out = jax.ShapeDtypeStruct((5,) + field, jnp.float32)
    results = pl.pallas_call(
        functools.partial(fused_body, count, starts),
        out_shape=(out, out),
        in_specs=[outside] * 3 + [scalar, outside],
        out_specs=(outside, outside),
        scratch_shapes=[
            vmem(5, *field), vmem(5, *field),
            vmem(*field), vmem(3, *field), vmem(*field), pltpu.VMEM(mats.shape, jnp.bfloat16),
            vmem(5, *field), vmem(5, *field), vmem(4, *field), vmem(4, *field), vmem(5, *field),
            *[vmem(4, *field)] * 5,
            vmem(2, 2, 5, span, stream), vmem(2, 2, 5, span, stream),
            *[vmem(2, 4, span, stream)] * 4,
            *lines_a, *lines_b, *lines_a,
            *totals_a, *totals_b, *totals_a,
            dma((7,)), dma((3,)), dma((3,)), dma((2, 2)), dma((2, 2)),
            dma((12, max(inner, outer))), dma((12, max(inner, outer))),
        ],
        compiler_params=pltpu.CompilerParams(
            collective_id=0, has_side_effects=True, vmem_limit_bytes=56 * 1024 * 1024
        ),
    )(
        mass_per_volume, mass_flux_vector, total_heat_content,
        jnp.asarray(np.concatenate(pieces)), jnp.asarray(mats),
    )
    return pl.pallas_call(
        results_body,
        out_shape=(out, out),
        in_specs=[outside] * 2,
        out_specs=(outside, outside),
        scratch_shapes=[vmem(2, 5, *field), dma((2, 2, 5))],
        compiler_params=pltpu.CompilerParams(vmem_limit_bytes=56 * 1024 * 1024),
    )(*results)


def solution(mesh):
    placed = (P("gy", "pa", None), P(None, "gy", "pa", None), P("gy", "pa", None))
    return jax.shard_map(
        per_device,
        mesh=mesh,
        in_specs=placed,
        out_specs=(P(None, "gy", "pa", None), P(None, "gy", "pa", None)),
        check_vma=False,
    )
```
